32 devices in a mesh: groups: 2 (over y), gx: 4 (over z), gz: 2 (over x), vert: 2 (over core).
Axes of the slice: x: 2, y: 2, z: 4, core: 2. Of those that a mesh axis runs over, the one named last changes fastest.
Arguments:
- flow_field: bfloat16 [4, 4, 5, 4, 256, 256], P('groups', 'vert', None, 'gx', None, 'gz'), parts along dimension 0, may hold values from -6 to 6
- test_streams: int32 [4], P('groups'), parts along dimension 0, may hold values from 0 to 999999
- snapshot_ids: int32 [4, 4], P('groups', 'vert'), parts along dimension 0, may hold values from 0 to 65535
Outputs:
- sketch_x: float32 [8, 128], P(('groups', 'gx')), parts along dimension 0
- sketch_y: float32 [512, 128], P(('groups', 'gx', 'gz', 'vert')), parts along dimension 0
- sketch_z: float32 [512, 128], P(('groups', 'gz'), ('gx', 'vert')), parts along dimension 0
- core_sketch: float32 [4608, 2, 48], P(('groups', 'gx')), parts along dimension 0
The draws below stay inside these ranges and needn't reach their ends.
There are 2 independent parts, one for each index of `groups`. The reference program is written for one: setup_inputs(seed, part) draws one part's arguments, and reference() takes and returns one part's arrays. A program takes and returns all parts, laid end to end along the dimension named above; each array names one. Nothing has to cross between parts.
All inputs are finite; a program needn't handle non-finite values.
Results may differ from the reference program's by a relative error of at most 0.007.
Values sent between devices are 32-bit elements; how exact they have to be, the bound alone decides.
A program may use at most 64 MiB of HBM per device.

```python
import math
import jax
import jax.numpy as jnp
from jax import lax

K = 128
S = 48
E = 2
V = 5
BATCHES = 2
SNAP_MB = 4
SNAP_RANGE = 65536
NY = 256
NX = 4
NZ = 256


def plant(values, stream_key, smallest, top_value):
    spot = [jax.random.randint(jax.random.fold_in(stream_key, axis), (), 0, length) for axis, length in enumerate(values.shape)]
    main_axis = values.shape.index(max(values.shape))
    beside = spot[:main_axis] + [(spot[main_axis] + 1) % values.shape[main_axis]] + spot[main_axis + 1:]
    return values.at[tuple(spot)].set(smallest).at[tuple(beside)].set(top_value)


def steps_of(key, dims, split, smallest, largest):
    factor_of = 1.0
    for dim, shards_of in split:
        draws = jax.random.uniform(jax.random.fold_in(jax.random.fold_in(key, 6), dim), (shards_of,), jnp.float32, smallest / len(split), largest / len(split))
        factor_of = factor_of * jnp.repeat(jnp.exp(draws), dims[dim] // shards_of).reshape((-1,) + (1,) * (len(dims) - 1 - dim))
    return factor_of


def noise(rng, extent, scale, bound, shards=(), kind=jnp.bfloat16):
    loudness = steps_of(rng, extent, shards, -0.22, 0.18) if shards else 1.0
    drawn = jax.random.normal(rng, extent, jnp.float32) * scale * loudness
    return jnp.minimum(jnp.maximum(drawn, -bound), bound).astype(kind)


def setup_inputs(seed: int = 0, part: int = 0) -> dict:
    arg_keys = jax.random.split(jax.random.key(seed), 4)
    part_splits = jax.random.split(jax.random.fold_in(arg_keys[3], part), 4)
    flow_field = noise(part_splits[0], (BATCHES, SNAP_MB, V, NX, NY, NZ), 1.0, 6.0, ((1, 2), (3, 4), (5, 2)))
    test_streams = jax.random.randint(part_splits[1], (2,), 0, 1000000).astype(jnp.int32)
    snapshot_ids = plant(jax.random.randint(part_splits[2], (BATCHES, SNAP_MB), 0, SNAP_RANGE), jax.random.fold_in(part_splits[2], 1), 0, SNAP_RANGE - 1).astype(jnp.int32)
    return {"flow_field": flow_field, "test_streams": test_streams, "snapshot_ids": snapshot_ids}


def hash_index(index, stream, salt):
    mixed = index * -1640531535 + stream * -2048144777 + salt
    mixed = jnp.bitwise_xor(mixed, lax.shift_right_logical(mixed, jnp.int32(16)))
    mixed = mixed * 739982445
    mixed = jnp.bitwise_xor(mixed, lax.shift_right_logical(mixed, jnp.int32(13)))
    mixed = mixed * 695872825
    return jnp.bitwise_xor(mixed, lax.shift_right_logical(mixed, jnp.int32(16)))

def unit_value(index, stream, salt):
    upper = lax.shift_right_logical(hash_index(index, stream, salt), jnp.int32(9))
    return ((2 * upper + 1).astype(jnp.float32) * 2.0 ** (-24) - 1.0).astype(jnp.bfloat16)

def test_table(row_ids, col_ids, stride, stream, salt):
    return unit_value(row_ids[:, None] * stride + col_ids[None, :], stream, salt)

def reference(flow_field, test_streams, snapshot_ids):
    highest = lax.Precision.HIGHEST
    factor_stream = test_streams[0]
    core_stream = test_streams[1]
    total_q = BATCHES * SNAP_MB * V
    rank_ids = jnp.arange(K, dtype=jnp.int32)
    sketch_ids = jnp.arange(S, dtype=jnp.int32)
    x_ids = jnp.arange(NX, dtype=jnp.int32)
    y_ids = jnp.arange(NY, dtype=jnp.int32)
    z_ids = jnp.arange(NZ, dtype=jnp.int32)
    ax_tab = test_table(x_ids, rank_ids, K, factor_stream, 1).astype(jnp.float32)
    ay_tab = test_table(y_ids, rank_ids, K, factor_stream, 2).astype(jnp.float32)
    az_low = test_table(z_ids, rank_ids, K, factor_stream, 3)
    phx_tab = test_table(sketch_ids, x_ids, NX, core_stream, 5).astype(jnp.float32)
    phy_tab = test_table(sketch_ids, y_ids, NY, core_stream, 6).astype(jnp.float32)
    phz_low = test_table(sketch_ids, z_ids, NZ, core_stream, 7)
    q_ids = (snapshot_ids[:, :, None] * V + jnp.arange(V, dtype=jnp.int32)[None, None, :]).reshape(-1)
    aq_tab = test_table(q_ids, rank_ids, K, factor_stream, 4).astype(jnp.float32)
    phq_tab = test_table(q_ids, jnp.arange(E, dtype=jnp.int32), E, core_stream, 8).astype(jnp.float32)
    slices = flow_field.reshape(total_q, NX, NY, NZ)

    def one_slice(carry, inputs):
        acc_x, acc_y, acc_z, acc_core = carry
        slab, aq_row, phq_row = inputs
        rows_z = slab.reshape(NX * NY, NZ)
        along_z = jnp.dot(rows_z, az_low, preferred_element_type=jnp.float32).reshape(NX, NY, K)
        along_y = jnp.einsum('xyz,yk->xzk', slab.astype(jnp.float32), ay_tab, precision=highest)
        weights = aq_row[None, :] * ax_tab
        acc_x = acc_x + lax.optimization_barrier(jnp.sum(along_z * ay_tab[None, :, :], axis=1)) * aq_row[None, :]
        acc_y = acc_y + lax.optimization_barrier(jnp.sum(along_z * weights[:, None, :], axis=0))
        acc_z = acc_z + lax.optimization_barrier(jnp.sum(along_y * weights[:, None, :], axis=0))
        first = jnp.dot(rows_z, phz_low.T, preferred_element_type=jnp.float32).reshape(NX, NY, S)
        second = jnp.einsum('xyc,by->bcx', first, phy_tab, precision=highest)
        acc_core = acc_core + second[:, :, None, :] * phq_row[None, None, :, None]
        return ((acc_x, acc_y, acc_z, acc_core), None)
    start_state = (jnp.zeros((NX, K), jnp.float32), jnp.zeros((NY, K), jnp.float32), jnp.zeros((NZ, K), jnp.float32), jnp.zeros((S, S, E, NX), jnp.float32))
    final_state, unused = lax.scan(one_slice, start_state, (slices, aq_tab, phq_tab))
    sum_x, sum_y, sum_z, partial_core = final_state
    core = jnp.einsum('bcex,ax->bcea', partial_core, phx_tab, precision=highest).reshape(S * S, E, S)
    scale_x = 3.0 ** 1.5 / math.sqrt(NY * NZ * total_q)
    scale_y = 3.0 ** 1.5 / math.sqrt(NX * NZ * total_q)
    scale_z = 3.0 ** 1.5 / math.sqrt(NX * NY * total_q)
    scale_core = 9.0 / math.sqrt(NX * NY * NZ * total_q)
    return (sum_x * scale_x, sum_y * scale_y, sum_z * scale_z, core * scale_core)
```

```python
import functools
import math

import jax
import jax.numpy as jnp
from jax import lax
from jax.experimental import pallas as pl
from jax.experimental.pallas import tpu as pltpu
from jax.sharding import PartitionSpec as P

K = 128
S = 48
E = 2


def hash_index(index, stream, salt):
    mixed = index * -1640531535 + stream * -2048144777 + salt
    mixed = jnp.bitwise_xor(mixed, lax.shift_right_logical(mixed, jnp.int32(16)))
    mixed = mixed * 739982445
    mixed = jnp.bitwise_xor(mixed, lax.shift_right_logical(mixed, jnp.int32(13)))
    mixed = mixed * 695872825
    return jnp.bitwise_xor(mixed, lax.shift_right_logical(mixed, jnp.int32(16)))


def unit_value(index, stream, salt):
    upper = lax.shift_right_logical(hash_index(index, stream, salt), jnp.int32(9))
    return ((2 * upper + 1).astype(jnp.float32) * 2.0 ** (-24) - 1.0).astype(jnp.bfloat16)


def test_table(row_ids, col_ids, stride, stream, salt):
    return unit_value(row_ids[:, None] * stride + col_ids[None, :], stream, salt)


def shards_general(flow_field, test_streams, snapshot_ids):
    highest = lax.Precision.HIGHEST
    batches, local_snaps, variables, cells_x, cells_y, cells_z = flow_field.shape
    slabs_x = lax.axis_size("gx")
    total_x = cells_x * slabs_x
    total_z = cells_z * lax.axis_size("gz")
    total_q = variables * batches * local_snaps * lax.axis_size("vert")
    factor_stream = test_streams[0]
    core_stream = test_streams[1]
    rank_ids = jnp.arange(K, dtype=jnp.int32)
    sketch_ids = jnp.arange(S, dtype=jnp.int32)
    x_ids = lax.axis_index("gx") * cells_x + jnp.arange(cells_x, dtype=jnp.int32)
    y_ids = jnp.arange(cells_y, dtype=jnp.int32)
    z_ids = lax.axis_index("gz") * cells_z + jnp.arange(cells_z, dtype=jnp.int32)
    ax_tab = test_table(x_ids, rank_ids, K, factor_stream, 1).astype(jnp.float32)
    ay_low = test_table(y_ids, rank_ids, K, factor_stream, 2)
    az_low = test_table(z_ids, rank_ids, K, factor_stream, 3)
    ay_tab = ay_low.astype(jnp.float32)
    phy_low = test_table(sketch_ids, y_ids, cells_y, core_stream, 6)
    phz_low = test_table(sketch_ids, z_ids, total_z, core_stream, 7)

    def batch_terms(batch_idx):
        blocks = flow_field[batch_idx].reshape(-1, cells_x, cells_y, cells_z)
        pairs = blocks.shape[0]
        q_ids = (
            snapshot_ids[batch_idx][:, None] * variables
            + jnp.arange(variables, dtype=jnp.int32)[None, :]
        ).reshape(-1)
        aq_tab = test_table(q_ids, rank_ids, K, factor_stream, 4).astype(jnp.float32)
        phq_low = test_table(q_ids, jnp.arange(E, dtype=jnp.int32), E, core_stream, 8)
        rows_z = blocks.reshape(-1, cells_z)
        along_z = jnp.dot(rows_z, az_low, preferred_element_type=jnp.float32).reshape(
            pairs, cells_x, cells_y, K
        )
        along_y = jnp.einsum("qxyz,yk->qxzk", blocks, ay_low, preferred_element_type=jnp.float32)
        weights = aq_tab[:, None, :] * ax_tab[None, :, :]
        part_x = jnp.sum(
            jnp.sum(along_z * ay_tab[None, None, :, :], axis=2) * aq_tab[:, None, :], axis=0
        )
        part_y = jnp.sum(along_z * weights[:, :, None, :], axis=(0, 1))
        part_z = jnp.sum(along_y * weights[:, :, None, :], axis=(0, 1))
        first = jnp.dot(rows_z, phz_low.T, preferred_element_type=jnp.float32).reshape(
            pairs, cells_x, cells_y, S
        )
        second = jnp.einsum("qxyc,by->qxbc", first, phy_low.astype(jnp.float32), precision=highest)
        partial_core = jnp.einsum(
            "qxbc,qe->bcex", second, phq_low.astype(jnp.float32), precision=highest
        )
        return (part_x, part_y, part_z, partial_core.reshape(S * S, E, cells_x))

    def finish(part_x, part_y, part_z, partial_core):
        summed, sum_x = lax.psum((partial_core, part_x), ("gz", "vert"))
        phx_whole = test_table(
            sketch_ids, jnp.arange(total_x, dtype=jnp.int32), total_x, core_stream, 5
        ).astype(jnp.float32)
        core = jnp.einsum(
            "rex,ax->rea",
            lax.all_to_all(summed, "gx", split_axis=0, concat_axis=2, tiled=True),
            phx_whole,
            precision=highest,
        )
        sum_z = lax.psum_scatter(part_z, ("gx", "vert"), scatter_dimension=1, tiled=True)
        sum_y = lax.psum_scatter(part_y, ("gx", "gz", "vert"), scatter_dimension=0, tiled=True)
        return (sum_x, sum_y, sum_z, core)

    terms = [batch_terms(batch_idx) for batch_idx in range(batches)]
    totals = finish(terms[0][0], terms[0][1], terms[0][2], terms[0][3])
    for later in terms[1:]:
        latest = finish(later[0], later[1], later[2], later[3])
        totals = tuple((earlier + newer for earlier, newer in zip(totals, latest)))
    scale_x = 3.0**1.5 / math.sqrt(cells_y * total_z * total_q)
    scale_y = 3.0**1.5 / math.sqrt(total_x * total_z * total_q)
    scale_z = 3.0**1.5 / math.sqrt(total_x * cells_y * total_q)
    scale_core = 9.0 / math.sqrt(total_x * cells_y * total_z * total_q)
    return (totals[0] * scale_x, totals[1] * scale_y, totals[2] * scale_z, totals[3] * scale_core)


MESH = pl.DeviceIdType.MESH
PAD = 16


def iota(shape, dim):
    return lax.broadcasted_iota(jnp.int32, shape, dim)


def unit_f32(index, stream, salt):
    return unit_value(index, stream, salt).astype(jnp.float32)


def dot_f32(left, right):
    return jnp.dot(left, right, preferred_element_type=jnp.float32)


def dot_split(left, right):
    upper = left.astype(jnp.bfloat16)
    lower = (left - upper.astype(jnp.float32)).astype(jnp.bfloat16)
    return dot_f32(upper, right) + dot_f32(lower, right)


def sketch_kernel(
    sizes,
    streams,
    snaps,
    flow_hbm,
    sums,
    flow,
    y_send,
    y_got,
    y_out,
    y_in,
    z_send,
    z_got,
    z_out,
    z_in,
    c_send,
    c_got,
    c_out,
    c_in,
    load_sem,
    pair_send,
    pair_recv,
    y_ssem,
    y_rsem,
    c_ssem,
    c_rsem,
    z_ssem,
    z_rsem,
):
    slabs, zsplit, pairs, variables, cells_y, cells_z = sizes
    chips = slabs * zsplit
    rows_y = cells_y // (2 * chips)
    rows_z = K // (2 * slabs)
    rows_m = S // slabs
    total_z = cells_z * zsplit
    gx = lax.axis_index("gx")
    gz = lax.axis_index("gz")
    vert = lax.axis_index("vert")
    other = 1 - vert
    offsets = [(dx, dz) for dx in range(slabs) for dz in range(zsplit)]

    def target(dx, dz):
        return {"gx": lax.rem(gx + dx, slabs), "gz": lax.rem(gz + dz, zsplit)}

    barrier = pltpu.get_barrier_semaphore()
    pl.semaphore_signal(barrier, inc=1, device_id={"vert": other}, device_id_type=MESH)
    for dx, dz in offsets[1:]:
        pl.semaphore_signal(barrier, inc=1, device_id=target(dx, dz), device_id_type=MESH)
    loads = [
        pltpu.make_async_copy(
            flow_hbm.at[pl.ds(p * variables, variables)],
            flow.at[pl.ds(p * variables, variables)],
            load_sem.at[p],
        )
        for p in range(pairs)
    ]
    for load in loads:
        load.start()

    fac = streams[0]
    cor = streams[1]
    total_q = pairs * variables
    q_rows = -(-total_q // 8) * 8

    def run_ids(q_index):
        ids = jnp.full(q_index.shape, 0, jnp.int32)
        for p in range(pairs):
            ids = jnp.where(q_index // variables == p, snaps[p], ids)
        return ids * variables + lax.rem(q_index, variables)

    z_base = gz * cells_z
    az_tab = unit_value(
        (z_base + iota((cells_z, K), 0)) * K + iota((cells_z, K), 1), fac, 3
    )
    r_rows = run_ids(iota((q_rows, K), 0))
    aq_tab = unit_f32(r_rows * K + iota((q_rows, K), 1), fac, 4)
    phq_tab = [unit_f32(r_rows * E + e, cor, 8) for e in range(E)]
    ax_row = unit_f32(gx * K + iota((8, K), 1), fac, 1)[0:1]
    ay_tab = unit_f32(iota((cells_y, K), 0) * K + iota((cells_y, K), 1), fac, 2)

    wide = jnp.zeros((cells_y, K), jnp.float32)
    for p in range(pairs):
        loads[p].wait()
        for v in range(variables):
            q = p * variables + v
            wide = wide + dot_f32(flow[q], az_tab) * aq_tab[q : q + 1]
    x_row = jnp.sum(wide * ay_tab, axis=0, keepdims=True)
    wide = wide * ax_row
    for c in range(chips):
        for v in range(2):
            at = (2 * c + v) * rows_y
            y_send[v, c] = wide[at : at + rows_y]

    pl.semaphore_wait(barrier, chips)

    def pair_copy(src, dst, which):
        return pltpu.make_async_remote_copy(
            src_ref=src,
            dst_ref=dst,
            send_sem=pair_send.at[which],
            recv_sem=pair_recv.at[which],
            device_id={"vert": other},
            device_id_type=MESH,
        )

    pair_y = pair_copy(y_send.at[other], y_got, 0)
    pair_y.start()

    ay_turned = unit_value(iota((K, cells_y), 1) * K + iota((K, cells_y), 0), fac, 2)
    rows_c = slabs * PAD
    m_row = iota((rows_c, cells_y), 0)
    m_ids = (m_row // PAD) * rows_m + lax.rem(m_row, PAD)
    phy_tab = unit_value(m_ids * cells_y + iota((rows_c, cells_y), 1), cor, 6)
    turned = jnp.concatenate([ay_turned, phy_tab], axis=0)
    aq_turned = unit_f32(run_ids(iota((K, K), 1)) * K + iota((K, K), 0), fac, 4)
    ax_turned = unit_f32(gx * K + iota((K, K), 0), fac, 1)
    weights = aq_turned * ax_turned
    lane = iota((cells_z, K), 1)
    phz_tab = unit_f32((lane // E) * total_z + z_base + iota((cells_z, K), 0), cor, 7)
    phz_tab = jnp.where(lane < E * S, phz_tab, 0.0)
    phz_e = [
        jnp.where(lax.rem(lane, E) == e, phz_tab, 0.0).astype(jnp.bfloat16) for e in range(E)
    ]

    copies = []
    deep = jnp.zeros((K, cells_z), jnp.float32)
    halves = [jnp.zeros((rows_c, cells_z), jnp.float32) for e in range(E)]
    for q in range(total_q):
        both = dot_f32(turned, flow[q])
        deep = deep + both[:K] * weights[:, q : q + 1]
        for e in range(E):
            halves[e] = halves[e] + both[K:] * phq_tab[e][q : q + 1]
        if q == total_q // 2:
            pair_y.wait_recv()
            y_out[...] = y_send[vert] + y_got[...]
            for i, (dx, dz) in enumerate(offsets[1:]):
                dest = target(dx, dz)
                copy = pltpu.make_async_remote_copy(
                    src_ref=y_out.at[dest["gx"] * zsplit + dest["gz"]],
                    dst_ref=y_in.at[i],
                    send_sem=y_ssem.at[i],
                    recv_sem=y_rsem.at[i],
                    device_id=dest,
                    device_id_type=MESH,
                )
                copy.start()
                copies.append(copy)
    y_copies = list(copies)

    for g in range(slabs):
        for v in range(2):
            at = (2 * g + v) * rows_z
            z_send[v, g] = deep[at : at + rows_z]
    pair_z = pair_copy(z_send.at[other], z_got, 1)
    pair_z.start()
    core = dot_split(halves[0], phz_e[0])
    for e in range(1, E):
        core = core + dot_split(halves[e], phz_e[e])
    core = jnp.where(lax.rem(iota((rows_c, K), 0), PAD) == rows_m, x_row, core)
    c_send[...] = core.reshape(slabs, PAD, K)
    pair_c = pair_copy(c_send, c_got, 2)
    pair_c.start()

    z_copies = []
    pair_z.wait_recv()
    z_out[...] = z_send[vert] + z_got[...]
    for dx in range(1, slabs):
        to = lax.rem(gx + dx, slabs)
        copy = pltpu.make_async_remote_copy(
            src_ref=z_out.at[to],
            dst_ref=z_in.at[dx - 1],
            send_sem=z_ssem.at[dx - 1],
            recv_sem=z_rsem.at[dx - 1],
            device_id={"gx": to},
            device_id_type=MESH,
        )
        copy.start()
        z_copies.append(copy)
    c_copies = []
    pair_c.wait_recv()
    c_out[...] = c_send[...] + c_got[...]
    for i, (dx, dz) in enumerate(offsets[1:]):
        dest = target(dx, dz)
        copy = pltpu.make_async_remote_copy(
            src_ref=c_out.at[dest["gx"]],
            dst_ref=c_in.at[i],
            send_sem=c_ssem.at[i],
            recv_sem=c_rsem.at[i],
            device_id=dest,
            device_id_type=MESH,
        )
        copy.start()
        c_copies.append(copy)

    total = y_out[gx * zsplit + gz]
    for i, copy in enumerate(y_copies):
        copy.wait_recv()
        total = total + y_in[i]
    sums[0:rows_y, :] = total
    total = z_out[gx]
    for i, copy in enumerate(z_copies):
        copy.wait_recv()
        total = total + z_in[i]
    sums[rows_y : rows_y + rows_z, :] = total
    for dx in range(slabs):
        total = c_out[gx] if dx == 0 else None
        for dz in range(zsplit):
            i = dx * zsplit + dz - 1
            if i < 0:
                continue
            c_copies[i].wait_recv()
            total = c_in[i] if total is None else total + c_in[i]
        at = rows_y + rows_z + dx * PAD
        sums[at : at + PAD, :] = total
    for copy in [pair_y, pair_z, pair_c] + y_copies + z_copies + c_copies:
        copy.wait_send()


def finish_kernel(sizes, scales, streams, sums, out_x, out_y, out_z, out_core):
    slabs, zsplit, pairs, variables, cells_y, cells_z = sizes
    rows_y = cells_y // (2 * slabs * zsplit)
    rows_z = K // (2 * slabs)
    rows_m = S // slabs
    gx = lax.axis_index("gx")
    scale_x, scale_y, scale_z, scale_core = scales
    top = rows_y + rows_z
    out_y[...] = sums[0:rows_y, :] * scale_y
    part_z = sums[rows_y:top, :] * scale_z
    filler = jnp.zeros((K - rows_z, cells_z), jnp.float32)
    out_z[...] = jnp.concatenate([part_z, filler], axis=0).T[:, :rows_z]
    out_x[...] = sums[top + rows_m : top + rows_m + 1, :] * scale_x
    rows_c = slabs * PAD
    slot = iota((rows_c, K), 0)
    x_ids = lax.rem(gx - slot // PAD + slabs, slabs)
    phx = unit_f32(iota((rows_c, K), 1) * slabs + x_ids, streams[1], 5)
    right = jnp.concatenate(
        [jnp.where(lax.rem(slot, PAD) == m, phx, 0.0).astype(jnp.bfloat16) for m in range(rows_m)],
        axis=1,
    )
    left = (sums[top : top + rows_c, :] * scale_core).T
    result = dot_split(left, right)
    for m in range(rows_m):
        out_core[m * E * S : (m + 1) * E * S, :] = result[: E * S, m * K : m * K + S]


def shards_fused(sizes, flow_field, test_streams, snapshot_ids):
    slabs, zsplit, pairs, variables, cells_y, cells_z = sizes
    chips = slabs * zsplit
    rows_y = cells_y // (2 * chips)
    rows_z = K // (2 * slabs)
    rows_m = S // slabs
    rows_c = slabs * PAD
    total_q = pairs * variables
    rows = rows_y + rows_z + rows_c
    f32 = jnp.float32
    smem = pl.BlockSpec(memory_space=pltpu.SMEM)
    vmem = pl.BlockSpec(memory_space=pltpu.VMEM)
    dma = pltpu.SemaphoreType.DMA
    sums = pl.pallas_call(
        functools.partial(sketch_kernel, sizes),
        name="sketch",
        out_shape=jax.ShapeDtypeStruct((rows, K), f32),
        in_specs=[smem, smem, pl.BlockSpec(memory_space=pl.ANY)],
        out_specs=vmem,
        scratch_shapes=[
            pltpu.VMEM((total_q, cells_y, cells_z), jnp.bfloat16),
            pltpu.VMEM((2, chips, rows_y, K), f32),
            pltpu.VMEM((chips, rows_y, K), f32),
            pltpu.VMEM((chips, rows_y, K), f32),
            pltpu.VMEM((chips - 1, rows_y, K), f32),
            pltpu.VMEM((2, slabs, rows_z, cells_z), f32),
            pltpu.VMEM((slabs, rows_z, cells_z), f32),
            pltpu.VMEM((slabs, rows_z, cells_z), f32),
            pltpu.VMEM((slabs - 1, rows_z, cells_z), f32),
            pltpu.VMEM((slabs, PAD, K), f32),
            pltpu.VMEM((slabs, PAD, K), f32),
            pltpu.VMEM((slabs, PAD, K), f32),
            pltpu.VMEM((chips - 1, PAD, K), f32),
            dma((pairs,)),
            dma((3,)),
            dma((3,)),
            dma((chips - 1,)),
            dma((chips - 1,)),
            dma((chips - 1,)),
            dma((chips - 1,)),
            dma((slabs - 1,)),
            dma((slabs - 1,)),
        ],
        compiler_params=pltpu.CompilerParams(
            collective_id=0, has_side_effects=True, vmem_limit_bytes=24 * 2**20
        ),
    )(
        test_streams,
        snapshot_ids.reshape(pairs),
        flow_field.reshape(total_q, cells_y, cells_z),
    )
    total_x = slabs
    total_z = cells_z * zsplit
    all_q = 2 * total_q
    scales = (
        3.0**1.5 / math.sqrt(cells_y * total_z * all_q),
        3.0**1.5 / math.sqrt(total_x * total_z * all_q),
        3.0**1.5 / math.sqrt(total_x * cells_y * all_q),
        9.0 / math.sqrt(total_x * cells_y * total_z * all_q),
    )
    out_x, out_y, out_z, out_core = pl.pallas_call(
        functools.partial(finish_kernel, sizes, scales),
        name="finish",
        out_shape=[
            jax.ShapeDtypeStruct((1, K), f32),
            jax.ShapeDtypeStruct((rows_y, K), f32),
            jax.ShapeDtypeStruct((cells_z, rows_z), f32),
            jax.ShapeDtypeStruct((rows_m * S * E, S), f32),
        ],
        in_specs=[smem, vmem],
        out_specs=[vmem, vmem, vmem, vmem],
        compiler_params=pltpu.CompilerParams(vmem_limit_bytes=24 * 2**20),
    )(test_streams, sums)
    return (out_x, out_y, out_z, out_core.reshape(rows_m * S, E, S))


def shards(flow_field, test_streams, snapshot_ids):
    batches, local_snaps, variables, cells_x, cells_y, cells_z = flow_field.shape
    slabs = lax.axis_size("gx")
    zsplit = lax.axis_size("gz")
    fits = (
        lax.axis_size("vert") == 2
        and cells_x == 1
        and cells_z == K
        and cells_y % (16 * slabs * zsplit) == 0
        and K % (16 * slabs) == 0
        and S % slabs == 0
        and S // slabs < PAD
        and batches * local_snaps * variables <= K
    )
    if not fits:
        return shards_general(flow_field, test_streams, snapshot_ids)
    sizes = (slabs, zsplit, batches * local_snaps, variables, cells_y, cells_z)
    return shards_fused(sizes, flow_field, test_streams, snapshot_ids)


def solution(mesh):
    in_specs = (P("groups", "vert", None, "gx", None, "gz"), P("groups"), P("groups", "vert"))
    out_specs = (
        P(("groups", "gx"), None),
        P(("groups", "gx", "gz", "vert"), None),
        P(("groups", "gz"), ("gx", "vert")),
        P(("groups", "gx"), None, None),
    )
    return jax.shard_map(shards, mesh=mesh, in_specs=in_specs, out_specs=out_specs, check_vma=False)
```

```python
import functools
import math

import jax
import jax.numpy as jnp
from jax import lax
from jax.experimental import pallas as pl
from jax.experimental.pallas import tpu as pltpu
from jax.sharding import PartitionSpec as P

K = 128
S = 48
E = 2


def hash_index(index, stream, salt):
    mixed = index * -1640531535 + stream * -2048144777 + salt
    mixed = jnp.bitwise_xor(mixed, lax.shift_right_logical(mixed, jnp.int32(16)))
    mixed = mixed * 739982445
    mixed = jnp.bitwise_xor(mixed, lax.shift_right_logical(mixed, jnp.int32(13)))
    mixed = mixed * 695872825
    return jnp.bitwise_xor(mixed, lax.shift_right_logical(mixed, jnp.int32(16)))


def unit_value(index, stream, salt):
    upper = lax.shift_right_logical(hash_index(index, stream, salt), jnp.int32(9))
    return ((2 * upper + 1).astype(jnp.float32) * 2.0 ** (-24) - 1.0).astype(jnp.bfloat16)


def test_table(row_ids, col_ids, stride, stream, salt):
    return unit_value(row_ids[:, None] * stride + col_ids[None, :], stream, salt)


def shards_general(flow_field, test_streams, snapshot_ids):
    highest = lax.Precision.HIGHEST
    batches, local_snaps, variables, cells_x, cells_y, cells_z = flow_field.shape
    slabs_x = lax.axis_size("gx")
    total_x = cells_x * slabs_x
    total_z = cells_z * lax.axis_size("gz")
    total_q = variables * batches * local_snaps * lax.axis_size("vert")
    factor_stream = test_streams[0]
    core_stream = test_streams[1]
    rank_ids = jnp.arange(K, dtype=jnp.int32)
    sketch_ids = jnp.arange(S, dtype=jnp.int32)
    x_ids = lax.axis_index("gx") * cells_x + jnp.arange(cells_x, dtype=jnp.int32)
    y_ids = jnp.arange(cells_y, dtype=jnp.int32)
    z_ids = lax.axis_index("gz") * cells_z + jnp.arange(cells_z, dtype=jnp.int32)
    ax_tab = test_table(x_ids, rank_ids, K, factor_stream, 1).astype(jnp.float32)
    ay_low = test_table(y_ids, rank_ids, K, factor_stream, 2)
    az_low = test_table(z_ids, rank_ids, K, factor_stream, 3)
    ay_tab = ay_low.astype(jnp.float32)
    phy_low = test_table(sketch_ids, y_ids, cells_y, core_stream, 6)
    phz_low = test_table(sketch_ids, z_ids, total_z, core_stream, 7)

    def batch_terms(batch_idx):
        blocks = flow_field[batch_idx].reshape(-1, cells_x, cells_y, cells_z)
        pairs = blocks.shape[0]
        q_ids = (
            snapshot_ids[batch_idx][:, None] * variables
            + jnp.arange(variables, dtype=jnp.int32)[None, :]
        ).reshape(-1)
        aq_tab = test_table(q_ids, rank_ids, K, factor_stream, 4).astype(jnp.float32)
        phq_low = test_table(q_ids, jnp.arange(E, dtype=jnp.int32), E, core_stream, 8)
        rows_z = blocks.reshape(-1, cells_z)
        along_z = jnp.dot(rows_z, az_low, preferred_element_type=jnp.float32).reshape(
            pairs, cells_x, cells_y, K
        )
        along_y = jnp.einsum("qxyz,yk->qxzk", blocks, ay_low, preferred_element_type=jnp.float32)
        weights = aq_tab[:, None, :] * ax_tab[None, :, :]
        part_x = jnp.sum(
            jnp.sum(along_z * ay_tab[None, None, :, :], axis=2) * aq_tab[:, None, :], axis=0
        )
        part_y = jnp.sum(along_z * weights[:, :, None, :], axis=(0, 1))
        part_z = jnp.sum(along_y * weights[:, :, None, :], axis=(0, 1))
        first = jnp.dot(rows_z, phz_low.T, preferred_element_type=jnp.float32).reshape(
            pairs, cells_x, cells_y, S
        )
        second = jnp.einsum("qxyc,by->qxbc", first, phy_low.astype(jnp.float32), precision=highest)
        partial_core = jnp.einsum(
            "qxbc,qe->bcex", second, phq_low.astype(jnp.float32), precision=highest
        )
        return (part_x, part_y, part_z, partial_core.reshape(S * S, E, cells_x))

    def finish(part_x, part_y, part_z, partial_core):
        summed, sum_x = lax.psum((partial_core, part_x), ("gz", "vert"))
        phx_whole = test_table(
            sketch_ids, jnp.arange(total_x, dtype=jnp.int32), total_x, core_stream, 5
        ).astype(jnp.float32)
        core = jnp.einsum(
            "rex,ax->rea",
            lax.all_to_all(summed, "gx", split_axis=0, concat_axis=2, tiled=True),
            phx_whole,
            precision=highest,
        )
        sum_z = lax.psum_scatter(part_z, ("gx", "vert"), scatter_dimension=1, tiled=True)
        sum_y = lax.psum_scatter(part_y, ("gx", "gz", "vert"), scatter_dimension=0, tiled=True)
        return (sum_x, sum_y, sum_z, core)

    terms = [batch_terms(batch_idx) for batch_idx in range(batches)]
    totals = finish(terms[0][0], terms[0][1], terms[0][2], terms[0][3])
    for later in terms[1:]:
        latest = finish(later[0], later[1], later[2], later[3])
        totals = tuple((earlier + newer for earlier, newer in zip(totals, latest)))
    scale_x = 3.0**1.5 / math.sqrt(cells_y * total_z * total_q)
    scale_y = 3.0**1.5 / math.sqrt(total_x * total_z * total_q)
    scale_z = 3.0**1.5 / math.sqrt(total_x * cells_y * total_q)
    scale_core = 9.0 / math.sqrt(total_x * cells_y * total_z * total_q)
    return (totals[0] * scale_x, totals[1] * scale_y, totals[2] * scale_z, totals[3] * scale_core)


MESH = pl.DeviceIdType.MESH
PAD = 16


def iota(shape, dim):
    return lax.broadcasted_iota(jnp.int32, shape, dim)


def unit_f32(index, stream, salt):
    return unit_value(index, stream, salt).astype(jnp.float32)


def dot_f32(left, right):
    return jnp.dot(left, right, preferred_element_type=jnp.float32)


def dot_split(left, right):
    upper = left.astype(jnp.bfloat16)
    lower = (left - upper.astype(jnp.float32)).astype(jnp.bfloat16)
    return dot_f32(upper, right) + dot_f32(lower, right)


def sketch_kernel(
    sizes,
    scales,
    streams_hbm,
    snaps_hbm,
    flow_hbm,
    out_x,
    out_y,
    out_z,
    out_core,
    streams,
    snaps,
    flow,
    x_send,
    x_got,
    x_out,
    x_in,
    y_send,
    y_got,
    y_out,
    y_in,
    z_send,
    z_got,
    z_out,
    z_in,
    c_send,
    c_got,
    c_out,
    c_in,
    small_sem,
    load_sem,
    pair_send,
    pair_recv,
    x_ssem,
    x_rsem,
    y_ssem,
    y_rsem,
    c_ssem,
    c_rsem,
    z_ssem,
    z_rsem,
):
    slabs, zsplit, batches, local_snaps, variables, cells_y, cells_z = sizes
    scale_x, scale_y, scale_z, scale_core = scales
    pairs = batches * local_snaps
    total_q = pairs * variables
    chips = slabs * zsplit
    rows_y = cells_y // (2 * chips)
    rows_z = K // (2 * slabs)
    rows_m = S // slabs
    rows_c = slabs * PAD
    total_z = cells_z * zsplit
    gx = lax.axis_index("gx")
    gz = lax.axis_index("gz")
    vert = lax.axis_index("vert")
    other = 1 - vert
    offsets = [(dx, dz) for dx in range(slabs) for dz in range(zsplit)]
    far_first = sorted(range(1, chips), key=lambda i: -min(offsets[i][0], slabs - offsets[i][0]))

    def target(dx, dz):
        return {"gx": lax.rem(gx + dx, slabs), "gz": lax.rem(gz + dz, zsplit)}

    smalls = [
        pltpu.make_async_copy(streams_hbm, streams, small_sem.at[0]),
        pltpu.make_async_copy(snaps_hbm, snaps, small_sem.at[1]),
    ]
    loads = [
        pltpu.make_async_copy(
            flow_hbm.at[pl.ds(p * variables, variables)],
            flow.at[pl.ds(p * variables, variables)],
            load_sem.at[p],
        )
        for p in range(pairs)
    ]
    for load in smalls + loads:
        load.start()
    barrier = pltpu.get_barrier_semaphore()
    pl.semaphore_signal(barrier, inc=1, device_id={"vert": other}, device_id_type=MESH)
    for dx, dz in offsets[1:]:
        pl.semaphore_signal(barrier, inc=1, device_id=target(dx, dz), device_id_type=MESH)

    low = jnp.bfloat16
    select_at = iota((1, 640), 1)
    lane_m = select_at // S
    lane_n = select_at - lane_m * S
    spread = jnp.where((iota((K, 640), 0) & 63) == lane_n, 1.0, 0.0).astype(low)
    keep = (iota((rows_c, 640), 0) & (PAD - 1)) == lane_m
    for load in smalls:
        load.wait()
    fac = streams[0]
    cor = streams[1]

    def run_ids(q_index):
        ids = jnp.zeros(q_index.shape, jnp.int32)
        for q in range(total_q):
            p = q // variables
            run = snaps[p // local_snaps, p % local_snaps] * variables + q % variables
            ids = jnp.where(q_index == q, run, ids)
        return ids

    z_base = gz * cells_z
    ay_turned = unit_value(iota((K, cells_y), 1) * K + iota((K, cells_y), 0), fac, 2)
    m_row = iota((rows_c, cells_y), 0)
    m_ids = (m_row >> 4) * rows_m + (m_row & (PAD - 1))
    phy_tab = unit_value(m_ids * cells_y + iota((rows_c, cells_y), 1), cor, 6)
    turned = jnp.concatenate([ay_turned, phy_tab], axis=0)
    q_rows = -(-total_q // 8) * 8
    r_rows = run_ids(iota((q_rows, K), 0))
    aq_tab = unit_f32(r_rows * K + iota((q_rows, K), 1), fac, 4)
    phq_tab = [unit_f32(r_rows * E + e, cor, 8) for e in range(E)]
    aq_turned = unit_f32(run_ids(iota((1, K), 1)) * K + iota((K, K), 0), fac, 4)
    ax_turned = unit_f32(gx * K + iota((K, K), 0), fac, 1)
    weights = aq_turned * ax_turned

    deep = jnp.zeros((K, cells_z), jnp.float32)
    halves = [jnp.zeros((rows_c, cells_z), jnp.float32) for e in range(E)]
    waited = 0
    for first in range(0, total_q, 2):
        while waited * variables < min(first + 2, total_q):
            loads[waited].wait()
            waited += 1
        group = range(first, min(first + 2, total_q))
        both = dot_f32(turned, jnp.concatenate([flow[q] for q in group], axis=1))
        for i, q in enumerate(group):
            lanes = both[:, i * cells_z : (i + 1) * cells_z]
            deep = deep + lanes[:K] * weights[:, q : q + 1]
            for e in range(E):
                halves[e] = halves[e] + lanes[K:] * phq_tab[e][q : q + 1]
    for g in range(slabs):
        for v in range(2):
            at = (2 * g + v) * rows_z
            z_send[v, g] = deep[at : at + rows_z]

    pl.semaphore_wait(barrier, chips)

    def pair_copy(src, dst, which):
        return pltpu.make_async_remote_copy(
            src_ref=src,
            dst_ref=dst,
            send_sem=pair_send.at[which],
            recv_sem=pair_recv.at[which],
            device_id={"vert": other},
            device_id_type=MESH,
        )

    pair_z = pair_copy(z_send.at[other], z_got, 0)
    pair_z.start()
    lane = iota((cells_z, K), 1)
    phz_tab = unit_f32((lane & 63) * total_z + z_base + iota((cells_z, K), 0), cor, 7)
    core = None
    for e in range(E):
        right = jnp.where((lane >> 6) == e, phz_tab, 0.0).astype(low)
        part = dot_split(halves[e], right)
        core = part if core is None else core + part
    c_send[...] = core.reshape(slabs, PAD, K)
    pair_c = pair_copy(c_send, c_got, 1)
    pair_c.start()

    az_tab = unit_value(
        (z_base + iota((cells_z, K), 0)) * K + iota((cells_z, K), 1), fac, 3
    )
    ax_row = unit_f32(gx * K + iota((8, K), 1), fac, 1)[0:1]
    half = cells_y // 2
    pairs_y = []
    z_copies = []
    c_copies = [None] * chips
    x_row = jnp.zeros((1, K), jnp.float32)
    for h in range(2):
        wide = jnp.zeros((half, K), jnp.float32)
        for q in range(total_q):
            wide = wide + dot_f32(flow[q, h * half : (h + 1) * half], az_tab) * aq_tab[q : q + 1]
        y_index = h * half + iota((half, K), 0)
        ay_tab = unit_f32(y_index * K + iota((half, K), 1), fac, 2)
        x_row = x_row + jnp.sum(wide * ay_tab, axis=0, keepdims=True)
        wide = wide * ax_row
        for c in range(chips // 2):
            for v in range(2):
                at = (2 * c + v) * rows_y
                y_send[v, h * (chips // 2) + c] = wide[at : at + rows_y]
        at = pl.ds(h * (chips // 2), chips // 2)
        pair_y = pair_copy(y_send.at[other, at], y_got.at[at], 2 + h)
        pair_y.start()
        pairs_y.append(pair_y)
        if h == 0:
            pair_z.wait_recv()
            z_out[...] = z_send[vert] + z_got[...]
            for dx in range(1, slabs):
                to = lax.rem(gx + dx, slabs)
                copy = pltpu.make_async_remote_copy(
                    src_ref=z_out.at[to],
                    dst_ref=z_in.at[dx - 1],
                    send_sem=z_ssem.at[dx - 1],
                    recv_sem=z_rsem.at[dx - 1],
                    device_id={"gx": to},
                    device_id_type=MESH,
                )
                copy.start()
                z_copies.append(copy)
            pair_c.wait_recv()
            c_out[...] = c_send[...] + c_got[...]
            for i in far_first:
                dest = target(*offsets[i])
                copy = pltpu.make_async_remote_copy(
                    src_ref=c_out.at[dest["gx"]],
                    dst_ref=c_in.at[i - 1],
                    send_sem=c_ssem.at[i - 1],
                    recv_sem=c_rsem.at[i - 1],
                    device_id=dest,
                    device_id_type=MESH,
                )
                copy.start()
                c_copies[i] = copy
    x_send[...] = jnp.broadcast_to(x_row, x_send.shape)
    pair_x = pair_copy(x_send, x_got, 4)
    pair_x.start()

    for pair_y in pairs_y:
        pair_y.wait_recv()
    y_out[...] = y_send[vert] + y_got[...]
    y_copies = [None] * chips
    for i in far_first:
        dest = target(*offsets[i])
        copy = pltpu.make_async_remote_copy(
            src_ref=y_out.at[dest["gx"] * zsplit + dest["gz"]],
            dst_ref=y_in.at[i - 1],
            send_sem=y_ssem.at[i - 1],
            recv_sem=y_rsem.at[i - 1],
            device_id=dest,
            device_id_type=MESH,
        )
        copy.start()
        y_copies[i] = copy
    pair_x.wait_recv()
    x_out[...] = x_send[...] + x_got[...]
    x_copies = []
    for dz in range(1, zsplit):
        copy = pltpu.make_async_remote_copy(
            src_ref=x_out,
            dst_ref=x_in.at[dz - 1],
            send_sem=x_ssem.at[dz - 1],
            recv_sem=x_rsem.at[dz - 1],
            device_id={"gz": lax.rem(gz + dz, zsplit)},
            device_id_type=MESH,
        )
        copy.start()
        x_copies.append(copy)

    total = z_out[gx]
    for i, copy in enumerate(z_copies):
        copy.wait_recv()
        total = total + z_in[i]
    out_z[...] = total * scale_z
    slots = []
    for dx in range(slabs):
        total = c_out[gx] if dx == 0 else None
        for dz in range(zsplit):
            i = dx * zsplit + dz
            if i == 0:
                continue
            c_copies[i].wait_recv()
            total = c_in[i - 1] if total is None else total + c_in[i - 1]
        slots.append(total)
    core = jnp.concatenate(slots, axis=0) * scale_core
    upper = core.astype(low)
    lower = (core - upper.astype(jnp.float32)).astype(low)
    core_lane = iota((rows_c, K), 1) >> 6
    zero = jnp.zeros((rows_c, K), low)
    left = jnp.concatenate(
        [jnp.where(core_lane == e, part, zero) for e in range(E) for part in (upper, lower)],
        axis=0,
    )
    placed = dot_f32(left, spread)
    slot = iota((S, K), 1) >> 4
    x_ids = (gx - slot + 2 * slabs) & (slabs - 1)
    phx = unit_value(iota((S, K), 0) * slabs + x_ids, cor, 5)
    for e in range(E):
        at = 2 * e * rows_c
        right = jnp.concatenate(
            [
                jnp.where(keep, placed[at + s * rows_c : at + (s + 1) * rows_c], 0.0)
                for s in range(2)
            ],
            axis=0,
        ).astype(low)
        out_core[e] = dot_f32(phx, right)[:, : rows_m * S]

    total = x_out[...]
    for i, copy in enumerate(x_copies):
        copy.wait_recv()
        total = total + x_in[i]
    out_x[...] = total[0:1] * scale_x
    total = y_out[gx * zsplit + gz]
    for i in range(1, chips):
        y_copies[i].wait_recv()
        total = total + y_in[i - 1]
    out_y[...] = total * scale_y
    started = [pair_x, pair_z, pair_c] + pairs_y + x_copies + z_copies + c_copies[1:] + y_copies[1:]
    for copy in started:
        copy.wait_send()


def finish_kernel(*refs):
    sems = refs[-1]
    count = len(refs) // 2
    copies = [
        pltpu.make_async_copy(refs[i], refs[count + i], sems.at[i]) for i in range(count)
    ]
    for copy in copies:
        copy.start()
    for copy in copies:
        copy.wait()


def shards_fused(sizes, flow_field, test_streams, snapshot_ids):
    slabs, zsplit, batches, local_snaps, variables, cells_y, cells_z = sizes
    pairs = batches * local_snaps
    chips = slabs * zsplit
    rows_y = cells_y // (2 * chips)
    rows_z = K // (2 * slabs)
    rows_m = S // slabs
    total_q = pairs * variables
    f32 = jnp.float32
    anywhere = pl.BlockSpec(memory_space=pl.ANY)
    vmem = pl.BlockSpec(memory_space=pltpu.VMEM)
    dma = pltpu.SemaphoreType.DMA
    total_z = cells_z * zsplit
    all_q = 2 * total_q
    scales = (
        3.0**1.5 / math.sqrt(cells_y * total_z * all_q),
        3.0**1.5 / math.sqrt(slabs * total_z * all_q),
        3.0**1.5 / math.sqrt(slabs * cells_y * all_q),
        9.0 / math.sqrt(slabs * cells_y * total_z * all_q),
    )
    outs = [
        jax.ShapeDtypeStruct((1, K), f32),
        jax.ShapeDtypeStruct((rows_y, K), f32),
        jax.ShapeDtypeStruct((rows_z, cells_z), f32),
        jax.ShapeDtypeStruct((E, S, rows_m * S), f32),
    ]
    parts = pl.pallas_call(
        functools.partial(sketch_kernel, sizes, scales),
        name="sketch",
        out_shape=outs,
        in_specs=[anywhere] * 3,
        out_specs=[vmem] * 4,
        scratch_shapes=[
            pltpu.SMEM(test_streams.shape, jnp.int32),
            pltpu.SMEM(snapshot_ids.shape, jnp.int32),
            pltpu.VMEM((total_q, cells_y, cells_z), jnp.bfloat16),
            pltpu.VMEM((8, K), f32),
            pltpu.VMEM((8, K), f32),
            pltpu.VMEM((8, K), f32),
            pltpu.VMEM((zsplit - 1, 8, K), f32),
            pltpu.VMEM((2, chips, rows_y, K), f32),
            pltpu.VMEM((chips, rows_y, K), f32),
            pltpu.VMEM((chips, rows_y, K), f32),
            pltpu.VMEM((chips - 1, rows_y, K), f32),
            pltpu.VMEM((2, slabs, rows_z, cells_z), f32),
            pltpu.VMEM((slabs, rows_z, cells_z), f32),
            pltpu.VMEM((slabs, rows_z, cells_z), f32),
            pltpu.VMEM((slabs - 1, rows_z, cells_z), f32),
            pltpu.VMEM((slabs, PAD, K), f32),
            pltpu.VMEM((slabs, PAD, K), f32),
            pltpu.VMEM((slabs, PAD, K), f32),
            pltpu.VMEM((chips - 1, PAD, K), f32),
            dma((2,)),
            dma((pairs,)),
            dma((5,)),
            dma((5,)),
            dma((zsplit - 1,)),
            dma((zsplit - 1,)),
            dma((chips - 1,)),
            dma((chips - 1,)),
            dma((chips - 1,)),
            dma((chips - 1,)),
            dma((slabs - 1,)),
            dma((slabs - 1,)),
        ],
        compiler_params=pltpu.CompilerParams(
            collective_id=0, has_side_effects=True, vmem_limit_bytes=63 * 2**20
        ),
    )(test_streams, snapshot_ids, flow_field.reshape(total_q, cells_y, cells_z))
    out_x, out_y, out_z, out_core = pl.pallas_call(
        finish_kernel,
        name="finish",
        out_shape=outs,
        in_specs=[anywhere] * 4,
        out_specs=[anywhere] * 4,
        scratch_shapes=[dma((4,))],
        compiler_params=pltpu.CompilerParams(vmem_limit_bytes=63 * 2**20),
    )(*parts)
    return (out_x, out_y, out_z.T, jnp.transpose(out_core, (2, 0, 1)))


def shards(flow_field, test_streams, snapshot_ids):
    batches, local_snaps, variables, cells_x, cells_y, cells_z = flow_field.shape
    slabs = lax.axis_size("gx")
    zsplit = lax.axis_size("gz")
    fits = (
        lax.axis_size("vert") == 2
        and cells_x == 1
        and cells_z == K
        and cells_y % (16 * slabs * zsplit) == 0
        and slabs == 4
        and zsplit > 1
        and batches * local_snaps * variables <= K
    )
    if not fits:
        return shards_general(flow_field, test_streams, snapshot_ids)
    sizes = (slabs, zsplit, batches, local_snaps, variables, cells_y, cells_z)
    return shards_fused(sizes, flow_field, test_streams, snapshot_ids)


def solution(mesh):
    in_specs = (P("groups", "vert", None, "gx", None, "gz"), P("groups"), P("groups", "vert"))
    out_specs = (
        P(("groups", "gx"), None),
        P(("groups", "gx", "gz", "vert"), None),
        P(("groups", "gz"), ("gx", "vert")),
        P(("groups", "gx"), None, None),
    )
    return jax.shard_map(shards, mesh=mesh, in_specs=in_specs, out_specs=out_specs, check_vma=False)
```

```python
import functools
import math

import jax
import jax.numpy as jnp
from jax import lax
from jax.experimental import pallas as pl
from jax.experimental.pallas import tpu as pltpu
from jax.sharding import PartitionSpec as P

K = 128
S = 48
E = 2


def hash_index(index, stream, salt):
    mixed = index * -1640531535 + stream * -2048144777 + salt
    mixed = jnp.bitwise_xor(mixed, lax.shift_right_logical(mixed, jnp.int32(16)))
    mixed = mixed * 739982445
    mixed = jnp.bitwise_xor(mixed, lax.shift_right_logical(mixed, jnp.int32(13)))
    mixed = mixed * 695872825
    return jnp.bitwise_xor(mixed, lax.shift_right_logical(mixed, jnp.int32(16)))


def unit_value(index, stream, salt):
    upper = lax.shift_right_logical(hash_index(index, stream, salt), jnp.int32(9))
    return ((2 * upper + 1).astype(jnp.float32) * 2.0 ** (-24) - 1.0).astype(jnp.bfloat16)


def test_table(row_ids, col_ids, stride, stream, salt):
    return unit_value(row_ids[:, None] * stride + col_ids[None, :], stream, salt)


def shards_general(flow_field, test_streams, snapshot_ids):
    highest = lax.Precision.HIGHEST
    batches, local_snaps, variables, cells_x, cells_y, cells_z = flow_field.shape
    slabs_x = lax.axis_size("gx")
    total_x = cells_x * slabs_x
    total_z = cells_z * lax.axis_size("gz")
    total_q = variables * batches * local_snaps * lax.axis_size("vert")
    factor_stream = test_streams[0]
    core_stream = test_streams[1]
    rank_ids = jnp.arange(K, dtype=jnp.int32)
    sketch_ids = jnp.arange(S, dtype=jnp.int32)
    x_ids = lax.axis_index("gx") * cells_x + jnp.arange(cells_x, dtype=jnp.int32)
    y_ids = jnp.arange(cells_y, dtype=jnp.int32)
    z_ids = lax.axis_index("gz") * cells_z + jnp.arange(cells_z, dtype=jnp.int32)
    ax_tab = test_table(x_ids, rank_ids, K, factor_stream, 1).astype(jnp.float32)
    ay_low = test_table(y_ids, rank_ids, K, factor_stream, 2)
    az_low = test_table(z_ids, rank_ids, K, factor_stream, 3)
    ay_tab = ay_low.astype(jnp.float32)
    phy_low = test_table(sketch_ids, y_ids, cells_y, core_stream, 6)
    phz_low = test_table(sketch_ids, z_ids, total_z, core_stream, 7)

    def batch_terms(batch_idx):
        blocks = flow_field[batch_idx].reshape(-1, cells_x, cells_y, cells_z)
        pairs = blocks.shape[0]
        q_ids = (
            snapshot_ids[batch_idx][:, None] * variables
            + jnp.arange(variables, dtype=jnp.int32)[None, :]
        ).reshape(-1)
        aq_tab = test_table(q_ids, rank_ids, K, factor_stream, 4).astype(jnp.float32)
        phq_low = test_table(q_ids, jnp.arange(E, dtype=jnp.int32), E, core_stream, 8)
        rows_z = blocks.reshape(-1, cells_z)
        along_z = jnp.dot(rows_z, az_low, preferred_element_type=jnp.float32).reshape(
            pairs, cells_x, cells_y, K
        )
        along_y = jnp.einsum("qxyz,yk->qxzk", blocks, ay_low, preferred_element_type=jnp.float32)
        weights = aq_tab[:, None, :] * ax_tab[None, :, :]
        part_x = jnp.sum(
            jnp.sum(along_z * ay_tab[None, None, :, :], axis=2) * aq_tab[:, None, :], axis=0
        )
        part_y = jnp.sum(along_z * weights[:, :, None, :], axis=(0, 1))
        part_z = jnp.sum(along_y * weights[:, :, None, :], axis=(0, 1))
        first = jnp.dot(rows_z, phz_low.T, preferred_element_type=jnp.float32).reshape(
            pairs, cells_x, cells_y, S
        )
        second = jnp.einsum("qxyc,by->qxbc", first, phy_low.astype(jnp.float32), precision=highest)
        partial_core = jnp.einsum(
            "qxbc,qe->bcex", second, phq_low.astype(jnp.float32), precision=highest
        )
        return (part_x, part_y, part_z, partial_core.reshape(S * S, E, cells_x))

    def finish(part_x, part_y, part_z, partial_core):
        summed, sum_x = lax.psum((partial_core, part_x), ("gz", "vert"))
        phx_whole = test_table(
            sketch_ids, jnp.arange(total_x, dtype=jnp.int32), total_x, core_stream, 5
        ).astype(jnp.float32)
        core = jnp.einsum(
            "rex,ax->rea",
            lax.all_to_all(summed, "gx", split_axis=0, concat_axis=2, tiled=True),
            phx_whole,
            precision=highest,
        )
        sum_z = lax.psum_scatter(part_z, ("gx", "vert"), scatter_dimension=1, tiled=True)
        sum_y = lax.psum_scatter(part_y, ("gx", "gz", "vert"), scatter_dimension=0, tiled=True)
        return (sum_x, sum_y, sum_z, core)

    terms = [batch_terms(batch_idx) for batch_idx in range(batches)]
    totals = finish(terms[0][0], terms[0][1], terms[0][2], terms[0][3])
    for later in terms[1:]:
        latest = finish(later[0], later[1], later[2], later[3])
        totals = tuple((earlier + newer for earlier, newer in zip(totals, latest)))
    scale_x = 3.0**1.5 / math.sqrt(cells_y * total_z * total_q)
    scale_y = 3.0**1.5 / math.sqrt(total_x * total_z * total_q)
    scale_z = 3.0**1.5 / math.sqrt(total_x * cells_y * total_q)
    scale_core = 9.0 / math.sqrt(total_x * cells_y * total_z * total_q)
    return (totals[0] * scale_x, totals[1] * scale_y, totals[2] * scale_z, totals[3] * scale_core)


MESH = pl.DeviceIdType.MESH
PAD = 16


def iota(shape, dim):
    return lax.broadcasted_iota(jnp.int32, shape, dim)


def unit_f32(index, stream, salt):
    return unit_value(index, stream, salt).astype(jnp.float32)


def dot_f32(left, right):
    return jnp.dot(left, right, preferred_element_type=jnp.float32)


def dot_split(left, right):
    upper = left.astype(jnp.bfloat16)
    lower = (left - upper.astype(jnp.float32)).astype(jnp.bfloat16)
    return dot_f32(upper, right) + dot_f32(lower, right)


def sketch_kernel(
    sizes,
    scales,
    streams_hbm,
    snaps_hbm,
    flow_hbm,
    out_x,
    out_y,
    out_z,
    out_core,
    streams,
    snaps,
    flow,
    x_send,
    x_got,
    x_out,
    x_in,
    y_send,
    y_got,
    y_out,
    y_in,
    z_send,
    z_got,
    z_out,
    z_in,
    c_send,
    c_got,
    c_out,
    c_in,
    small_sem,
    load_sem,
    pair_send,
    pair_recv,
    x_ssem,
    x_rsem,
    y_ssem,
    y_rsem,
    c_ssem,
    c_rsem,
    z_ssem,
    z_rsem,
):
    slabs, zsplit, batches, local_snaps, variables, cells_y, cells_z = sizes
    scale_x, scale_y, scale_z, scale_core = scales
    pairs = batches * local_snaps
    total_q = pairs * variables
    chips = slabs * zsplit
    rows_y = cells_y // (2 * chips)
    rows_z = K // (2 * slabs)
    rows_m = S // slabs
    rows_c = slabs * PAD
    total_z = cells_z * zsplit
    gx = lax.axis_index("gx")
    gz = lax.axis_index("gz")
    vert = lax.axis_index("vert")
    other = 1 - vert
    offsets = [(dx, dz) for dx in range(slabs) for dz in range(zsplit)]
    far_first = sorted(range(1, chips), key=lambda i: -min(offsets[i][0], slabs - offsets[i][0]))

    def target(dx, dz):
        return {"gx": lax.rem(gx + dx, slabs), "gz": lax.rem(gz + dz, zsplit)}

    smalls = [
        pltpu.make_async_copy(streams_hbm, streams, small_sem.at[0]),
        pltpu.make_async_copy(snaps_hbm, snaps, small_sem.at[1]),
    ]
    loads = [
        pltpu.make_async_copy(
            flow_hbm.at[pl.ds(p * variables, variables)],
            flow.at[pl.ds(p * variables, variables)],
            load_sem.at[p],
        )
        for p in range(pairs)
    ]
    for load in smalls + loads:
        load.start()
    barrier = pltpu.get_barrier_semaphore()
    pl.semaphore_signal(barrier, inc=1, device_id={"vert": other}, device_id_type=MESH)
    for dx, dz in offsets[1:]:
        pl.semaphore_signal(barrier, inc=1, device_id=target(dx, dz), device_id_type=MESH)

    low = jnp.bfloat16
    select_at = iota((1, 640), 1)
    lane_m = select_at // S
    lane_n = select_at - lane_m * S
    spread = jnp.where((iota((K, 640), 0) & 63) == lane_n, 1.0, 0.0).astype(low)
    keep = (iota((rows_c, 640), 0) & (PAD - 1)) == lane_m
    for load in smalls:
        load.wait()
    fac = streams[0]
    cor = streams[1]

    def run_ids(q_index):
        ids = jnp.zeros(q_index.shape, jnp.int32)
        for q in range(total_q):
            p = q // variables
            run = snaps[p // local_snaps, p % local_snaps] * variables + q % variables
            ids = jnp.where(q_index == q, run, ids)
        return ids

    z_base = gz * cells_z
    ay_turned = unit_value(iota((K, cells_y), 1) * K + iota((K, cells_y), 0), fac, 2)
    m_row = iota((rows_c, cells_y), 0)
    m_ids = (m_row >> 4) * rows_m + (m_row & (PAD - 1))
    phy_tab = unit_value(m_ids * cells_y + iota((rows_c, cells_y), 1), cor, 6)
    turned = jnp.concatenate([ay_turned, phy_tab], axis=0)
    q_rows = -(-total_q // 8) * 8
    r_rows = run_ids(iota((q_rows, K), 0))
    aq_tab = unit_f32(r_rows * K + iota((q_rows, K), 1), fac, 4)
    phq_tab = [unit_f32(r_rows * E + e, cor, 8) for e in range(E)]
    aq_turned = unit_f32(run_ids(iota((1, K), 1)) * K + iota((K, K), 0), fac, 4)
    ax_turned = unit_f32(gx * K + iota((K, K), 0), fac, 1)
    weights = aq_turned * ax_turned

    deep = jnp.zeros((K, cells_z), jnp.float32)
    halves = [jnp.zeros((rows_c, cells_z), jnp.float32) for e in range(E)]
    waited = 0
    for first in range(0, total_q, 2):
        while waited * variables < min(first + 2, total_q):
            loads[waited].wait()
            waited += 1
        group = range(first, min(first + 2, total_q))
        both = dot_f32(turned, jnp.concatenate([flow[q] for q in group], axis=1))
        for i, q in enumerate(group):
            lanes = both[:, i * cells_z : (i + 1) * cells_z]
            deep = deep + lanes[:K] * weights[:, q : q + 1]
            for e in range(E):
                halves[e] = halves[e] + lanes[K:] * phq_tab[e][q : q + 1]
    for g in range(slabs):
        for v in range(2):
            at = (2 * g + v) * rows_z
            z_send[v, g] = deep[at : at + rows_z]

    pl.semaphore_wait(barrier, chips)

    def pair_copy(src, dst, which):
        return pltpu.make_async_remote_copy(
            src_ref=src,
            dst_ref=dst,
            send_sem=pair_send.at[which],
            recv_sem=pair_recv.at[which],
            device_id={"vert": other},
            device_id_type=MESH,
        )

    pair_z = pair_copy(z_send.at[other], z_got, 0)
    pair_z.start()
    lane = iota((cells_z, K), 1)
    phz_tab = unit_f32((lane & 63) * total_z + z_base + iota((cells_z, K), 0), cor, 7)
    core = None
    for e in range(E):
        right = jnp.where((lane >> 6) == e, phz_tab, 0.0).astype(low)
        part = dot_split(halves[e], right)
        core = part if core is None else core + part
    c_send[...] = core.reshape(slabs, PAD, K)
    pair_c = pair_copy(c_send, c_got, 1)
    pair_c.start()

    az_tab = unit_value(
        (z_base + iota((cells_z, K), 0)) * K + iota((cells_z, K), 1), fac, 3
    )
    ax_row = unit_f32(gx * K + iota((8, K), 1), fac, 1)[0:1]
    half = cells_y // 2
    pairs_y = []
    z_copies = []
    c_copies = [None] * chips
    x_row = jnp.zeros((1, K), jnp.float32)
    for h in range(2):
        wide = jnp.zeros((half, K), jnp.float32)
        for q in range(total_q):
            wide = wide + dot_f32(flow[q, h * half : (h + 1) * half], az_tab) * aq_tab[q : q + 1]
        y_index = h * half + iota((half, K), 0)
        ay_tab = unit_f32(y_index * K + iota((half, K), 1), fac, 2)
        x_row = x_row + jnp.sum(wide * ay_tab, axis=0, keepdims=True)
        wide = wide * ax_row
        for c in range(chips // 2):
            for v in range(2):
                at = (2 * c + v) * rows_y
                y_send[v, h * (chips // 2) + c] = wide[at : at + rows_y]
        at = pl.ds(h * (chips // 2), chips // 2)
        pair_y = pair_copy(y_send.at[other, at], y_got.at[at], 2 + h)
        pair_y.start()
        pairs_y.append(pair_y)
        if h == 0:
            pair_z.wait_recv()
            z_out[...] = z_send[vert] + z_got[...]
            for dx in range(1, slabs):
                to = lax.rem(gx + dx, slabs)
                copy = pltpu.make_async_remote_copy(
                    src_ref=z_out.at[to],
                    dst_ref=z_in.at[dx - 1],
                    send_sem=z_ssem.at[dx - 1],
                    recv_sem=z_rsem.at[dx - 1],
                    device_id={"gx": to},
                    device_id_type=MESH,
                )
                copy.start()
                z_copies.append(copy)
            pair_c.wait_recv()
            c_out[...] = c_send[...] + c_got[...]
            for i in far_first:
                dest = target(*offsets[i])
                copy = pltpu.make_async_remote_copy(
                    src_ref=c_out.at[dest["gx"]],
                    dst_ref=c_in.at[i - 1],
                    send_sem=c_ssem.at[i - 1],
                    recv_sem=c_rsem.at[i - 1],
                    device_id=dest,
                    device_id_type=MESH,
                )
                copy.start()
                c_copies[i] = copy
    x_send[...] = jnp.broadcast_to(x_row, x_send.shape)
    pair_x = pair_copy(x_send, x_got, 4)
    pair_x.start()

    for pair_y in pairs_y:
        pair_y.wait_recv()
    y_out[...] = y_send[vert] + y_got[...]
    y_copies = [None] * chips
    for i in far_first:
        dest = target(*offsets[i])
        copy = pltpu.make_async_remote_copy(
            src_ref=y_out.at[dest["gx"] * zsplit + dest["gz"]],
            dst_ref=y_in.at[i - 1],
            send_sem=y_ssem.at[i - 1],
            recv_sem=y_rsem.at[i - 1],
            device_id=dest,
            device_id_type=MESH,
        )
        copy.start()
        y_copies[i] = copy
    pair_x.wait_recv()
    x_out[...] = x_send[...] + x_got[...]
    x_copies = []
    for dz in range(1, zsplit):
        copy = pltpu.make_async_remote_copy(
            src_ref=x_out,
            dst_ref=x_in.at[dz - 1],
            send_sem=x_ssem.at[dz - 1],
            recv_sem=x_rsem.at[dz - 1],
            device_id={"gz": lax.rem(gz + dz, zsplit)},
            device_id_type=MESH,
        )
        copy.start()
        x_copies.append(copy)

    total = z_out[gx]
    for i, copy in enumerate(z_copies):
        copy.wait_recv()
        total = total + z_in[i]
    out_z[...] = total * scale_z
    slots = []
    for dx in range(slabs):
        total = c_out[gx] if dx == 0 else None
        for dz in range(zsplit):
            i = dx * zsplit + dz
            if i == 0:
                continue
            c_copies[i].wait_recv()
            total = c_in[i - 1] if total is None else total + c_in[i - 1]
        slots.append(total)
    core = jnp.concatenate(slots, axis=0) * scale_core
    upper = core.astype(low)
    lower = (core - upper.astype(jnp.float32)).astype(low)
    core_lane = iota((rows_c, K), 1) >> 6
    zero = jnp.zeros((rows_c, K), low)
    left = jnp.concatenate(
        [jnp.where(core_lane == e, part, zero) for e in range(E) for part in (upper, lower)],
        axis=0,
    )
    placed = dot_f32(left, spread)
    slot = iota((S, K), 1) >> 4
    x_ids = (gx - slot + 2 * slabs) & (slabs - 1)
    phx = unit_value(iota((S, K), 0) * slabs + x_ids, cor, 5)
    for e in range(E):
        at = 2 * e * rows_c
        right = jnp.concatenate(
            [
                jnp.where(keep, placed[at + s * rows_c : at + (s + 1) * rows_c], 0.0)
                for s in range(2)
            ],
            axis=0,
        ).astype(low)
        out_core[e] = dot_f32(phx, right)[:, : rows_m * S]

    total = x_out[...]
    for i, copy in enumerate(x_copies):
        copy.wait_recv()
        total = total + x_in[i]
    out_x[...] = total[0:1] * scale_x
    total = y_out[gx * zsplit + gz]
    for i in range(1, chips):
        y_copies[i].wait_recv()
        total = total + y_in[i - 1]
    out_y[...] = total * scale_y
    started = [pair_x, pair_z, pair_c] + pairs_y + x_copies + z_copies + c_copies[1:] + y_copies[1:]
    for copy in started:
        copy.wait_send()


def finish_kernel(*refs):
    count = len(refs) // 2
    for i in range(count):
        refs[count + i][...] = refs[i][...]


def shards_fused(sizes, flow_field, test_streams, snapshot_ids):
    slabs, zsplit, batches, local_snaps, variables, cells_y, cells_z = sizes
    pairs = batches * local_snaps
    chips = slabs * zsplit
    rows_y = cells_y // (2 * chips)
    rows_z = K // (2 * slabs)
    rows_m = S // slabs
    total_q = pairs * variables
    f32 = jnp.float32
    anywhere = pl.BlockSpec(memory_space=pl.ANY)
    vmem = pl.BlockSpec(memory_space=pltpu.VMEM)
    dma = pltpu.SemaphoreType.DMA
    total_z = cells_z * zsplit
    all_q = 2 * total_q
    scales = (
        3.0**1.5 / math.sqrt(cells_y * total_z * all_q),
        3.0**1.5 / math.sqrt(slabs * total_z * all_q),
        3.0**1.5 / math.sqrt(slabs * cells_y * all_q),
        9.0 / math.sqrt(slabs * cells_y * total_z * all_q),
    )
    outs = [
        jax.ShapeDtypeStruct((1, K), f32),
        jax.ShapeDtypeStruct((rows_y, K), f32),
        jax.ShapeDtypeStruct((rows_z, cells_z), f32),
        jax.ShapeDtypeStruct((E, S, rows_m * S), f32),
    ]
    parts = pl.pallas_call(
        functools.partial(sketch_kernel, sizes, scales),
        name="sketch",
        out_shape=outs,
        in_specs=[anywhere] * 3,
        out_specs=[vmem] * 4,
        scratch_shapes=[
            pltpu.SMEM(test_streams.shape, jnp.int32),
            pltpu.SMEM(snapshot_ids.shape, jnp.int32),
            pltpu.VMEM((total_q, cells_y, cells_z), jnp.bfloat16),
            pltpu.VMEM((8, K), f32),
            pltpu.VMEM((8, K), f32),
            pltpu.VMEM((8, K), f32),
            pltpu.VMEM((zsplit - 1, 8, K), f32),
            pltpu.VMEM((2, chips, rows_y, K), f32),
            pltpu.VMEM((chips, rows_y, K), f32),
            pltpu.VMEM((chips, rows_y, K), f32),
            pltpu.VMEM((chips - 1, rows_y, K), f32),
            pltpu.VMEM((2, slabs, rows_z, cells_z), f32),
            pltpu.VMEM((slabs, rows_z, cells_z), f32),
            pltpu.VMEM((slabs, rows_z, cells_z), f32),
            pltpu.VMEM((slabs - 1, rows_z, cells_z), f32),
            pltpu.VMEM((slabs, PAD, K), f32),
            pltpu.VMEM((slabs, PAD, K), f32),
            pltpu.VMEM((slabs, PAD, K), f32),
            pltpu.VMEM((chips - 1, PAD, K), f32),
            dma((2,)),
            dma((pairs,)),
            dma((5,)),
            dma((5,)),
            dma((zsplit - 1,)),
            dma((zsplit - 1,)),
            dma((chips - 1,)),
            dma((chips - 1,)),
            dma((chips - 1,)),
            dma((chips - 1,)),
            dma((slabs - 1,)),
            dma((slabs - 1,)),
        ],
        compiler_params=pltpu.CompilerParams(
            collective_id=0, has_side_effects=True, vmem_limit_bytes=63 * 2**20
        ),
    )(test_streams, snapshot_ids, flow_field.reshape(total_q, cells_y, cells_z))
    out_x, out_y, out_z, out_core = pl.pallas_call(
        finish_kernel,
        name="finish",
        out_shape=outs,
        in_specs=[vmem] * 4,
        out_specs=[vmem] * 4,
        compiler_params=pltpu.CompilerParams(vmem_limit_bytes=63 * 2**20),
    )(*parts)
    return (out_x, out_y, out_z.T, jnp.transpose(out_core, (2, 0, 1)))


def shards(flow_field, test_streams, snapshot_ids):
    batches, local_snaps, variables, cells_x, cells_y, cells_z = flow_field.shape
    slabs = lax.axis_size("gx")
    zsplit = lax.axis_size("gz")
    fits = (
        lax.axis_size("vert") == 2
        and cells_x == 1
        and cells_z == K
        and cells_y % (16 * slabs * zsplit) == 0
        and slabs == 4
        and zsplit > 1
        and batches * local_snaps * variables <= K
    )
    if not fits:
        return shards_general(flow_field, test_streams, snapshot_ids)
    sizes = (slabs, zsplit, batches, local_snaps, variables, cells_y, cells_z)
    return shards_fused(sizes, flow_field, test_streams, snapshot_ids)


def solution(mesh):
    in_specs = (P("groups", "vert", None, "gx", None, "gz"), P("groups"), P("groups", "vert"))
    out_specs = (
        P(("groups", "gx"), None),
        P(("groups", "gx", "gz", "vert"), None),
        P(("groups", "gz"), ("gx", "vert")),
        P(("groups", "gx"), None, None),
    )
    return jax.shard_map(shards, mesh=mesh, in_specs=in_specs, out_specs=out_specs, check_vma=False)
```

```python
import functools
import math

import jax
import jax.numpy as jnp
from jax import lax
from jax.experimental import pallas as pl
from jax.experimental.pallas import tpu as pltpu
from jax.sharding import PartitionSpec as P

K = 128
S = 48
E = 2


def hash_index(index, stream, salt):
    mixed = index * -1640531535 + stream * -2048144777 + salt
    mixed = jnp.bitwise_xor(mixed, lax.shift_right_logical(mixed, jnp.int32(16)))
    mixed = mixed * 739982445
    mixed = jnp.bitwise_xor(mixed, lax.shift_right_logical(mixed, jnp.int32(13)))
    mixed = mixed * 695872825
    return jnp.bitwise_xor(mixed, lax.shift_right_logical(mixed, jnp.int32(16)))


def unit_value(index, stream, salt):
    upper = lax.shift_right_logical(hash_index(index, stream, salt), jnp.int32(9))
    return ((2 * upper + 1).astype(jnp.float32) * 2.0 ** (-24) - 1.0).astype(jnp.bfloat16)


def test_table(row_ids, col_ids, stride, stream, salt):
    return unit_value(row_ids[:, None] * stride + col_ids[None, :], stream, salt)


def shards_general(flow_field, test_streams, snapshot_ids):
    highest = lax.Precision.HIGHEST
    batches, local_snaps, variables, cells_x, cells_y, cells_z = flow_field.shape
    slabs_x = lax.axis_size("gx")
    total_x = cells_x * slabs_x
    total_z = cells_z * lax.axis_size("gz")
    total_q = variables * batches * local_snaps * lax.axis_size("vert")
    factor_stream = test_streams[0]
    core_stream = test_streams[1]
    rank_ids = jnp.arange(K, dtype=jnp.int32)
    sketch_ids = jnp.arange(S, dtype=jnp.int32)
    x_ids = lax.axis_index("gx") * cells_x + jnp.arange(cells_x, dtype=jnp.int32)
    y_ids = jnp.arange(cells_y, dtype=jnp.int32)
    z_ids = lax.axis_index("gz") * cells_z + jnp.arange(cells_z, dtype=jnp.int32)
    ax_tab = test_table(x_ids, rank_ids, K, factor_stream, 1).astype(jnp.float32)
    ay_low = test_table(y_ids, rank_ids, K, factor_stream, 2)
    az_low = test_table(z_ids, rank_ids, K, factor_stream, 3)
    ay_tab = ay_low.astype(jnp.float32)
    phy_low = test_table(sketch_ids, y_ids, cells_y, core_stream, 6)
    phz_low = test_table(sketch_ids, z_ids, total_z, core_stream, 7)

    def batch_terms(batch_idx):
        blocks = flow_field[batch_idx].reshape(-1, cells_x, cells_y, cells_z)
        pairs = blocks.shape[0]
        q_ids = (
            snapshot_ids[batch_idx][:, None] * variables
            + jnp.arange(variables, dtype=jnp.int32)[None, :]
        ).reshape(-1)
        aq_tab = test_table(q_ids, rank_ids, K, factor_stream, 4).astype(jnp.float32)
        phq_low = test_table(q_ids, jnp.arange(E, dtype=jnp.int32), E, core_stream, 8)
        rows_z = blocks.reshape(-1, cells_z)
        along_z = jnp.dot(rows_z, az_low, preferred_element_type=jnp.float32).reshape(
            pairs, cells_x, cells_y, K
        )
        along_y = jnp.einsum("qxyz,yk->qxzk", blocks, ay_low, preferred_element_type=jnp.float32)
        weights = aq_tab[:, None, :] * ax_tab[None, :, :]
        part_x = jnp.sum(
            jnp.sum(along_z * ay_tab[None, None, :, :], axis=2) * aq_tab[:, None, :], axis=0
        )
        part_y = jnp.sum(along_z * weights[:, :, None, :], axis=(0, 1))
        part_z = jnp.sum(along_y * weights[:, :, None, :], axis=(0, 1))
        first = jnp.dot(rows_z, phz_low.T, preferred_element_type=jnp.float32).reshape(
            pairs, cells_x, cells_y, S
        )
        second = jnp.einsum("qxyc,by->qxbc", first, phy_low.astype(jnp.float32), precision=highest)
        partial_core = jnp.einsum(
            "qxbc,qe->bcex", second, phq_low.astype(jnp.float32), precision=highest
        )
        return (part_x, part_y, part_z, partial_core.reshape(S * S, E, cells_x))

    def finish(part_x, part_y, part_z, partial_core):
        summed, sum_x = lax.psum((partial_core, part_x), ("gz", "vert"))
        phx_whole = test_table(
            sketch_ids, jnp.arange(total_x, dtype=jnp.int32), total_x, core_stream, 5
        ).astype(jnp.float32)
        core = jnp.einsum(
            "rex,ax->rea",
            lax.all_to_all(summed, "gx", split_axis=0, concat_axis=2, tiled=True),
            phx_whole,
            precision=highest,
        )
        sum_z = lax.psum_scatter(part_z, ("gx", "vert"), scatter_dimension=1, tiled=True)
        sum_y = lax.psum_scatter(part_y, ("gx", "gz", "vert"), scatter_dimension=0, tiled=True)
        return (sum_x, sum_y, sum_z, core)

    terms = [batch_terms(batch_idx) for batch_idx in range(batches)]
    totals = finish(terms[0][0], terms[0][1], terms[0][2], terms[0][3])
    for later in terms[1:]:
        latest = finish(later[0], later[1], later[2], later[3])
        totals = tuple((earlier + newer for earlier, newer in zip(totals, latest)))
    scale_x = 3.0**1.5 / math.sqrt(cells_y * total_z * total_q)
    scale_y = 3.0**1.5 / math.sqrt(total_x * total_z * total_q)
    scale_z = 3.0**1.5 / math.sqrt(total_x * cells_y * total_q)
    scale_core = 9.0 / math.sqrt(total_x * cells_y * total_z * total_q)
    return (totals[0] * scale_x, totals[1] * scale_y, totals[2] * scale_z, totals[3] * scale_core)


MESH = pl.DeviceIdType.MESH
PAD = 16


def iota(shape, dim):
    return lax.broadcasted_iota(jnp.int32, shape, dim)


def unit_f32(index, stream, salt):
    return unit_value(index, stream, salt).astype(jnp.float32)


def dot_f32(left, right):
    return jnp.dot(left, right, preferred_element_type=jnp.float32)


def dot_split(left, right):
    upper = left.astype(jnp.bfloat16)
    lower = (left - upper.astype(jnp.float32)).astype(jnp.bfloat16)
    return dot_f32(upper, right) + dot_f32(lower, right)


def sketch_kernel(
    sizes,
    scales,
    streams_hbm,
    snaps_hbm,
    flow_hbm,
    out_x,
    out_y,
    out_z,
    out_core,
    streams,
    snaps,
    flow,
    y_send,
    y_got,
    y_out,
    y_in,
    z_send,
    z_got,
    z_out,
    z_in,
    c_send,
    c_got,
    c_out,
    c_in,
    small_sem,
    load_sem,
    pair_send,
    pair_recv,
    y_ssem,
    y_rsem,
    c_ssem,
    c_rsem,
    z_ssem,
    z_rsem,
):
    slabs, zsplit, batches, local_snaps, variables, cells_y, cells_z = sizes
    scale_x, scale_y, scale_z, scale_core = scales
    pairs = batches * local_snaps
    total_q = pairs * variables
    chips = slabs * zsplit
    rows_y = cells_y // (2 * chips)
    rows_z = K // (2 * slabs)
    rows_m = S // slabs
    rows_c = slabs * PAD
    total_z = cells_z * zsplit
    gx = lax.axis_index("gx")
    gz = lax.axis_index("gz")
    vert = lax.axis_index("vert")
    other = 1 - vert
    offsets = [(dx, dz) for dx in range(slabs) for dz in range(zsplit)]
    far_first = sorted(range(1, chips), key=lambda i: -min(offsets[i][0], slabs - offsets[i][0]))

    def target(dx, dz):
        return {"gx": lax.rem(gx + dx, slabs), "gz": lax.rem(gz + dz, zsplit)}

    smalls = [
        pltpu.make_async_copy(streams_hbm, streams, small_sem.at[0]),
        pltpu.make_async_copy(snaps_hbm, snaps, small_sem.at[1]),
    ]
    loads = [
        pltpu.make_async_copy(
            flow_hbm.at[pl.ds(p * variables, variables)],
            flow.at[pl.ds(p * variables, variables)],
            load_sem.at[p],
        )
        for p in range(pairs)
    ]
    for load in smalls + loads:
        load.start()
    barrier = pltpu.get_barrier_semaphore()
    pl.semaphore_signal(barrier, inc=1, device_id={"vert": other}, device_id_type=MESH)
    for dx, dz in offsets[1:]:
        pl.semaphore_signal(barrier, inc=1, device_id=target(dx, dz), device_id_type=MESH)

    low = jnp.bfloat16
    select_at = iota((1, 640), 1)
    lane_m = select_at // S
    lane_n = select_at - lane_m * S
    spread = jnp.where((iota((K, 640), 0) & 63) == lane_n, 1.0, 0.0).astype(low)
    keep = (iota((rows_c, 640), 0) & (PAD - 1)) == lane_m
    for load in smalls:
        load.wait()
    fac = streams[0]
    cor = streams[1]

    def run_ids(q_index):
        ids = jnp.zeros(q_index.shape, jnp.int32)
        for q in range(total_q):
            p = q // variables
            run = snaps[p // local_snaps, p % local_snaps] * variables + q % variables
            ids = jnp.where(q_index == q, run, ids)
        return ids

    z_base = gz * cells_z
    ay_turned = unit_value(iota((K, cells_y), 1) * K + iota((K, cells_y), 0), fac, 2)
    m_row = iota((rows_c, cells_y), 0)
    m_ids = (m_row >> 4) * rows_m + (m_row & (PAD - 1))
    phy_tab = unit_value(m_ids * cells_y + iota((rows_c, cells_y), 1), cor, 6)
    turned = jnp.concatenate([ay_turned, phy_tab], axis=0)
    q_rows = -(-total_q // 8) * 8
    r_rows = run_ids(iota((q_rows, K), 0))
    aq_tab = unit_f32(r_rows * K + iota((q_rows, K), 1), fac, 4)
    phq_tab = [unit_f32(r_rows * E + e, cor, 8) for e in range(E)]
    aq_turned = unit_f32(run_ids(iota((1, K), 1)) * K + iota((K, K), 0), fac, 4)
    ax_turned = unit_f32(gx * K + iota((K, K), 0), fac, 1)
    az_tab = unit_value(
        (z_base + iota((cells_z, K), 0)) * K + iota((cells_z, K), 1), fac, 3
    )

    deep = jnp.zeros((K, cells_z), jnp.float32)
    halves = [jnp.zeros((rows_c, cells_z), jnp.float32) for e in range(E)]
    waited = 0
    for first in range(0, total_q, 2):
        while waited * variables < min(first + 2, total_q):
            loads[waited].wait()
            waited += 1
        group = range(first, min(first + 2, total_q))
        both = dot_f32(turned, jnp.concatenate([flow[q].reshape(cells_y, cells_z) for q in group], axis=1))
        for i, q in enumerate(group):
            lanes = both[:, i * cells_z : (i + 1) * cells_z]
            deep = deep + lanes[:K] * aq_turned[:, q : q + 1]
            for e in range(E):
                halves[e] = halves[e] + lanes[K:] * phq_tab[e][q : q + 1]
    for g in range(slabs):
        for v in range(2):
            at = (2 * g + v) * rows_z
            z_send[v, g] = deep[at : at + rows_z] * ax_turned[at : at + rows_z]

    pl.semaphore_wait(barrier, chips)

    def pair_copy(src, dst, which):
        return pltpu.make_async_remote_copy(
            src_ref=src,
            dst_ref=dst,
            send_sem=pair_send.at[which],
            recv_sem=pair_recv.at[which],
            device_id={"vert": other},
            device_id_type=MESH,
        )

    pair_z = pair_copy(z_send.at[other], z_got, 0)
    pair_z.start()
    lane = iota((cells_z, K), 1)
    phz_tab = unit_f32((lane & 63) * total_z + z_base + iota((cells_z, K), 0), cor, 7)
    core = None
    for e in range(E):
        right = jnp.where((lane >> 6) == e, phz_tab, 0.0).astype(low)
        part = dot_split(halves[e], right)
        core = part if core is None else core + part
    x_row = jnp.sum(deep.T * az_tab.astype(jnp.float32), axis=0, keepdims=True)
    core = jnp.where((iota((rows_c, K), 0) & (PAD - 1)) == rows_m, x_row, core)
    c_send[...] = core.reshape(slabs, PAD, K)
    pair_c = pair_copy(c_send, c_got, 1)
    pair_c.start()

    ax_row = unit_f32(gx * K + iota((8, K), 1), fac, 1)[0:1]
    z_copies = []
    c_copies = [None] * chips
    for h, side in enumerate((other, vert)):
        wide = jnp.zeros((chips * rows_y, K), jnp.float32)
        for q in range(total_q):
            rows = flow[q, :, side].reshape(chips * rows_y, cells_z)
            wide = wide + dot_f32(rows, az_tab) * aq_tab[q : q + 1]
        wide = (wide * ax_row).reshape(chips, rows_y, K)
        if h == 0:
            y_send[...] = wide
            pair_y = pair_copy(y_send, y_got, 2)
            pair_y.start()
        if h == 0:
            pair_z.wait_recv()
            z_out[...] = z_send[vert] + z_got[...]
            for dx in range(1, slabs):
                to = lax.rem(gx + dx, slabs)
                copy = pltpu.make_async_remote_copy(
                    src_ref=z_out.at[to],
                    dst_ref=z_in.at[dx - 1],
                    send_sem=z_ssem.at[dx - 1],
                    recv_sem=z_rsem.at[dx - 1],
                    device_id={"gx": to},
                    device_id_type=MESH,
                )
                copy.start()
                z_copies.append(copy)
            pair_c.wait_recv()
            c_out[...] = c_send[...] + c_got[...]
            for i in far_first:
                dest = target(*offsets[i])
                copy = pltpu.make_async_remote_copy(
                    src_ref=c_out.at[dest["gx"]],
                    dst_ref=c_in.at[i - 1],
                    send_sem=c_ssem.at[i - 1],
                    recv_sem=c_rsem.at[i - 1],
                    device_id=dest,
                    device_id_type=MESH,
                )
                copy.start()
                c_copies[i] = copy
    pair_y.wait_recv()
    y_out[...] = wide + y_got[...]
    y_copies = [None] * chips
    for i in far_first:
        dest = target(*offsets[i])
        copy = pltpu.make_async_remote_copy(
            src_ref=y_out.at[dest["gx"] * zsplit + dest["gz"]],
            dst_ref=y_in.at[i - 1],
            send_sem=y_ssem.at[i - 1],
            recv_sem=y_rsem.at[i - 1],
            device_id=dest,
            device_id_type=MESH,
        )
        copy.start()
        y_copies[i] = copy
    total = z_out[gx]
    for i, copy in enumerate(z_copies):
        copy.wait_recv()
        total = total + z_in[i]
    out_z[...] = total * scale_z
    slots = []
    for dx in range(slabs):
        total = c_out[gx] if dx == 0 else None
        for dz in range(zsplit):
            i = dx * zsplit + dz
            if i == 0:
                continue
            c_copies[i].wait_recv()
            total = c_in[i - 1] if total is None else total + c_in[i - 1]
        slots.append(total)
    out_x[...] = slots[0][rows_m : rows_m + 1] * scale_x
    core = jnp.concatenate(slots, axis=0) * scale_core
    upper = core.astype(low)
    lower = (core - upper.astype(jnp.float32)).astype(low)
    core_lane = iota((rows_c, K), 1) >> 6
    zero = jnp.zeros((rows_c, K), low)
    left = jnp.concatenate(
        [jnp.where(core_lane == e, part, zero) for e in range(E) for part in (upper, lower)],
        axis=0,
    )
    placed = dot_f32(left, spread)
    slot = iota((S, K), 1) >> 4
    x_ids = (gx - slot + 2 * slabs) & (slabs - 1)
    phx = unit_value(iota((S, K), 0) * slabs + x_ids, cor, 5)
    for e in range(E):
        at = 2 * e * rows_c
        right = jnp.concatenate(
            [
                jnp.where(keep, placed[at + s * rows_c : at + (s + 1) * rows_c], 0.0)
                for s in range(2)
            ],
            axis=0,
        ).astype(low)
        out_core[e] = dot_f32(phx, right)[:, : rows_m * S]

    total = y_out[gx * zsplit + gz]
    for i in range(1, chips):
        y_copies[i].wait_recv()
        total = total + y_in[i - 1]
    out_y[...] = total * scale_y
    started = [pair_z, pair_c, pair_y] + z_copies + c_copies[1:] + y_copies[1:]
    for copy in started:
        copy.wait_send()


def finish_kernel(*refs):
    count = len(refs) // 2
    for i in range(count):
        refs[count + i][...] = refs[i][...]


def shards_fused(sizes, flow_field, test_streams, snapshot_ids):
    slabs, zsplit, batches, local_snaps, variables, cells_y, cells_z = sizes
    pairs = batches * local_snaps
    chips = slabs * zsplit
    rows_y = cells_y // (2 * chips)
    rows_z = K // (2 * slabs)
    rows_m = S // slabs
    total_q = pairs * variables
    f32 = jnp.float32
    anywhere = pl.BlockSpec(memory_space=pl.ANY)
    vmem = pl.BlockSpec(memory_space=pltpu.VMEM)
    dma = pltpu.SemaphoreType.DMA
    total_z = cells_z * zsplit
    all_q = 2 * total_q
    scales = (
        3.0**1.5 / math.sqrt(cells_y * total_z * all_q),
        3.0**1.5 / math.sqrt(slabs * total_z * all_q),
        3.0**1.5 / math.sqrt(slabs * cells_y * all_q),
        9.0 / math.sqrt(slabs * cells_y * total_z * all_q),
    )
    outs = [
        jax.ShapeDtypeStruct((1, K), f32),
        jax.ShapeDtypeStruct((rows_y, K), f32),
        jax.ShapeDtypeStruct((rows_z, cells_z), f32),
        jax.ShapeDtypeStruct((E, S, rows_m * S), f32),
    ]
    parts = pl.pallas_call(
        functools.partial(sketch_kernel, sizes, scales),
        name="sketch",
        out_shape=outs,
        in_specs=[anywhere] * 3,
        out_specs=[vmem] * 4,
        scratch_shapes=[
            pltpu.SMEM(test_streams.shape, jnp.int32),
            pltpu.SMEM(snapshot_ids.shape, jnp.int32),
            pltpu.VMEM((total_q, chips, 2, rows_y, cells_z), jnp.bfloat16),
            pltpu.VMEM((chips, rows_y, K), f32),
            pltpu.VMEM((chips, rows_y, K), f32),
            pltpu.VMEM((chips, rows_y, K), f32),
            pltpu.VMEM((chips - 1, rows_y, K), f32),
            pltpu.VMEM((2, slabs, rows_z, cells_z), f32),
            pltpu.VMEM((slabs, rows_z, cells_z), f32),
            pltpu.VMEM((slabs, rows_z, cells_z), f32),
            pltpu.VMEM((slabs - 1, rows_z, cells_z), f32),
            pltpu.VMEM((slabs, PAD, K), f32),
            pltpu.VMEM((slabs, PAD, K), f32),
            pltpu.VMEM((slabs, PAD, K), f32),
            pltpu.VMEM((chips - 1, PAD, K), f32),
            dma((2,)),
            dma((pairs,)),
            dma((3,)),
            dma((3,)),
            dma((chips - 1,)),
            dma((chips - 1,)),
            dma((chips - 1,)),
            dma((chips - 1,)),
            dma((slabs - 1,)),
            dma((slabs - 1,)),
        ],
        compiler_params=pltpu.CompilerParams(
            collective_id=0, has_side_effects=True, vmem_limit_bytes=63 * 2**20
        ),
    )(test_streams, snapshot_ids, flow_field.reshape(total_q, chips, 2, rows_y, cells_z))
    out_x, out_y, out_z, out_core = pl.pallas_call(
        finish_kernel,
        name="finish",
        out_shape=outs,
        in_specs=[vmem] * 4,
        out_specs=[vmem] * 4,
        compiler_params=pltpu.CompilerParams(vmem_limit_bytes=63 * 2**20),
    )(*parts)
    return (out_x, out_y, out_z.T, jnp.transpose(out_core, (2, 0, 1)))


def shards(flow_field, test_streams, snapshot_ids):
    batches, local_snaps, variables, cells_x, cells_y, cells_z = flow_field.shape
    slabs = lax.axis_size("gx")
    zsplit = lax.axis_size("gz")
    fits = (
        lax.axis_size("vert") == 2
        and cells_x == 1
        and cells_z == K
        and cells_y % (16 * slabs * zsplit) == 0
        and slabs == 4
        and zsplit > 1
        and cells_y % (32 * slabs * zsplit) == 0
        and batches * local_snaps * variables <= K
    )
    if not fits:
        return shards_general(flow_field, test_streams, snapshot_ids)
    sizes = (slabs, zsplit, batches, local_snaps, variables, cells_y, cells_z)
    return shards_fused(sizes, flow_field, test_streams, snapshot_ids)


def solution(mesh):
    in_specs = (P("groups", "vert", None, "gx", None, "gz"), P("groups"), P("groups", "vert"))
    out_specs = (
        P(("groups", "gx"), None),
        P(("groups", "gx", "gz", "vert"), None),
        P(("groups", "gz"), ("gx", "vert")),
        P(("groups", "gx"), None, None),
    )
    return jax.shard_map(shards, mesh=mesh, in_specs=in_specs, out_specs=out_specs, check_vma=False)
```

```python
import functools
import math

import jax
import jax.numpy as jnp
from jax import lax
from jax.experimental import pallas as pl
from jax.experimental.pallas import tpu as pltpu
from jax.sharding import PartitionSpec as P

K = 128
S = 48
E = 2


def hash_index(index, stream, salt):
    mixed = index * -1640531535 + stream * -2048144777 + salt
    mixed = jnp.bitwise_xor(mixed, lax.shift_right_logical(mixed, jnp.int32(16)))
    mixed = mixed * 739982445
    mixed = jnp.bitwise_xor(mixed, lax.shift_right_logical(mixed, jnp.int32(13)))
    mixed = mixed * 695872825
    return jnp.bitwise_xor(mixed, lax.shift_right_logical(mixed, jnp.int32(16)))


def unit_value(index, stream, salt):
    upper = lax.shift_right_logical(hash_index(index, stream, salt), jnp.int32(9))
    return ((2 * upper + 1).astype(jnp.float32) * 2.0 ** (-24) - 1.0).astype(jnp.bfloat16)


def test_table(row_ids, col_ids, stride, stream, salt):
    return unit_value(row_ids[:, None] * stride + col_ids[None, :], stream, salt)


def shards_general(flow_field, test_streams, snapshot_ids):
    highest = lax.Precision.HIGHEST
    batches, local_snaps, variables, cells_x, cells_y, cells_z = flow_field.shape
    slabs_x = lax.axis_size("gx")
    total_x = cells_x * slabs_x
    total_z = cells_z * lax.axis_size("gz")
    total_q = variables * batches * local_snaps * lax.axis_size("vert")
    factor_stream = test_streams[0]
    core_stream = test_streams[1]
    rank_ids = jnp.arange(K, dtype=jnp.int32)
    sketch_ids = jnp.arange(S, dtype=jnp.int32)
    x_ids = lax.axis_index("gx") * cells_x + jnp.arange(cells_x, dtype=jnp.int32)
    y_ids = jnp.arange(cells_y, dtype=jnp.int32)
    z_ids = lax.axis_index("gz") * cells_z + jnp.arange(cells_z, dtype=jnp.int32)
    ax_tab = test_table(x_ids, rank_ids, K, factor_stream, 1).astype(jnp.float32)
    ay_low = test_table(y_ids, rank_ids, K, factor_stream, 2)
    az_low = test_table(z_ids, rank_ids, K, factor_stream, 3)
    ay_tab = ay_low.astype(jnp.float32)
    phy_low = test_table(sketch_ids, y_ids, cells_y, core_stream, 6)
    phz_low = test_table(sketch_ids, z_ids, total_z, core_stream, 7)

    def batch_terms(batch_idx):
        blocks = flow_field[batch_idx].reshape(-1, cells_x, cells_y, cells_z)
        pairs = blocks.shape[0]
        q_ids = (
            snapshot_ids[batch_idx][:, None] * variables
            + jnp.arange(variables, dtype=jnp.int32)[None, :]
        ).reshape(-1)
        aq_tab = test_table(q_ids, rank_ids, K, factor_stream, 4).astype(jnp.float32)
        phq_low = test_table(q_ids, jnp.arange(E, dtype=jnp.int32), E, core_stream, 8)
        rows_z = blocks.reshape(-1, cells_z)
        along_z = jnp.dot(rows_z, az_low, preferred_element_type=jnp.float32).reshape(
            pairs, cells_x, cells_y, K
        )
        along_y = jnp.einsum("qxyz,yk->qxzk", blocks, ay_low, preferred_element_type=jnp.float32)
        weights = aq_tab[:, None, :] * ax_tab[None, :, :]
        part_x = jnp.sum(
            jnp.sum(along_z * ay_tab[None, None, :, :], axis=2) * aq_tab[:, None, :], axis=0
        )
        part_y = jnp.sum(along_z * weights[:, :, None, :], axis=(0, 1))
        part_z = jnp.sum(along_y * weights[:, :, None, :], axis=(0, 1))
        first = jnp.dot(rows_z, phz_low.T, preferred_element_type=jnp.float32).reshape(
            pairs, cells_x, cells_y, S
        )
        second = jnp.einsum("qxyc,by->qxbc", first, phy_low.astype(jnp.float32), precision=highest)
        partial_core = jnp.einsum(
            "qxbc,qe->bcex", second, phq_low.astype(jnp.float32), precision=highest
        )
        return (part_x, part_y, part_z, partial_core.reshape(S * S, E, cells_x))

    def finish(part_x, part_y, part_z, partial_core):
        summed, sum_x = lax.psum((partial_core, part_x), ("gz", "vert"))
        phx_whole = test_table(
            sketch_ids, jnp.arange(total_x, dtype=jnp.int32), total_x, core_stream, 5
        ).astype(jnp.float32)
        core = jnp.einsum(
            "rex,ax->rea",
            lax.all_to_all(summed, "gx", split_axis=0, concat_axis=2, tiled=True),
            phx_whole,
            precision=highest,
        )
        sum_z = lax.psum_scatter(part_z, ("gx", "vert"), scatter_dimension=1, tiled=True)
        sum_y = lax.psum_scatter(part_y, ("gx", "gz", "vert"), scatter_dimension=0, tiled=True)
        return (sum_x, sum_y, sum_z, core)

    terms = [batch_terms(batch_idx) for batch_idx in range(batches)]
    totals = finish(terms[0][0], terms[0][1], terms[0][2], terms[0][3])
    for later in terms[1:]:
        latest = finish(later[0], later[1], later[2], later[3])
        totals = tuple((earlier + newer for earlier, newer in zip(totals, latest)))
    scale_x = 3.0**1.5 / math.sqrt(cells_y * total_z * total_q)
    scale_y = 3.0**1.5 / math.sqrt(total_x * total_z * total_q)
    scale_z = 3.0**1.5 / math.sqrt(total_x * cells_y * total_q)
    scale_core = 9.0 / math.sqrt(total_x * cells_y * total_z * total_q)
    return (totals[0] * scale_x, totals[1] * scale_y, totals[2] * scale_z, totals[3] * scale_core)


MESH = pl.DeviceIdType.MESH
PAD = 16
GROUP = 4


def iota(shape, dim):
    return lax.broadcasted_iota(jnp.int32, shape, dim)


def unit_f32(index, stream, salt):
    return unit_value(index, stream, salt).astype(jnp.float32)


def dot_f32(left, right):
    return jnp.dot(left, right, preferred_element_type=jnp.float32)


def dot_split(left, right):
    upper = left.astype(jnp.bfloat16)
    lower = (left - upper.astype(jnp.float32)).astype(jnp.bfloat16)
    return dot_f32(upper, right) + dot_f32(lower, right)


def sketch_kernel(
    sizes,
    scales,
    streams_hbm,
    snaps_hbm,
    flow_hbm,
    out_x,
    out_y,
    out_z,
    out_core,
    streams,
    snaps,
    flow,
    row_tabs,
    col_tabs,
    y_send,
    y_got,
    y_out,
    y_in,
    z_send,
    z_got,
    z_out,
    z_in,
    c_send,
    c_got,
    c_out,
    c_in,
    small_sem,
    load_sem,
    pair_send,
    pair_recv,
    y_ssem,
    y_rsem,
    c_ssem,
    c_rsem,
    z_ssem,
    z_rsem,
):
    slabs, zsplit, batches, local_snaps, variables, cells_y, cells_z = sizes
    scale_x, scale_y, scale_z, scale_core = scales
    pairs = batches * local_snaps
    total_q = pairs * variables
    chips = slabs * zsplit
    rows_y = cells_y // (2 * chips)
    rows_z = K // (2 * slabs)
    rows_m = S // slabs
    rows_c = slabs * PAD
    total_z = cells_z * zsplit
    gx = lax.axis_index("gx")
    gz = lax.axis_index("gz")
    vert = lax.axis_index("vert")
    other = 1 - vert
    offsets = [(dx, dz) for dx in range(slabs) for dz in range(zsplit)]
    far_first = sorted(range(1, chips), key=lambda i: -min(offsets[i][0], slabs - offsets[i][0]))

    def target(dx, dz):
        return {"gx": lax.rem(gx + dx, slabs), "gz": lax.rem(gz + dz, zsplit)}

    smalls = [
        pltpu.make_async_copy(streams_hbm, streams, small_sem.at[0]),
        pltpu.make_async_copy(snaps_hbm, snaps, small_sem.at[1]),
    ]
    loads = [
        pltpu.make_async_copy(
            flow_hbm.at[pl.ds(p * variables, variables)],
            flow.at[pl.ds(p * variables, variables)],
            load_sem.at[p],
        )
        for p in range(pairs)
    ]
    for load in smalls + loads:
        load.start()
    barrier = pltpu.get_barrier_semaphore()
    pl.semaphore_signal(barrier, inc=1, device_id={"vert": other}, device_id_type=MESH)
    for dx, dz in offsets[1:]:
        pl.semaphore_signal(barrier, inc=1, device_id=target(dx, dz), device_id_type=MESH)

    low = jnp.bfloat16
    select_at = iota((1, 640), 1)
    lane_m = select_at // S
    lane_n = select_at - lane_m * S
    spread = jnp.where((iota((K, 640), 0) & 63) == lane_n, 1.0, 0.0).astype(low)
    keep = (iota((rows_c, 640), 0) & (PAD - 1)) == lane_m
    for load in smalls:
        load.wait()
    fac = streams[0]
    cor = streams[1]

    def run_ids(q_index):
        ids = jnp.zeros(q_index.shape, jnp.int32)
        for q in range(total_q):
            p = q // variables
            run = snaps[p // local_snaps, p % local_snaps] * variables + q % variables
            ids = jnp.where(q_index == q, run, ids)
        return ids

    z_base = gz * cells_z
    ay_turned = unit_value(iota((K, cells_y), 1) * K + iota((K, cells_y), 0), fac, 2)
    m_row = iota((rows_c, cells_y), 0)
    m_ids = (m_row >> 4) * rows_m + (m_row & (PAD - 1))
    phy_tab = unit_value(m_ids * cells_y + iota((rows_c, cells_y), 1), cor, 6)
    turned = jnp.concatenate([ay_turned, phy_tab], axis=0)
    q_rows = -(-total_q // 8) * 8
    r_rows = run_ids(iota((q_rows, K), 0))
    row_tabs[0] = unit_f32(r_rows * K + iota((q_rows, K), 1), fac, 4)
    for e in range(E):
        row_tabs[1 + e] = unit_f32(r_rows * E + e, cor, 8)
    aq_turned = unit_f32(run_ids(iota((1, K), 1)) * K + iota((K, K), 0), fac, 4)
    for i in range(total_q // GROUP):
        col_tabs[i] = pltpu.roll(aq_turned, K - i * GROUP, 1) if i else aq_turned
    ax_turned = unit_f32(gx * K + iota((K, K), 0), fac, 1)
    az_tab = unit_value(
        (z_base + iota((cells_z, K), 0)) * K + iota((cells_z, K), 1), fac, 3
    )

    for load in loads:
        load.wait()

    def project_y(i, carry):
        deep, halves = carry[0], list(carry[1:])
        for first in range(0, GROUP, 2):
            at = i * GROUP + first
            planes = [flow[at + j].reshape(cells_y, cells_z) for j in range(2)]
            both = dot_f32(turned, jnp.concatenate(planes, axis=1))
            for j in range(2):
                lanes = both[:, j * cells_z : (j + 1) * cells_z]
                deep = deep + lanes[:K] * col_tabs[i, :, first + j : first + j + 1]
                for e in range(E):
                    halves[e] = halves[e] + lanes[K:] * row_tabs[1 + e, pl.ds(at + j, 1), :]
        return (deep, *halves)

    start = [jnp.zeros((rows, cells_z), jnp.float32) for rows in [K] + [rows_c] * E]
    deep, *halves = lax.fori_loop(0, total_q // GROUP, project_y, tuple(start))
    for g in range(slabs):
        for v in range(2):
            at = (2 * g + v) * rows_z
            z_send[v, g] = deep[at : at + rows_z] * ax_turned[at : at + rows_z]

    pl.semaphore_wait(barrier, chips)

    def pair_copy(src, dst, which):
        return pltpu.make_async_remote_copy(
            src_ref=src,
            dst_ref=dst,
            send_sem=pair_send.at[which],
            recv_sem=pair_recv.at[which],
            device_id={"vert": other},
            device_id_type=MESH,
        )

    pair_z = pair_copy(z_send.at[other], z_got, 0)
    pair_z.start()
    lane = iota((cells_z, K), 1)
    phz_tab = unit_f32((lane & 63) * total_z + z_base + iota((cells_z, K), 0), cor, 7)
    core = None
    for e in range(E):
        right = jnp.where((lane >> 6) == e, phz_tab, 0.0).astype(low)
        part = dot_split(halves[e], right)
        core = part if core is None else core + part
    x_row = jnp.sum(deep.T * az_tab.astype(jnp.float32), axis=0, keepdims=True)
    core = jnp.where((iota((rows_c, K), 0) & (PAD - 1)) == rows_m, x_row, core)
    c_send[...] = core.reshape(slabs, PAD, K)
    pair_c = pair_copy(c_send, c_got, 1)
    pair_c.start()

    ax_row = unit_f32(gx * K + iota((8, K), 1), fac, 1)[0:1]
    z_copies = []
    c_copies = [None] * chips
    for h, side in enumerate((other, vert)):

        def project_z(i, wide, side=side):
            for j in range(GROUP):
                q = i * GROUP + j
                rows = flow[q, :, side].reshape(chips * rows_y, cells_z)
                wide = wide + dot_f32(rows, az_tab) * row_tabs[0, pl.ds(q, 1), :]
            return wide

        start = jnp.zeros((chips * rows_y, K), jnp.float32)
        wide = lax.fori_loop(0, total_q // GROUP, project_z, start)
        wide = (wide * ax_row).reshape(chips, rows_y, K)
        if h == 0:
            y_send[...] = wide
            pair_y = pair_copy(y_send, y_got, 2)
            pair_y.start()
        if h == 0:
            pair_z.wait_recv()
            z_out[...] = z_send[vert] + z_got[...]
            for dx in range(1, slabs):
                to = lax.rem(gx + dx, slabs)
                copy = pltpu.make_async_remote_copy(
                    src_ref=z_out.at[to],
                    dst_ref=z_in.at[dx - 1],
                    send_sem=z_ssem.at[dx - 1],
                    recv_sem=z_rsem.at[dx - 1],
                    device_id={"gx": to},
                    device_id_type=MESH,
                )
                copy.start()
                z_copies.append(copy)
            pair_c.wait_recv()
            c_out[...] = c_send[...] + c_got[...]
            for i in far_first:
                dest = target(*offsets[i])
                copy = pltpu.make_async_remote_copy(
                    src_ref=c_out.at[dest["gx"]],
                    dst_ref=c_in.at[i - 1],
                    send_sem=c_ssem.at[i - 1],
                    recv_sem=c_rsem.at[i - 1],
                    device_id=dest,
                    device_id_type=MESH,
                )
                copy.start()
                c_copies[i] = copy
    pair_y.wait_recv()
    y_out[...] = wide + y_got[...]
    y_copies = [None] * chips
    for i in far_first:
        dest = target(*offsets[i])
        copy = pltpu.make_async_remote_copy(
            src_ref=y_out.at[dest["gx"] * zsplit + dest["gz"]],
            dst_ref=y_in.at[i - 1],
            send_sem=y_ssem.at[i - 1],
            recv_sem=y_rsem.at[i - 1],
            device_id=dest,
            device_id_type=MESH,
        )
        copy.start()
        y_copies[i] = copy
    total = z_out[gx]
    for i, copy in enumerate(z_copies):
        copy.wait_recv()
        total = total + z_in[i]
    out_z[...] = total * scale_z
    slots = []
    for dx in range(slabs):
        total = c_out[gx] if dx == 0 else None
        for dz in range(zsplit):
            i = dx * zsplit + dz
            if i == 0:
                continue
            c_copies[i].wait_recv()
            total = c_in[i - 1] if total is None else total + c_in[i - 1]
        slots.append(total)
    out_x[...] = slots[0][rows_m : rows_m + 1] * scale_x
    core = jnp.concatenate(slots, axis=0) * scale_core
    upper = core.astype(low)
    lower = (core - upper.astype(jnp.float32)).astype(low)
    core_lane = iota((rows_c, K), 1) >> 6
    zero = jnp.zeros((rows_c, K), low)
    left = jnp.concatenate(
        [jnp.where(core_lane == e, part, zero) for e in range(E) for part in (upper, lower)],
        axis=0,
    )
    placed = dot_f32(left, spread)
    slot = iota((S, K), 1) >> 4
    x_ids = (gx - slot + 2 * slabs) & (slabs - 1)
    phx = unit_value(iota((S, K), 0) * slabs + x_ids, cor, 5)
    for e in range(E):
        at = 2 * e * rows_c
        right = jnp.concatenate(
            [
                jnp.where(keep, placed[at + s * rows_c : at + (s + 1) * rows_c], 0.0)
                for s in range(2)
            ],
            axis=0,
        ).astype(low)
        out_core[e] = dot_f32(phx, right)[:, : rows_m * S]

    total = y_out[gx * zsplit + gz]
    for i in range(1, chips):
        y_copies[i].wait_recv()
        total = total + y_in[i - 1]
    out_y[...] = total * scale_y
    started = [pair_z, pair_c, pair_y] + z_copies + c_copies[1:] + y_copies[1:]
    for copy in started:
        copy.wait_send()


def finish_kernel(*refs):
    count = len(refs) // 2
    for i in range(count):
        refs[count + i][...] = refs[i][...]


def shards_fused(sizes, flow_field, test_streams, snapshot_ids):
    slabs, zsplit, batches, local_snaps, variables, cells_y, cells_z = sizes
    pairs = batches * local_snaps
    chips = slabs * zsplit
    rows_y = cells_y // (2 * chips)
    rows_z = K // (2 * slabs)
    rows_m = S // slabs
    total_q = pairs * variables
    f32 = jnp.float32
    anywhere = pl.BlockSpec(memory_space=pl.ANY)
    vmem = pl.BlockSpec(memory_space=pltpu.VMEM)
    dma = pltpu.SemaphoreType.DMA
    total_z = cells_z * zsplit
    all_q = 2 * total_q
    scales = (
        3.0**1.5 / math.sqrt(cells_y * total_z * all_q),
        3.0**1.5 / math.sqrt(slabs * total_z * all_q),
        3.0**1.5 / math.sqrt(slabs * cells_y * all_q),
        9.0 / math.sqrt(slabs * cells_y * total_z * all_q),
    )
    outs = [
        jax.ShapeDtypeStruct((1, K), f32),
        jax.ShapeDtypeStruct((rows_y, K), f32),
        jax.ShapeDtypeStruct((rows_z, cells_z), f32),
        jax.ShapeDtypeStruct((E, S, rows_m * S), f32),
    ]
    parts = pl.pallas_call(
        functools.partial(sketch_kernel, sizes, scales),
        name="sketch",
        out_shape=outs,
        in_specs=[anywhere] * 3,
        out_specs=[vmem] * 4,
        scratch_shapes=[
            pltpu.SMEM(test_streams.shape, jnp.int32),
            pltpu.SMEM(snapshot_ids.shape, jnp.int32),
            pltpu.VMEM((total_q, chips, 2, rows_y, cells_z), jnp.bfloat16),
            pltpu.VMEM((1 + E, -(-total_q // 8) * 8, K), f32),
            pltpu.VMEM((total_q // GROUP, K, K), f32),
            pltpu.VMEM((chips, rows_y, K), f32),
            pltpu.VMEM((chips, rows_y, K), f32),
            pltpu.VMEM((chips, rows_y, K), f32),
            pltpu.VMEM((chips - 1, rows_y, K), f32),
            pltpu.VMEM((2, slabs, rows_z, cells_z), f32),
            pltpu.VMEM((slabs, rows_z, cells_z), f32),
            pltpu.VMEM((slabs, rows_z, cells_z), f32),
            pltpu.VMEM((slabs - 1, rows_z, cells_z), f32),
            pltpu.VMEM((slabs, PAD, K), f32),
            pltpu.VMEM((slabs, PAD, K), f32),
            pltpu.VMEM((slabs, PAD, K), f32),
            pltpu.VMEM((chips - 1, PAD, K), f32),
            dma((2,)),
            dma((pairs,)),
            dma((3,)),
            dma((3,)),
            dma((chips - 1,)),
            dma((chips - 1,)),
            dma((chips - 1,)),
            dma((chips - 1,)),
            dma((slabs - 1,)),
            dma((slabs - 1,)),
        ],
        compiler_params=pltpu.CompilerParams(
            collective_id=0, has_side_effects=True, vmem_limit_bytes=63 * 2**20
        ),
    )(test_streams, snapshot_ids, flow_field.reshape(total_q, chips, 2, rows_y, cells_z))
    out_x, out_y, out_z, out_core = pl.pallas_call(
        finish_kernel,
        name="finish",
        out_shape=outs,
        in_specs=[vmem] * 4,
        out_specs=[vmem] * 4,
        compiler_params=pltpu.CompilerParams(vmem_limit_bytes=63 * 2**20),
    )(*parts)
    return (out_x, out_y, out_z.T, jnp.transpose(out_core, (2, 0, 1)))


def shards(flow_field, test_streams, snapshot_ids):
    batches, local_snaps, variables, cells_x, cells_y, cells_z = flow_field.shape
    slabs = lax.axis_size("gx")
    zsplit = lax.axis_size("gz")
    fits = (
        lax.axis_size("vert") == 2
        and cells_x == 1
        and cells_z == K
        and cells_y % (16 * slabs * zsplit) == 0
        and slabs == 4
        and zsplit > 1
        and batches * local_snaps * variables % GROUP == 0
        and cells_y % (32 * slabs * zsplit) == 0
        and batches * local_snaps * variables <= K
    )
    if not fits:
        return shards_general(flow_field, test_streams, snapshot_ids)
    sizes = (slabs, zsplit, batches, local_snaps, variables, cells_y, cells_z)
    return shards_fused(sizes, flow_field, test_streams, snapshot_ids)


def solution(mesh):
    in_specs = (P("groups", "vert", None, "gx", None, "gz"), P("groups"), P("groups", "vert"))
    out_specs = (
        P(("groups", "gx"), None),
        P(("groups", "gx", "gz", "vert"), None),
        P(("groups", "gz"), ("gx", "vert")),
        P(("groups", "gx"), None, None),
    )
    return jax.shard_map(shards, mesh=mesh, in_specs=in_specs, out_specs=out_specs, check_vma=False)
```

```python
import functools
import math

import jax
import jax.numpy as jnp
from jax import lax
from jax.experimental import pallas as pl
from jax.experimental.pallas import tpu as pltpu
from jax.sharding import PartitionSpec as P

K = 128
S = 48
E = 2


def hash_index(index, stream, salt):
    mixed = index * -1640531535 + stream * -2048144777 + salt
    mixed = jnp.bitwise_xor(mixed, lax.shift_right_logical(mixed, jnp.int32(16)))
    mixed = mixed * 739982445
    mixed = jnp.bitwise_xor(mixed, lax.shift_right_logical(mixed, jnp.int32(13)))
    mixed = mixed * 695872825
    return jnp.bitwise_xor(mixed, lax.shift_right_logical(mixed, jnp.int32(16)))


def unit_value(index, stream, salt):
    upper = lax.shift_right_logical(hash_index(index, stream, salt), jnp.int32(9))
    return ((2 * upper + 1).astype(jnp.float32) * 2.0 ** (-24) - 1.0).astype(jnp.bfloat16)


def test_table(row_ids, col_ids, stride, stream, salt):
    return unit_value(row_ids[:, None] * stride + col_ids[None, :], stream, salt)


def shards_general(flow_field, test_streams, snapshot_ids):
    highest = lax.Precision.HIGHEST
    batches, local_snaps, variables, cells_x, cells_y, cells_z = flow_field.shape
    slabs_x = lax.axis_size("gx")
    total_x = cells_x * slabs_x
    total_z = cells_z * lax.axis_size("gz")
    total_q = variables * batches * local_snaps * lax.axis_size("vert")
    factor_stream = test_streams[0]
    core_stream = test_streams[1]
    rank_ids = jnp.arange(K, dtype=jnp.int32)
    sketch_ids = jnp.arange(S, dtype=jnp.int32)
    x_ids = lax.axis_index("gx") * cells_x + jnp.arange(cells_x, dtype=jnp.int32)
    y_ids = jnp.arange(cells_y, dtype=jnp.int32)
    z_ids = lax.axis_index("gz") * cells_z + jnp.arange(cells_z, dtype=jnp.int32)
    ax_tab = test_table(x_ids, rank_ids, K, factor_stream, 1).astype(jnp.float32)
    ay_low = test_table(y_ids, rank_ids, K, factor_stream, 2)
    az_low = test_table(z_ids, rank_ids, K, factor_stream, 3)
    ay_tab = ay_low.astype(jnp.float32)
    phy_low = test_table(sketch_ids, y_ids, cells_y, core_stream, 6)
    phz_low = test_table(sketch_ids, z_ids, total_z, core_stream, 7)

    def batch_terms(batch_idx):
        blocks = flow_field[batch_idx].reshape(-1, cells_x, cells_y, cells_z)
        pairs = blocks.shape[0]
        q_ids = (
            snapshot_ids[batch_idx][:, None] * variables
            + jnp.arange(variables, dtype=jnp.int32)[None, :]
        ).reshape(-1)
        aq_tab = test_table(q_ids, rank_ids, K, factor_stream, 4).astype(jnp.float32)
        phq_low = test_table(q_ids, jnp.arange(E, dtype=jnp.int32), E, core_stream, 8)
        rows_z = blocks.reshape(-1, cells_z)
        along_z = jnp.dot(rows_z, az_low, preferred_element_type=jnp.float32).reshape(
            pairs, cells_x, cells_y, K
        )
        along_y = jnp.einsum("qxyz,yk->qxzk", blocks, ay_low, preferred_element_type=jnp.float32)
        weights = aq_tab[:, None, :] * ax_tab[None, :, :]
        part_x = jnp.sum(
            jnp.sum(along_z * ay_tab[None, None, :, :], axis=2) * aq_tab[:, None, :], axis=0
        )
        part_y = jnp.sum(along_z * weights[:, :, None, :], axis=(0, 1))
        part_z = jnp.sum(along_y * weights[:, :, None, :], axis=(0, 1))
        first = jnp.dot(rows_z, phz_low.T, preferred_element_type=jnp.float32).reshape(
            pairs, cells_x, cells_y, S
        )
        second = jnp.einsum("qxyc,by->qxbc", first, phy_low.astype(jnp.float32), precision=highest)
        partial_core = jnp.einsum(
            "qxbc,qe->bcex", second, phq_low.astype(jnp.float32), precision=highest
        )
        return (part_x, part_y, part_z, partial_core.reshape(S * S, E, cells_x))

    def finish(part_x, part_y, part_z, partial_core):
        summed, sum_x = lax.psum((partial_core, part_x), ("gz", "vert"))
        phx_whole = test_table(
            sketch_ids, jnp.arange(total_x, dtype=jnp.int32), total_x, core_stream, 5
        ).astype(jnp.float32)
        core = jnp.einsum(
            "rex,ax->rea",
            lax.all_to_all(summed, "gx", split_axis=0, concat_axis=2, tiled=True),
            phx_whole,
            precision=highest,
        )
        sum_z = lax.psum_scatter(part_z, ("gx", "vert"), scatter_dimension=1, tiled=True)
        sum_y = lax.psum_scatter(part_y, ("gx", "gz", "vert"), scatter_dimension=0, tiled=True)
        return (sum_x, sum_y, sum_z, core)

    terms = [batch_terms(batch_idx) for batch_idx in range(batches)]
    totals = finish(terms[0][0], terms[0][1], terms[0][2], terms[0][3])
    for later in terms[1:]:
        latest = finish(later[0], later[1], later[2], later[3])
        totals = tuple((earlier + newer for earlier, newer in zip(totals, latest)))
    scale_x = 3.0**1.5 / math.sqrt(cells_y * total_z * total_q)
    scale_y = 3.0**1.5 / math.sqrt(total_x * total_z * total_q)
    scale_z = 3.0**1.5 / math.sqrt(total_x * cells_y * total_q)
    scale_core = 9.0 / math.sqrt(total_x * cells_y * total_z * total_q)
    return (totals[0] * scale_x, totals[1] * scale_y, totals[2] * scale_z, totals[3] * scale_core)


MESH = pl.DeviceIdType.MESH
PAD = 16


def iota(shape, dim):
    return lax.broadcasted_iota(jnp.int32, shape, dim)


def unit_f32(index, stream, salt):
    return unit_value(index, stream, salt).astype(jnp.float32)


def dot_f32(left, right):
    return jnp.dot(left, right, preferred_element_type=jnp.float32)


def dot_split(left, right):
    upper = left.astype(jnp.bfloat16)
    lower = (left - upper.astype(jnp.float32)).astype(jnp.bfloat16)
    return dot_f32(upper, right) + dot_f32(lower, right)


def sketch_kernel(
    sizes,
    scales,
    streams_hbm,
    snaps_hbm,
    flow_hbm,
    out_x,
    out_y,
    out_z,
    out_core,
    streams,
    snaps,
    flow,
    y_send,
    y_got,
    y_out,
    y_in,
    z_send,
    z_got,
    z_out,
    z_in,
    c_send,
    c_got,
    c_out,
    c_in,
    small_sem,
    load_sem,
    pair_send,
    pair_recv,
    y_ssem,
    y_rsem,
    c_ssem,
    c_rsem,
    z_ssem,
    z_rsem,
):
    slabs, zsplit, batches, local_snaps, variables, cells_y, cells_z = sizes
    scale_x, scale_y, scale_z, scale_core = scales
    pairs = batches * local_snaps
    total_q = pairs * variables
    chips = slabs * zsplit
    rows_y = cells_y // (2 * chips)
    rows_z = K // (2 * slabs)
    rows_m = S // slabs
    rows_c = slabs * PAD
    total_z = cells_z * zsplit
    gx = lax.axis_index("gx")
    gz = lax.axis_index("gz")
    vert = lax.axis_index("vert")
    other = 1 - vert
    offsets = [(dx, dz) for dx in range(slabs) for dz in range(zsplit)]
    far_first = sorted(range(1, chips), key=lambda i: -min(offsets[i][0], slabs - offsets[i][0]))

    def target(dx, dz):
        return {"gx": lax.rem(gx + dx, slabs), "gz": lax.rem(gz + dz, zsplit)}

    smalls = [
        pltpu.make_async_copy(streams_hbm, streams, small_sem.at[0]),
        pltpu.make_async_copy(snaps_hbm, snaps, small_sem.at[1]),
    ]
    loads = [
        pltpu.make_async_copy(
            flow_hbm.at[pl.ds(p * variables, variables)],
            flow.at[pl.ds(p * variables, variables)],
            load_sem.at[p],
        )
        for p in range(pairs)
    ]
    for load in smalls + loads:
        load.start()
    barrier = pltpu.get_barrier_semaphore()
    pl.semaphore_signal(barrier, inc=1, device_id={"vert": other}, device_id_type=MESH)
    for dx, dz in offsets[1:]:
        pl.semaphore_signal(barrier, inc=1, device_id=target(dx, dz), device_id_type=MESH)

    low = jnp.bfloat16
    for load in smalls:
        load.wait()
    fac = streams[0]
    cor = streams[1]

    def run_ids(q_index):
        ids = jnp.zeros(q_index.shape, jnp.int32)
        for q in range(total_q):
            p = q // variables
            run = snaps[p // local_snaps, p % local_snaps] * variables + q % variables
            ids = jnp.where(q_index == q, run, ids)
        return ids

    def pair_copy(src, dst, which):
        return pltpu.make_async_remote_copy(
            src_ref=src,
            dst_ref=dst,
            send_sem=pair_send.at[which],
            recv_sem=pair_recv.at[which],
            device_id={"vert": other},
            device_id_type=MESH,
        )

    z_base = gz * cells_z
    az_tab = unit_value(
        (z_base + iota((cells_z, K), 0)) * K + iota((cells_z, K), 1), fac, 3
    )
    q_rows = -(-total_q // 8) * 8
    r_rows = run_ids(iota((q_rows, K), 0))
    aq_tab = unit_f32(r_rows * K + iota((q_rows, K), 1), fac, 4)
    ax_row = unit_f32(gx * K + iota((8, K), 1), fac, 1)[0:1]
    for h, side in enumerate((other, vert)):
        wide = jnp.zeros((chips * rows_y, K), jnp.float32)
        for q in range(total_q):
            if h == 0 and q % variables == 0:
                loads[q // variables].wait()
            rows = flow[q, :, side].reshape(chips * rows_y, cells_z)
            wide = wide + dot_f32(rows, az_tab) * aq_tab[q : q + 1]
        wide = (wide * ax_row).reshape(chips, rows_y, K)
        if h == 0:
            y_send[...] = wide
            pl.semaphore_wait(barrier, chips)
            pair_y = pair_copy(y_send, y_got, 2)
            pair_y.start()

    ay_turned = unit_value(iota((K, cells_y), 1) * K + iota((K, cells_y), 0), fac, 2)
    m_row = iota((rows_c, cells_y), 0)
    m_ids = (m_row >> 4) * rows_m + (m_row & (PAD - 1))
    phy_tab = unit_value(m_ids * cells_y + iota((rows_c, cells_y), 1), cor, 6)
    turned = jnp.concatenate([ay_turned, phy_tab], axis=0)
    phq_tab = [unit_f32(r_rows * E + e, cor, 8) for e in range(E)]
    aq_turned = unit_f32(run_ids(iota((1, K), 1)) * K + iota((K, K), 0), fac, 4)

    pair_y.wait_recv()
    y_out[...] = wide + y_got[...]
    y_copies = [None] * chips
    for i in far_first:
        dest = target(*offsets[i])
        copy = pltpu.make_async_remote_copy(
            src_ref=y_out.at[dest["gx"] * zsplit + dest["gz"]],
            dst_ref=y_in.at[i - 1],
            send_sem=y_ssem.at[i - 1],
            recv_sem=y_rsem.at[i - 1],
            device_id=dest,
            device_id_type=MESH,
        )
        copy.start()
        y_copies[i] = copy

    deep = jnp.zeros((K, cells_z), jnp.float32)
    halves = [jnp.zeros((rows_c, cells_z), jnp.float32) for e in range(E)]
    for first in range(0, total_q, 2):
        group = range(first, min(first + 2, total_q))
        planes = [flow[q].reshape(cells_y, cells_z) for q in group]
        both = dot_f32(turned, jnp.concatenate(planes, axis=1))
        for i, q in enumerate(group):
            lanes = both[:, i * cells_z : (i + 1) * cells_z]
            deep = deep + lanes[:K] * aq_turned[:, q : q + 1]
            for e in range(E):
                halves[e] = halves[e] + lanes[K:] * phq_tab[e][q : q + 1]
    lane = iota((cells_z, K), 1)
    phz_tab = unit_f32((lane & 63) * total_z + z_base + iota((cells_z, K), 0), cor, 7)
    core = None
    for e in range(E):
        right = jnp.where((lane >> 6) == e, phz_tab, 0.0).astype(low)
        part = dot_split(halves[e], right)
        core = part if core is None else core + part
    x_row = jnp.sum(deep.T * az_tab.astype(jnp.float32), axis=0, keepdims=True)
    core = jnp.where((iota((rows_c, K), 0) & (PAD - 1)) == rows_m, x_row, core)
    for g in range(slabs):
        c_send[g] = core[g * PAD : g * PAD + rows_m + 1]
    pair_c = pair_copy(c_send, c_got, 1)
    pair_c.start()
    ax_turned = unit_f32(gx * K + iota((K, K), 0), fac, 1)
    deep = deep * ax_turned
    for g in range(slabs):
        for v in range(2):
            at = (2 * g + v) * rows_z
            z_send[v, g] = deep[at : at + rows_z]
    pair_z = pair_copy(z_send.at[other], z_got, 0)
    pair_z.start()

    select_at = iota((1, 640), 1)
    lane_m = select_at // S
    lane_n = select_at - lane_m * S
    spread = jnp.where((iota((K, 640), 0) & 63) == lane_n, 1.0, 0.0).astype(low)
    keep = (iota((rows_c, 640), 0) & (PAD - 1)) == lane_m
    slot = iota((S, K), 1) >> 4
    x_ids = (gx - slot + 2 * slabs) & (slabs - 1)
    phx = unit_value(iota((S, K), 0) * slabs + x_ids, cor, 5)

    c_copies = [None] * chips
    pair_c.wait_recv()
    c_out[...] = c_send[...] + c_got[...]
    for i in far_first:
        dest = target(*offsets[i])
        copy = pltpu.make_async_remote_copy(
            src_ref=c_out.at[dest["gx"]],
            dst_ref=c_in.at[i - 1],
            send_sem=c_ssem.at[i - 1],
            recv_sem=c_rsem.at[i - 1],
            device_id=dest,
            device_id_type=MESH,
        )
        copy.start()
        c_copies[i] = copy
    z_copies = []
    pair_z.wait_recv()
    z_out[...] = z_send[vert] + z_got[...]
    for dx in range(1, slabs):
        to = lax.rem(gx + dx, slabs)
        copy = pltpu.make_async_remote_copy(
            src_ref=z_out.at[to],
            dst_ref=z_in.at[dx - 1],
            send_sem=z_ssem.at[dx - 1],
            recv_sem=z_rsem.at[dx - 1],
            device_id={"gx": to},
            device_id_type=MESH,
        )
        copy.start()
        z_copies.append(copy)

    total = y_out[gx * zsplit + gz]
    for i in range(1, chips):
        y_copies[i].wait_recv()
        total = total + y_in[i - 1]
    out_y[...] = total * scale_y
    slots = []
    for dx in range(slabs):
        total = c_out[gx] if dx == 0 else None
        for dz in range(zsplit):
            i = dx * zsplit + dz
            if i == 0:
                continue
            c_copies[i].wait_recv()
            total = c_in[i - 1] if total is None else total + c_in[i - 1]
        if dx == 0:
            out_x[...] = total[rows_m : rows_m + 1] * scale_x
        slots.append(jnp.concatenate([total, jnp.zeros((PAD - rows_m - 1, K), jnp.float32)], axis=0))
    core = jnp.concatenate(slots, axis=0) * scale_core
    upper = core.astype(low)
    lower = (core - upper.astype(jnp.float32)).astype(low)
    core_lane = iota((rows_c, K), 1) >> 6
    zero = jnp.zeros((rows_c, K), low)
    left = jnp.concatenate(
        [jnp.where(core_lane == e, part, zero) for e in range(E) for part in (upper, lower)],
        axis=0,
    )
    placed = dot_f32(left, spread)
    for e in range(E):
        at = 2 * e * rows_c
        right = jnp.concatenate(
            [
                jnp.where(keep, placed[at + s * rows_c : at + (s + 1) * rows_c], 0.0)
                for s in range(2)
            ],
            axis=0,
        ).astype(low)
        out_core[e] = dot_f32(phx, right)[:, : rows_m * S]

    total = z_out[gx]
    for i, copy in enumerate(z_copies):
        copy.wait_recv()
        total = total + z_in[i]
    out_z[...] = total * scale_z
    started = [pair_z, pair_c, pair_y] + z_copies + c_copies[1:] + y_copies[1:]
    for copy in started:
        copy.wait_send()


def finish_kernel(*refs):
    count = len(refs) // 2
    for i in range(count):
        refs[count + i][...] = refs[i][...]


def shards_fused(sizes, flow_field, test_streams, snapshot_ids):
    slabs, zsplit, batches, local_snaps, variables, cells_y, cells_z = sizes
    pairs = batches * local_snaps
    chips = slabs * zsplit
    rows_y = cells_y // (2 * chips)
    rows_z = K // (2 * slabs)
    rows_m = S // slabs
    total_q = pairs * variables
    f32 = jnp.float32
    anywhere = pl.BlockSpec(memory_space=pl.ANY)
    vmem = pl.BlockSpec(memory_space=pltpu.VMEM)
    dma = pltpu.SemaphoreType.DMA
    total_z = cells_z * zsplit
    all_q = 2 * total_q
    scales = (
        3.0**1.5 / math.sqrt(cells_y * total_z * all_q),
        3.0**1.5 / math.sqrt(slabs * total_z * all_q),
        3.0**1.5 / math.sqrt(slabs * cells_y * all_q),
        9.0 / math.sqrt(slabs * cells_y * total_z * all_q),
    )
    outs = [
        jax.ShapeDtypeStruct((1, K), f32),
        jax.ShapeDtypeStruct((rows_y, K), f32),
        jax.ShapeDtypeStruct((rows_z, cells_z), f32),
        jax.ShapeDtypeStruct((E, S, rows_m * S), f32),
    ]
    parts = pl.pallas_call(
        functools.partial(sketch_kernel, sizes, scales),
        name="sketch",
        out_shape=outs,
        in_specs=[anywhere] * 3,
        out_specs=[vmem] * 4,
        scratch_shapes=[
            pltpu.SMEM(test_streams.shape, jnp.int32),
            pltpu.SMEM(snapshot_ids.shape, jnp.int32),
            pltpu.VMEM((total_q, chips, 2, rows_y, cells_z), jnp.bfloat16),
            pltpu.VMEM((chips, rows_y, K), f32),
            pltpu.VMEM((chips, rows_y, K), f32),
            pltpu.VMEM((chips, rows_y, K), f32),
            pltpu.VMEM((chips - 1, rows_y, K), f32),
            pltpu.VMEM((2, slabs, rows_z, cells_z), f32),
            pltpu.VMEM((slabs, rows_z, cells_z), f32),
            pltpu.VMEM((slabs, rows_z, cells_z), f32),
            pltpu.VMEM((slabs - 1, rows_z, cells_z), f32),
            pltpu.VMEM((slabs, rows_m + 1, K), f32),
            pltpu.VMEM((slabs, rows_m + 1, K), f32),
            pltpu.VMEM((slabs, rows_m + 1, K), f32),
            pltpu.VMEM((chips - 1, rows_m + 1, K), f32),
            dma((2,)),
            dma((pairs,)),
            dma((3,)),
            dma((3,)),
            dma((chips - 1,)),
            dma((chips - 1,)),
            dma((chips - 1,)),
            dma((chips - 1,)),
            dma((slabs - 1,)),
            dma((slabs - 1,)),
        ],
        compiler_params=pltpu.CompilerParams(
            collective_id=0, has_side_effects=True, vmem_limit_bytes=63 * 2**20
        ),
    )(test_streams, snapshot_ids, flow_field.reshape(total_q, chips, 2, rows_y, cells_z))
    out_x, out_y, out_z, out_core = pl.pallas_call(
        finish_kernel,
        name="finish",
        out_shape=outs,
        in_specs=[vmem] * 4,
        out_specs=[vmem] * 4,
        compiler_params=pltpu.CompilerParams(vmem_limit_bytes=63 * 2**20),
    )(*parts)
    return (out_x, out_y, out_z.T, jnp.transpose(out_core, (2, 0, 1)))


def shards(flow_field, test_streams, snapshot_ids):
    batches, local_snaps, variables, cells_x, cells_y, cells_z = flow_field.shape
    slabs = lax.axis_size("gx")
    zsplit = lax.axis_size("gz")
    fits = (
        lax.axis_size("vert") == 2
        and cells_x == 1
        and cells_z == K
        and cells_y % (16 * slabs * zsplit) == 0
        and slabs == 4
        and zsplit > 1
        and cells_y % (32 * slabs * zsplit) == 0
        and batches * local_snaps * variables <= K
    )
    if not fits:
        return shards_general(flow_field, test_streams, snapshot_ids)
    sizes = (slabs, zsplit, batches, local_snaps, variables, cells_y, cells_z)
    return shards_fused(sizes, flow_field, test_streams, snapshot_ids)


def solution(mesh):
    in_specs = (P("groups", "vert", None, "gx", None, "gz"), P("groups"), P("groups", "vert"))
    out_specs = (
        P(("groups", "gx"), None),
        P(("groups", "gx", "gz", "vert"), None),
        P(("groups", "gz"), ("gx", "vert")),
        P(("groups", "gx"), None, None),
    )
    return jax.shard_map(shards, mesh=mesh, in_specs=in_specs, out_specs=out_specs, check_vma=False)
```

```python
import functools
import math

import jax
import jax.numpy as jnp
from jax import lax
from jax.experimental import pallas as pl
from jax.experimental.pallas import tpu as pltpu
from jax.sharding import PartitionSpec as P

K = 128
S = 48
E = 2


def hash_index(index, stream, salt):
    mixed = index * -1640531535 + stream * -2048144777 + salt
    mixed = jnp.bitwise_xor(mixed, lax.shift_right_logical(mixed, jnp.int32(16)))
    mixed = mixed * 739982445
    mixed = jnp.bitwise_xor(mixed, lax.shift_right_logical(mixed, jnp.int32(13)))
    mixed = mixed * 695872825
    return jnp.bitwise_xor(mixed, lax.shift_right_logical(mixed, jnp.int32(16)))


def unit_value(index, stream, salt):
    upper = lax.shift_right_logical(hash_index(index, stream, salt), jnp.int32(9))
    return ((2 * upper + 1).astype(jnp.float32) * 2.0 ** (-24) - 1.0).astype(jnp.bfloat16)


def test_table(row_ids, col_ids, stride, stream, salt):
    return unit_value(row_ids[:, None] * stride + col_ids[None, :], stream, salt)


def shards_general(flow_field, test_streams, snapshot_ids):
    highest = lax.Precision.HIGHEST
    batches, local_snaps, variables, cells_x, cells_y, cells_z = flow_field.shape
    slabs_x = lax.axis_size("gx")
    total_x = cells_x * slabs_x
    total_z = cells_z * lax.axis_size("gz")
    total_q = variables * batches * local_snaps * lax.axis_size("vert")
    factor_stream = test_streams[0]
    core_stream = test_streams[1]
    rank_ids = jnp.arange(K, dtype=jnp.int32)
    sketch_ids = jnp.arange(S, dtype=jnp.int32)
    x_ids = lax.axis_index("gx") * cells_x + jnp.arange(cells_x, dtype=jnp.int32)
    y_ids = jnp.arange(cells_y, dtype=jnp.int32)
    z_ids = lax.axis_index("gz") * cells_z + jnp.arange(cells_z, dtype=jnp.int32)
    ax_tab = test_table(x_ids, rank_ids, K, factor_stream, 1).astype(jnp.float32)
    ay_low = test_table(y_ids, rank_ids, K, factor_stream, 2)
    az_low = test_table(z_ids, rank_ids, K, factor_stream, 3)
    ay_tab = ay_low.astype(jnp.float32)
    phy_low = test_table(sketch_ids, y_ids, cells_y, core_stream, 6)
    phz_low = test_table(sketch_ids, z_ids, total_z, core_stream, 7)

    def batch_terms(batch_idx):
        blocks = flow_field[batch_idx].reshape(-1, cells_x, cells_y, cells_z)
        pairs = blocks.shape[0]
        q_ids = (
            snapshot_ids[batch_idx][:, None] * variables
            + jnp.arange(variables, dtype=jnp.int32)[None, :]
        ).reshape(-1)
        aq_tab = test_table(q_ids, rank_ids, K, factor_stream, 4).astype(jnp.float32)
        phq_low = test_table(q_ids, jnp.arange(E, dtype=jnp.int32), E, core_stream, 8)
        rows_z = blocks.reshape(-1, cells_z)
        along_z = jnp.dot(rows_z, az_low, preferred_element_type=jnp.float32).reshape(
            pairs, cells_x, cells_y, K
        )
        along_y = jnp.einsum("qxyz,yk->qxzk", blocks, ay_low, preferred_element_type=jnp.float32)
        weights = aq_tab[:, None, :] * ax_tab[None, :, :]
        part_x = jnp.sum(
            jnp.sum(along_z * ay_tab[None, None, :, :], axis=2) * aq_tab[:, None, :], axis=0
        )
        part_y = jnp.sum(along_z * weights[:, :, None, :], axis=(0, 1))
        part_z = jnp.sum(along_y * weights[:, :, None, :], axis=(0, 1))
        first = jnp.dot(rows_z, phz_low.T, preferred_element_type=jnp.float32).reshape(
            pairs, cells_x, cells_y, S
        )
        second = jnp.einsum("qxyc,by->qxbc", first, phy_low.astype(jnp.float32), precision=highest)
        partial_core = jnp.einsum(
            "qxbc,qe->bcex", second, phq_low.astype(jnp.float32), precision=highest
        )
        return (part_x, part_y, part_z, partial_core.reshape(S * S, E, cells_x))

    def finish(part_x, part_y, part_z, partial_core):
        summed, sum_x = lax.psum((partial_core, part_x), ("gz", "vert"))
        phx_whole = test_table(
            sketch_ids, jnp.arange(total_x, dtype=jnp.int32), total_x, core_stream, 5
        ).astype(jnp.float32)
        core = jnp.einsum(
            "rex,ax->rea",
            lax.all_to_all(summed, "gx", split_axis=0, concat_axis=2, tiled=True),
            phx_whole,
            precision=highest,
        )
        sum_z = lax.psum_scatter(part_z, ("gx", "vert"), scatter_dimension=1, tiled=True)
        sum_y = lax.psum_scatter(part_y, ("gx", "gz", "vert"), scatter_dimension=0, tiled=True)
        return (sum_x, sum_y, sum_z, core)

    terms = [batch_terms(batch_idx) for batch_idx in range(batches)]
    totals = finish(terms[0][0], terms[0][1], terms[0][2], terms[0][3])
    for later in terms[1:]:
        latest = finish(later[0], later[1], later[2], later[3])
        totals = tuple((earlier + newer for earlier, newer in zip(totals, latest)))
    scale_x = 3.0**1.5 / math.sqrt(cells_y * total_z * total_q)
    scale_y = 3.0**1.5 / math.sqrt(total_x * total_z * total_q)
    scale_z = 3.0**1.5 / math.sqrt(total_x * cells_y * total_q)
    scale_core = 9.0 / math.sqrt(total_x * cells_y * total_z * total_q)
    return (totals[0] * scale_x, totals[1] * scale_y, totals[2] * scale_z, totals[3] * scale_core)


MESH = pl.DeviceIdType.MESH
PAD = 16


def iota(shape, dim):
    return lax.broadcasted_iota(jnp.int32, shape, dim)


def unit_f32(index, stream, salt):
    return unit_value(index, stream, salt).astype(jnp.float32)


def dot_f32(left, right):
    return jnp.dot(left, right, preferred_element_type=jnp.float32)


def dot_split(left, right):
    upper = left.astype(jnp.bfloat16)
    lower = (left - upper.astype(jnp.float32)).astype(jnp.bfloat16)
    return dot_f32(upper, right) + dot_f32(lower, right)


def sketch_kernel(
    sizes,
    scales,
    streams_hbm,
    snaps_hbm,
    flow_hbm,
    out_x,
    out_y,
    out_z,
    out_core_hbm,
    streams,
    snaps,
    flow,
    y_send,
    y_got,
    y_out,
    y_in,
    z_send,
    z_got,
    z_out,
    z_in,
    c_send,
    c_got,
    c_out,
    c_in,
    out_core,
    small_sem,
    load_sem,
    pair_send,
    pair_recv,
    y_ssem,
    y_rsem,
    c_ssem,
    c_rsem,
    z_ssem,
    z_rsem,
):
    slabs, zsplit, batches, local_snaps, variables, cells_y, cells_z = sizes
    scale_x, scale_y, scale_z, scale_core = scales
    pairs = batches * local_snaps
    total_q = pairs * variables
    chips = slabs * zsplit
    rows_y = cells_y // (2 * chips)
    rows_z = K // (2 * slabs)
    rows_m = S // slabs
    rows_c = slabs * PAD
    total_z = cells_z * zsplit
    gx = lax.axis_index("gx")
    gz = lax.axis_index("gz")
    vert = lax.axis_index("vert")
    other = 1 - vert
    offsets = [(dx, dz) for dx in range(slabs) for dz in range(zsplit)]
    far_first = sorted(range(1, chips), key=lambda i: -min(offsets[i][0], slabs - offsets[i][0]))

    def target(dx, dz):
        return {"gx": lax.rem(gx + dx, slabs), "gz": lax.rem(gz + dz, zsplit)}

    smalls = [
        pltpu.make_async_copy(streams_hbm, streams, small_sem.at[0]),
        pltpu.make_async_copy(snaps_hbm, snaps, small_sem.at[1]),
    ]
    loads = [
        pltpu.make_async_copy(
            flow_hbm.at[pl.ds(p * variables, variables)],
            flow.at[pl.ds(p * variables, variables)],
            load_sem.at[p],
        )
        for p in range(pairs)
    ]
    for load in smalls + loads:
        load.start()
    barrier = pltpu.get_barrier_semaphore()
    pl.semaphore_signal(barrier, inc=1, device_id={"vert": other}, device_id_type=MESH)
    for dx, dz in offsets[1:]:
        pl.semaphore_signal(barrier, inc=1, device_id=target(dx, dz), device_id_type=MESH)

    low = jnp.bfloat16
    for load in smalls:
        load.wait()
    fac = streams[0]
    cor = streams[1]

    def run_ids(q_index):
        ids = jnp.zeros(q_index.shape, jnp.int32)
        for q in range(total_q):
            p = q // variables
            run = snaps[p // local_snaps, p % local_snaps] * variables + q % variables
            ids = jnp.where(q_index == q, run, ids)
        return ids

    def pair_copy(src, dst, which):
        return pltpu.make_async_remote_copy(
            src_ref=src,
            dst_ref=dst,
            send_sem=pair_send.at[which],
            recv_sem=pair_recv.at[which],
            device_id={"vert": other},
            device_id_type=MESH,
        )

    z_base = gz * cells_z
    az_tab = unit_value(
        (z_base + iota((cells_z, K), 0)) * K + iota((cells_z, K), 1), fac, 3
    )
    q_rows = -(-total_q // 8) * 8
    r_rows = run_ids(iota((q_rows, K), 0))
    aq_tab = unit_f32(r_rows * K + iota((q_rows, K), 1), fac, 4)
    ax_row = unit_f32(gx * K + iota((8, K), 1), fac, 1)[0:1]
    x_rows = []
    for h, side in enumerate((other, vert)):
        wide = jnp.zeros((chips * rows_y, K), jnp.float32)
        for q in range(total_q):
            if h == 0 and q % variables == 0:
                loads[q // variables].wait()
            rows = flow[q, :, side].reshape(chips * rows_y, cells_z)
            wide = wide + dot_f32(rows, az_tab) * aq_tab[q : q + 1]
        side_row = iota((chips * rows_y, K), 0)
        y_index = (2 * (side_row // rows_y) + side) * rows_y + lax.rem(side_row, rows_y)
        ay_tab = unit_f32(y_index * K + iota((chips * rows_y, K), 1), fac, 2)
        x_rows.append(jnp.sum(wide * ay_tab, axis=0, keepdims=True))
        wide = (wide * ax_row).reshape(chips, rows_y, K)
        if h == 0:
            y_send[...] = wide
            pl.semaphore_wait(barrier, chips)
            pair_y = pair_copy(y_send, y_got, 2)
            pair_y.start()

    m_row = iota((rows_c, cells_y), 0)
    m_ids = (m_row >> 4) * rows_m + (m_row & (PAD - 1))
    phy_tab = unit_value(m_ids * cells_y + iota((rows_c, cells_y), 1), cor, 6)
    phq_tab = [unit_f32(r_rows * E + e, cor, 8) for e in range(E)]

    pair_y.wait_recv()
    y_out[...] = wide + y_got[...]
    y_copies = [None] * chips
    for i in far_first:
        dest = target(*offsets[i])
        copy = pltpu.make_async_remote_copy(
            src_ref=y_out.at[dest["gx"] * zsplit + dest["gz"]],
            dst_ref=y_in.at[i - 1],
            send_sem=y_ssem.at[i - 1],
            recv_sem=y_rsem.at[i - 1],
            device_id=dest,
            device_id_type=MESH,
        )
        copy.start()
        y_copies[i] = copy

    def planes_of(first):
        group = [flow[q].reshape(cells_y, cells_z) for q in (first, first + 1)]
        return jnp.concatenate(group, axis=1)

    halves = [jnp.zeros((rows_c, cells_z), jnp.float32) for e in range(E)]
    for first in range(0, total_q, 2):
        both = dot_f32(phy_tab, planes_of(first))
        for i in range(2):
            lanes = both[:, i * cells_z : (i + 1) * cells_z]
            q = first + i
            for e in range(E):
                halves[e] = halves[e] + lanes * phq_tab[e][q : q + 1]
    lane = iota((cells_z, K), 1)
    phz_tab = unit_f32((lane & 63) * total_z + z_base + iota((cells_z, K), 0), cor, 7)
    core = None
    for e in range(E):
        right = jnp.where((lane >> 6) == e, phz_tab, 0.0).astype(low)
        part = dot_split(halves[e], right)
        core = part if core is None else core + part
    x_row = x_rows[0] + x_rows[1]
    core = jnp.where((iota((rows_c, K), 0) & (PAD - 1)) == rows_m, x_row, core)
    for g in range(slabs):
        c_send[g] = core[g * PAD : g * PAD + rows_m + 1]
    pair_c = pair_copy(c_send, c_got, 1)
    pair_c.start()

    ay_turned = unit_value(iota((K, cells_y), 1) * K + iota((K, cells_y), 0), fac, 2)
    aq_turned = unit_f32(run_ids(iota((1, K), 1)) * K + iota((K, K), 0), fac, 4)
    deep = jnp.zeros((K, cells_z), jnp.float32)
    for first in range(0, total_q, 2):
        both = dot_f32(ay_turned, planes_of(first))
        for i in range(2):
            q = first + i
            deep = deep + both[:, i * cells_z : (i + 1) * cells_z] * aq_turned[:, q : q + 1]
        if first == total_q // 4 * 2:
            c_copies = [None] * chips
            pair_c.wait_recv()
            c_out[...] = c_send[...] + c_got[...]
            for i in far_first:
                dest = target(*offsets[i])
                copy = pltpu.make_async_remote_copy(
                    src_ref=c_out.at[dest["gx"]],
                    dst_ref=c_in.at[i - 1],
                    send_sem=c_ssem.at[i - 1],
                    recv_sem=c_rsem.at[i - 1],
                    device_id=dest,
                    device_id_type=MESH,
                )
                copy.start()
                c_copies[i] = copy
    ax_turned = unit_f32(gx * K + iota((K, K), 0), fac, 1)
    deep = deep * ax_turned
    for g in range(slabs):
        for v in range(2):
            at = (2 * g + v) * rows_z
            z_send[v, g] = deep[at : at + rows_z]
    pair_z = pair_copy(z_send.at[other], z_got, 0)
    pair_z.start()

    select_at = iota((1, 640), 1)
    lane_m = select_at // S
    lane_n = select_at - lane_m * S
    spread = jnp.where((iota((K, 640), 0) & 63) == lane_n, 1.0, 0.0).astype(low)
    keep = (iota((rows_c, 640), 0) & (PAD - 1)) == lane_m
    slot = iota((S, K), 1) >> 4
    x_ids = (gx - slot + 2 * slabs) & (slabs - 1)
    phx = unit_value(iota((S, K), 0) * slabs + x_ids, cor, 5)

    total = y_out[gx * zsplit + gz]
    for i in range(1, chips):
        y_copies[i].wait_recv()
        total = total + y_in[i - 1]
    out_y[...] = total * scale_y
    z_copies = []
    pair_z.wait_recv()
    z_out[...] = z_send[vert] + z_got[...]
    for dx in range(1, slabs):
        to = lax.rem(gx + dx, slabs)
        copy = pltpu.make_async_remote_copy(
            src_ref=z_out.at[to],
            dst_ref=z_in.at[dx - 1],
            send_sem=z_ssem.at[dx - 1],
            recv_sem=z_rsem.at[dx - 1],
            device_id={"gx": to},
            device_id_type=MESH,
        )
        copy.start()
        z_copies.append(copy)

    slots = []
    for dx in range(slabs):
        total = c_out[gx] if dx == 0 else None
        for dz in range(zsplit):
            i = dx * zsplit + dz
            if i == 0:
                continue
            c_copies[i].wait_recv()
            total = c_in[i - 1] if total is None else total + c_in[i - 1]
        if dx == 0:
            out_x[...] = total[rows_m : rows_m + 1] * scale_x
        slots.append(jnp.concatenate([total, jnp.zeros((PAD - rows_m - 1, K), jnp.float32)], axis=0))
    core = jnp.concatenate(slots, axis=0) * scale_core
    upper = core.astype(low)
    lower = (core - upper.astype(jnp.float32)).astype(low)
    core_lane = iota((rows_c, K), 1) >> 6
    zero = jnp.zeros((rows_c, K), low)
    left = jnp.concatenate(
        [jnp.where(core_lane == e, part, zero) for e in range(E) for part in (upper, lower)],
        axis=0,
    )
    placed = dot_f32(left, spread)
    for e in range(E):
        at = 2 * e * rows_c
        right = jnp.concatenate(
            [
                jnp.where(keep, placed[at + s * rows_c : at + (s + 1) * rows_c], 0.0)
                for s in range(2)
            ],
            axis=0,
        ).astype(low)
        out_core[e] = dot_f32(phx, right)[:, : rows_m * S]

    store_core = pltpu.make_async_copy(out_core, out_core_hbm, small_sem.at[2])
    store_core.start()
    total = z_out[gx]
    for i, copy in enumerate(z_copies):
        copy.wait_recv()
        total = total + z_in[i]
    out_z[...] = total * scale_z
    started = [pair_z, pair_c, pair_y] + z_copies + c_copies[1:] + y_copies[1:]
    for copy in started:
        copy.wait_send()
    store_core.wait()


def finish_kernel(*refs):
    count = len(refs) // 2
    for i in range(count):
        refs[count + i][...] = refs[i][...]


def shards_fused(sizes, flow_field, test_streams, snapshot_ids):
    slabs, zsplit, batches, local_snaps, variables, cells_y, cells_z = sizes
    pairs = batches * local_snaps
    chips = slabs * zsplit
    rows_y = cells_y // (2 * chips)
    rows_z = K // (2 * slabs)
    rows_m = S // slabs
    total_q = pairs * variables
    f32 = jnp.float32
    anywhere = pl.BlockSpec(memory_space=pl.ANY)
    vmem = pl.BlockSpec(memory_space=pltpu.VMEM)
    dma = pltpu.SemaphoreType.DMA
    total_z = cells_z * zsplit
    all_q = 2 * total_q
    scales = (
        3.0**1.5 / math.sqrt(cells_y * total_z * all_q),
        3.0**1.5 / math.sqrt(slabs * total_z * all_q),
        3.0**1.5 / math.sqrt(slabs * cells_y * all_q),
        9.0 / math.sqrt(slabs * cells_y * total_z * all_q),
    )
    outs = [
        jax.ShapeDtypeStruct((1, K), f32),
        jax.ShapeDtypeStruct((rows_y, K), f32),
        jax.ShapeDtypeStruct((rows_z, cells_z), f32),
        jax.ShapeDtypeStruct((E, S, rows_m * S), f32),
    ]
    parts = pl.pallas_call(
        functools.partial(sketch_kernel, sizes, scales),
        name="sketch",
        out_shape=outs,
        in_specs=[anywhere] * 3,
        out_specs=[vmem] * 3 + [anywhere],
        scratch_shapes=[
            pltpu.SMEM(test_streams.shape, jnp.int32),
            pltpu.SMEM(snapshot_ids.shape, jnp.int32),
            pltpu.VMEM((total_q, chips, 2, rows_y, cells_z), jnp.bfloat16),
            pltpu.VMEM((chips, rows_y, K), f32),
            pltpu.VMEM((chips, rows_y, K), f32),
            pltpu.VMEM((chips, rows_y, K), f32),
            pltpu.VMEM((chips - 1, rows_y, K), f32),
            pltpu.VMEM((2, slabs, rows_z, cells_z), f32),
            pltpu.VMEM((slabs, rows_z, cells_z), f32),
            pltpu.VMEM((slabs, rows_z, cells_z), f32),
            pltpu.VMEM((slabs - 1, rows_z, cells_z), f32),
            pltpu.VMEM((slabs, rows_m + 1, K), f32),
            pltpu.VMEM((slabs, rows_m + 1, K), f32),
            pltpu.VMEM((slabs, rows_m + 1, K), f32),
            pltpu.VMEM((chips - 1, rows_m + 1, K), f32),
            pltpu.VMEM((E, S, rows_m * S), f32),
            dma((3,)),
            dma((pairs,)),
            dma((3,)),
            dma((3,)),
            dma((chips - 1,)),
            dma((chips - 1,)),
            dma((chips - 1,)),
            dma((chips - 1,)),
            dma((slabs - 1,)),
            dma((slabs - 1,)),
        ],
        compiler_params=pltpu.CompilerParams(
            collective_id=0, has_side_effects=True, vmem_limit_bytes=63 * 2**20
        ),
    )(test_streams, snapshot_ids, flow_field.reshape(total_q, chips, 2, rows_y, cells_z))
    out_x, out_y, out_z, out_core = pl.pallas_call(
        finish_kernel,
        name="finish",
        out_shape=outs,
        in_specs=[vmem] * 4,
        out_specs=[vmem] * 4,
        compiler_params=pltpu.CompilerParams(vmem_limit_bytes=63 * 2**20),
    )(*parts)
    return (out_x, out_y, out_z.T, jnp.transpose(out_core, (2, 0, 1)))


def shards(flow_field, test_streams, snapshot_ids):
    batches, local_snaps, variables, cells_x, cells_y, cells_z = flow_field.shape
    slabs = lax.axis_size("gx")
    zsplit = lax.axis_size("gz")
    fits = (
        lax.axis_size("vert") == 2
        and cells_x == 1
        and cells_z == K
        and cells_y % (16 * slabs * zsplit) == 0
        and slabs == 4
        and zsplit > 1
        and cells_y % (32 * slabs * zsplit) == 0
        and batches * local_snaps * variables % 2 == 0
        and batches * local_snaps * variables <= K
    )
    if not fits:
        return shards_general(flow_field, test_streams, snapshot_ids)
    sizes = (slabs, zsplit, batches, local_snaps, variables, cells_y, cells_z)
    return shards_fused(sizes, flow_field, test_streams, snapshot_ids)


def solution(mesh):
    in_specs = (P("groups", "vert", None, "gx", None, "gz"), P("groups"), P("groups", "vert"))
    out_specs = (
        P(("groups", "gx"), None),
        P(("groups", "gx", "gz", "vert"), None),
        P(("groups", "gz"), ("gx", "vert")),
        P(("groups", "gx"), None, None),
    )
    return jax.shard_map(shards, mesh=mesh, in_specs=in_specs, out_specs=out_specs, check_vma=False)
```

```python
import functools
import math

import jax
import jax.numpy as jnp
from jax import lax
from jax.experimental import pallas as pl
from jax.experimental.pallas import tpu as pltpu
from jax.sharding import PartitionSpec as P

K = 128
S = 48
E = 2


def hash_index(index, stream, salt):
    mixed = index * -1640531535 + stream * -2048144777 + salt
    mixed = jnp.bitwise_xor(mixed, lax.shift_right_logical(mixed, jnp.int32(16)))
    mixed = mixed * 739982445
    mixed = jnp.bitwise_xor(mixed, lax.shift_right_logical(mixed, jnp.int32(13)))
    mixed = mixed * 695872825
    return jnp.bitwise_xor(mixed, lax.shift_right_logical(mixed, jnp.int32(16)))


def unit_value(index, stream, salt):
    upper = lax.shift_right_logical(hash_index(index, stream, salt), jnp.int32(9))
    return ((2 * upper + 1).astype(jnp.float32) * 2.0 ** (-24) - 1.0).astype(jnp.bfloat16)


def test_table(row_ids, col_ids, stride, stream, salt):
    return unit_value(row_ids[:, None] * stride + col_ids[None, :], stream, salt)


def shards_general(flow_field, test_streams, snapshot_ids):
    highest = lax.Precision.HIGHEST
    batches, local_snaps, variables, cells_x, cells_y, cells_z = flow_field.shape
    slabs_x = lax.axis_size("gx")
    total_x = cells_x * slabs_x
    total_z = cells_z * lax.axis_size("gz")
    total_q = variables * batches * local_snaps * lax.axis_size("vert")
    factor_stream = test_streams[0]
    core_stream = test_streams[1]
    rank_ids = jnp.arange(K, dtype=jnp.int32)
    sketch_ids = jnp.arange(S, dtype=jnp.int32)
    x_ids = lax.axis_index("gx") * cells_x + jnp.arange(cells_x, dtype=jnp.int32)
    y_ids = jnp.arange(cells_y, dtype=jnp.int32)
    z_ids = lax.axis_index("gz") * cells_z + jnp.arange(cells_z, dtype=jnp.int32)
    ax_tab = test_table(x_ids, rank_ids, K, factor_stream, 1).astype(jnp.float32)
    ay_low = test_table(y_ids, rank_ids, K, factor_stream, 2)
    az_low = test_table(z_ids, rank_ids, K, factor_stream, 3)
    ay_tab = ay_low.astype(jnp.float32)
    phy_low = test_table(sketch_ids, y_ids, cells_y, core_stream, 6)
    phz_low = test_table(sketch_ids, z_ids, total_z, core_stream, 7)

    def batch_terms(batch_idx):
        blocks = flow_field[batch_idx].reshape(-1, cells_x, cells_y, cells_z)
        pairs = blocks.shape[0]
        q_ids = (
            snapshot_ids[batch_idx][:, None] * variables
            + jnp.arange(variables, dtype=jnp.int32)[None, :]
        ).reshape(-1)
        aq_tab = test_table(q_ids, rank_ids, K, factor_stream, 4).astype(jnp.float32)
        phq_low = test_table(q_ids, jnp.arange(E, dtype=jnp.int32), E, core_stream, 8)
        rows_z = blocks.reshape(-1, cells_z)
        along_z = jnp.dot(rows_z, az_low, preferred_element_type=jnp.float32).reshape(
            pairs, cells_x, cells_y, K
        )
        along_y = jnp.einsum("qxyz,yk->qxzk", blocks, ay_low, preferred_element_type=jnp.float32)
        weights = aq_tab[:, None, :] * ax_tab[None, :, :]
        part_x = jnp.sum(
            jnp.sum(along_z * ay_tab[None, None, :, :], axis=2) * aq_tab[:, None, :], axis=0
        )
        part_y = jnp.sum(along_z * weights[:, :, None, :], axis=(0, 1))
        part_z = jnp.sum(along_y * weights[:, :, None, :], axis=(0, 1))
        first = jnp.dot(rows_z, phz_low.T, preferred_element_type=jnp.float32).reshape(
            pairs, cells_x, cells_y, S
        )
        second = jnp.einsum("qxyc,by->qxbc", first, phy_low.astype(jnp.float32), precision=highest)
        partial_core = jnp.einsum(
            "qxbc,qe->bcex", second, phq_low.astype(jnp.float32), precision=highest
        )
        return (part_x, part_y, part_z, partial_core.reshape(S * S, E, cells_x))

    def finish(part_x, part_y, part_z, partial_core):
        summed, sum_x = lax.psum((partial_core, part_x), ("gz", "vert"))
        phx_whole = test_table(
            sketch_ids, jnp.arange(total_x, dtype=jnp.int32), total_x, core_stream, 5
        ).astype(jnp.float32)
        core = jnp.einsum(
            "rex,ax->rea",
            lax.all_to_all(summed, "gx", split_axis=0, concat_axis=2, tiled=True),
            phx_whole,
            precision=highest,
        )
        sum_z = lax.psum_scatter(part_z, ("gx", "vert"), scatter_dimension=1, tiled=True)
        sum_y = lax.psum_scatter(part_y, ("gx", "gz", "vert"), scatter_dimension=0, tiled=True)
        return (sum_x, sum_y, sum_z, core)

    terms = [batch_terms(batch_idx) for batch_idx in range(batches)]
    totals = finish(terms[0][0], terms[0][1], terms[0][2], terms[0][3])
    for later in terms[1:]:
        latest = finish(later[0], later[1], later[2], later[3])
        totals = tuple((earlier + newer for earlier, newer in zip(totals, latest)))
    scale_x = 3.0**1.5 / math.sqrt(cells_y * total_z * total_q)
    scale_y = 3.0**1.5 / math.sqrt(total_x * total_z * total_q)
    scale_z = 3.0**1.5 / math.sqrt(total_x * cells_y * total_q)
    scale_core = 9.0 / math.sqrt(total_x * cells_y * total_z * total_q)
    return (totals[0] * scale_x, totals[1] * scale_y, totals[2] * scale_z, totals[3] * scale_core)


MESH = pl.DeviceIdType.MESH
PAD = 16


def iota(shape, dim):
    return lax.broadcasted_iota(jnp.int32, shape, dim)


def unit_f32(index, stream, salt):
    return unit_value(index, stream, salt).astype(jnp.float32)


def dot_f32(left, right):
    return jnp.dot(left, right, preferred_element_type=jnp.float32)


def dot_split(left, right):
    upper = left.astype(jnp.bfloat16)
    lower = (left - upper.astype(jnp.float32)).astype(jnp.bfloat16)
    return dot_f32(upper, right) + dot_f32(lower, right)


def sketch_kernel(
    sizes,
    scales,
    streams_hbm,
    snaps_hbm,
    flow_hbm,
    out_x,
    out_y,
    out_z,
    out_core,
    streams,
    snaps,
    flow,
    y_send,
    y_got,
    y_out,
    y_in,
    z_send,
    z_got,
    z_out,
    z_in,
    c_send,
    c_got,
    c_out,
    c_in,
    small_sem,
    load_sem,
    pair_send,
    pair_recv,
    y_ssem,
    y_rsem,
    c_ssem,
    c_rsem,
    z_ssem,
    z_rsem,
):
    slabs, zsplit, batches, local_snaps, variables, cells_y, cells_z = sizes
    scale_x, scale_y, scale_z, scale_core = scales
    pairs = batches * local_snaps
    total_q = pairs * variables
    chips = slabs * zsplit
    rows_y = cells_y // (2 * chips)
    rows_z = K // (2 * slabs)
    rows_m = S // slabs
    rows_c = slabs * PAD
    total_z = cells_z * zsplit
    gx = lax.axis_index("gx")
    gz = lax.axis_index("gz")
    vert = lax.axis_index("vert")
    other = 1 - vert
    offsets = [(dx, dz) for dx in range(slabs) for dz in range(zsplit)]
    far_first = sorted(range(1, chips), key=lambda i: -min(offsets[i][0], slabs - offsets[i][0]))

    def target(dx, dz):
        return {"gx": lax.rem(gx + dx, slabs), "gz": lax.rem(gz + dz, zsplit)}

    smalls = [
        pltpu.make_async_copy(streams_hbm, streams, small_sem.at[0]),
        pltpu.make_async_copy(snaps_hbm, snaps, small_sem.at[1]),
    ]
    loads = [
        pltpu.make_async_copy(
            flow_hbm.at[pl.ds(p * variables, variables)],
            flow.at[pl.ds(p * variables, variables)],
            load_sem.at[p],
        )
        for p in range(pairs)
    ]
    for load in smalls + loads:
        load.start()
    barrier = pltpu.get_barrier_semaphore()
    pl.semaphore_signal(barrier, inc=1, device_id={"vert": other}, device_id_type=MESH)
    for dx, dz in offsets[1:]:
        pl.semaphore_signal(barrier, inc=1, device_id=target(dx, dz), device_id_type=MESH)

    low = jnp.bfloat16
    for load in smalls:
        load.wait()
    fac = streams[0]
    cor = streams[1]

    def run_ids(q_index):
        ids = jnp.zeros(q_index.shape, jnp.int32)
        for q in range(total_q):
            p = q // variables
            run = snaps[p // local_snaps, p % local_snaps] * variables + q % variables
            ids = jnp.where(q_index == q, run, ids)
        return ids

    def pair_copy(src, dst, which):
        return pltpu.make_async_remote_copy(
            src_ref=src,
            dst_ref=dst,
            send_sem=pair_send.at[which],
            recv_sem=pair_recv.at[which],
            device_id={"vert": other},
            device_id_type=MESH,
        )

    z_base = gz * cells_z
    az_tab = unit_value(
        (z_base + iota((cells_z, K), 0)) * K + iota((cells_z, K), 1), fac, 3
    )
    q_rows = -(-total_q // 8) * 8
    r_rows = run_ids(iota((q_rows, K), 0))
    aq_tab = unit_f32(r_rows * K + iota((q_rows, K), 1), fac, 4)
    ax_row = unit_f32(gx * K + iota((8, K), 1), fac, 1)[0:1]
    for h, side in enumerate((other, vert)):
        wide = jnp.zeros((chips * rows_y, K), jnp.float32)
        for q in range(total_q):
            if h == 0 and q % variables == 0:
                loads[q // variables].wait()
            rows = flow[q, :, side].reshape(chips * rows_y, cells_z)
            wide = wide + dot_f32(rows, az_tab) * aq_tab[q : q + 1]
        wide = (wide * ax_row).reshape(chips, rows_y, K)
        if h == 0:
            y_send[...] = wide
            pl.semaphore_wait(barrier, chips)
            pair_y = pair_copy(y_send, y_got, 2)
            pair_y.start()

    y_row = iota((cells_y, K), 0)
    ay_tab = unit_value(y_row * K + iota((cells_y, K), 1), fac, 2)
    m_lane = iota((cells_y, K), 1)
    m_ids = (m_lane >> 4) * rows_m + (m_lane & (PAD - 1))
    phy_tab = unit_value(m_ids * cells_y + y_row, cor, 6)
    y_tabs = jnp.concatenate([ay_tab, phy_tab], axis=1)
    phq_tab = [unit_f32(r_rows * E + e, cor, 8) for e in range(E)]

    pair_y.wait_recv()
    y_out[...] = wide + y_got[...]
    y_copies = [None] * chips
    for i in far_first:
        dest = target(*offsets[i])
        copy = pltpu.make_async_remote_copy(
            src_ref=y_out.at[dest["gx"] * zsplit + dest["gz"]],
            dst_ref=y_in.at[i - 1],
            send_sem=y_ssem.at[i - 1],
            recv_sem=y_rsem.at[i - 1],
            device_id=dest,
            device_id_type=MESH,
        )
        copy.start()
        y_copies[i] = copy

    deep = jnp.zeros((cells_z, K), jnp.float32)
    halves = [jnp.zeros((cells_z, K), jnp.float32) for e in range(E)]
    for q in range(total_q):
        both = lax.dot_general(
            flow[q].reshape(cells_y, cells_z),
            y_tabs,
            (((0,), (0,)), ((), ())),
            preferred_element_type=jnp.float32,
        )
        deep = deep + both[:, :K] * aq_tab[q : q + 1]
        for e in range(E):
            halves[e] = halves[e] + both[:, K:] * phq_tab[e][q : q + 1]
    lane = iota((cells_z, K), 1)
    phz_tab = unit_f32((lane & 63) * total_z + z_base + iota((cells_z, K), 0), cor, 7)
    core = None
    for e in range(E):
        right = jnp.where((lane >> 6) == e, phz_tab, 0.0).astype(low)
        part = dot_split(halves[e].T[:rows_c], right)
        core = part if core is None else core + part
    x_row = jnp.sum(deep * az_tab.astype(jnp.float32), axis=0, keepdims=True)
    core = jnp.where((iota((rows_c, K), 0) & (PAD - 1)) == rows_m, x_row, core)
    for g in range(slabs):
        c_send[g] = core[g * PAD : g * PAD + rows_m + 1]
    pair_c = pair_copy(c_send, c_got, 1)
    pair_c.start()
    ax_turned = unit_f32(gx * K + iota((K, K), 0), fac, 1)
    deep = deep.T * ax_turned
    for g in range(slabs):
        for v in range(2):
            at = (2 * g + v) * rows_z
            z_send[v, g] = deep[at : at + rows_z]
    pair_z = pair_copy(z_send.at[other], z_got, 0)
    pair_z.start()

    select_at = iota((1, 640), 1)
    lane_m = select_at // S
    lane_n = select_at - lane_m * S
    spread = jnp.where((iota((K, 640), 0) & 63) == lane_n, 1.0, 0.0).astype(low)
    keep = (iota((rows_c, 640), 0) & (PAD - 1)) == lane_m
    slot = iota((S, K), 1) >> 4
    x_ids = (gx - slot + 2 * slabs) & (slabs - 1)
    phx = unit_value(iota((S, K), 0) * slabs + x_ids, cor, 5)

    c_copies = [None] * chips
    pair_c.wait_recv()
    c_out[...] = c_send[...] + c_got[...]
    for i in far_first:
        dest = target(*offsets[i])
        copy = pltpu.make_async_remote_copy(
            src_ref=c_out.at[dest["gx"]],
            dst_ref=c_in.at[i - 1],
            send_sem=c_ssem.at[i - 1],
            recv_sem=c_rsem.at[i - 1],
            device_id=dest,
            device_id_type=MESH,
        )
        copy.start()
        c_copies[i] = copy
    z_copies = []
    pair_z.wait_recv()
    z_out[...] = z_send[vert] + z_got[...]
    for dx in range(1, slabs):
        to = lax.rem(gx + dx, slabs)
        copy = pltpu.make_async_remote_copy(
            src_ref=z_out.at[to],
            dst_ref=z_in.at[dx - 1],
            send_sem=z_ssem.at[dx - 1],
            recv_sem=z_rsem.at[dx - 1],
            device_id={"gx": to},
            device_id_type=MESH,
        )
        copy.start()
        z_copies.append(copy)

    total = y_out[gx * zsplit + gz]
    for i in range(1, chips):
        y_copies[i].wait_recv()
        total = total + y_in[i - 1]
    out_y[...] = total * scale_y
    slots = []
    for dx in range(slabs):
        total = c_out[gx] if dx == 0 else None
        for dz in range(zsplit):
            i = dx * zsplit + dz
            if i == 0:
                continue
            c_copies[i].wait_recv()
            total = c_in[i - 1] if total is None else total + c_in[i - 1]
        if dx == 0:
            out_x[...] = total[rows_m : rows_m + 1] * scale_x
        slots.append(jnp.concatenate([total, jnp.zeros((PAD - rows_m - 1, K), jnp.float32)], axis=0))
    core = jnp.concatenate(slots, axis=0) * scale_core
    upper = core.astype(low)
    lower = (core - upper.astype(jnp.float32)).astype(low)
    core_lane = iota((rows_c, K), 1) >> 6
    zero = jnp.zeros((rows_c, K), low)
    left = jnp.concatenate(
        [jnp.where(core_lane == e, part, zero) for e in range(E) for part in (upper, lower)],
        axis=0,
    )
    placed = dot_f32(left, spread)
    for e in range(E):
        at = 2 * e * rows_c
        right = jnp.concatenate(
            [
                jnp.where(keep, placed[at + s * rows_c : at + (s + 1) * rows_c], 0.0)
                for s in range(2)
            ],
            axis=0,
        ).astype(low)
        out_core[e] = dot_f32(phx, right)[:, : rows_m * S]

    total = z_out[gx]
    for i, copy in enumerate(z_copies):
        copy.wait_recv()
        total = total + z_in[i]
    out_z[...] = total * scale_z
    started = [pair_z, pair_c, pair_y] + z_copies + c_copies[1:] + y_copies[1:]
    for copy in started:
        copy.wait_send()


def finish_kernel(*refs):
    count = len(refs) // 2
    for i in range(count):
        refs[count + i][...] = refs[i][...]


def shards_fused(sizes, flow_field, test_streams, snapshot_ids):
    slabs, zsplit, batches, local_snaps, variables, cells_y, cells_z = sizes
    pairs = batches * local_snaps
    chips = slabs * zsplit
    rows_y = cells_y // (2 * chips)
    rows_z = K // (2 * slabs)
    rows_m = S // slabs
    total_q = pairs * variables
    f32 = jnp.float32
    anywhere = pl.BlockSpec(memory_space=pl.ANY)
    vmem = pl.BlockSpec(memory_space=pltpu.VMEM)
    dma = pltpu.SemaphoreType.DMA
    total_z = cells_z * zsplit
    all_q = 2 * total_q
    scales = (
        3.0**1.5 / math.sqrt(cells_y * total_z * all_q),
        3.0**1.5 / math.sqrt(slabs * total_z * all_q),
        3.0**1.5 / math.sqrt(slabs * cells_y * all_q),
        9.0 / math.sqrt(slabs * cells_y * total_z * all_q),
    )
    outs = [
        jax.ShapeDtypeStruct((1, K), f32),
        jax.ShapeDtypeStruct((rows_y, K), f32),
        jax.ShapeDtypeStruct((rows_z, cells_z), f32),
        jax.ShapeDtypeStruct((E, S, rows_m * S), f32),
    ]
    parts = pl.pallas_call(
        functools.partial(sketch_kernel, sizes, scales),
        name="sketch",
        out_shape=outs,
        in_specs=[anywhere] * 3,
        out_specs=[vmem] * 4,
        scratch_shapes=[
            pltpu.SMEM(test_streams.shape, jnp.int32),
            pltpu.SMEM(snapshot_ids.shape, jnp.int32),
            pltpu.VMEM((total_q, chips, 2, rows_y, cells_z), jnp.bfloat16),
            pltpu.VMEM((chips, rows_y, K), f32),
            pltpu.VMEM((chips, rows_y, K), f32),
            pltpu.VMEM((chips, rows_y, K), f32),
            pltpu.VMEM((chips - 1, rows_y, K), f32),
            pltpu.VMEM((2, slabs, rows_z, cells_z), f32),
            pltpu.VMEM((slabs, rows_z, cells_z), f32),
            pltpu.VMEM((slabs, rows_z, cells_z), f32),
            pltpu.VMEM((slabs - 1, rows_z, cells_z), f32),
            pltpu.VMEM((slabs, rows_m + 1, K), f32),
            pltpu.VMEM((slabs, rows_m + 1, K), f32),
            pltpu.VMEM((slabs, rows_m + 1, K), f32),
            pltpu.VMEM((chips - 1, rows_m + 1, K), f32),
            dma((2,)),
            dma((pairs,)),
            dma((3,)),
            dma((3,)),
            dma((chips - 1,)),
            dma((chips - 1,)),
            dma((chips - 1,)),
            dma((chips - 1,)),
            dma((slabs - 1,)),
            dma((slabs - 1,)),
        ],
        compiler_params=pltpu.CompilerParams(
            collective_id=0, has_side_effects=True, vmem_limit_bytes=63 * 2**20
        ),
    )(test_streams, snapshot_ids, flow_field.reshape(total_q, chips, 2, rows_y, cells_z))
    out_x, out_y, out_z, out_core = pl.pallas_call(
        finish_kernel,
        name="finish",
        out_shape=outs,
        in_specs=[vmem] * 4,
        out_specs=[vmem] * 4,
        compiler_params=pltpu.CompilerParams(vmem_limit_bytes=63 * 2**20),
    )(*parts)
    return (out_x, out_y, out_z.T, jnp.transpose(out_core, (2, 0, 1)))


def shards(flow_field, test_streams, snapshot_ids):
    batches, local_snaps, variables, cells_x, cells_y, cells_z = flow_field.shape
    slabs = lax.axis_size("gx")
    zsplit = lax.axis_size("gz")
    fits = (
        lax.axis_size("vert") == 2
        and cells_x == 1
        and cells_z == K
        and cells_y % (16 * slabs * zsplit) == 0
        and slabs == 4
        and zsplit > 1
        and cells_y % (32 * slabs * zsplit) == 0
        and batches * local_snaps * variables <= K
    )
    if not fits:
        return shards_general(flow_field, test_streams, snapshot_ids)
    sizes = (slabs, zsplit, batches, local_snaps, variables, cells_y, cells_z)
    return shards_fused(sizes, flow_field, test_streams, snapshot_ids)


def solution(mesh):
    in_specs = (P("groups", "vert", None, "gx", None, "gz"), P("groups"), P("groups", "vert"))
    out_specs = (
        P(("groups", "gx"), None),
        P(("groups", "gx", "gz", "vert"), None),
        P(("groups", "gz"), ("gx", "vert")),
        P(("groups", "gx"), None, None),
    )
    return jax.shard_map(shards, mesh=mesh, in_specs=in_specs, out_specs=out_specs, check_vma=False)
```

```python
import functools
import math

import jax
import jax.numpy as jnp
from jax import lax
from jax.experimental import pallas as pl
from jax.experimental.pallas import tpu as pltpu
from jax.sharding import PartitionSpec as P

K = 128
S = 48
E = 2


def hash_index(index, stream, salt):
    mixed = index * -1640531535 + stream * -2048144777 + salt
    mixed = jnp.bitwise_xor(mixed, lax.shift_right_logical(mixed, jnp.int32(16)))
    mixed = mixed * 739982445
    mixed = jnp.bitwise_xor(mixed, lax.shift_right_logical(mixed, jnp.int32(13)))
    mixed = mixed * 695872825
    return jnp.bitwise_xor(mixed, lax.shift_right_logical(mixed, jnp.int32(16)))


def unit_value(index, stream, salt):
    upper = lax.shift_right_logical(hash_index(index, stream, salt), jnp.int32(9))
    return ((2 * upper + 1).astype(jnp.float32) * 2.0 ** (-24) - 1.0).astype(jnp.bfloat16)


def test_table(row_ids, col_ids, stride, stream, salt):
    return unit_value(row_ids[:, None] * stride + col_ids[None, :], stream, salt)


def shards_general(flow_field, test_streams, snapshot_ids):
    highest = lax.Precision.HIGHEST
    batches, local_snaps, variables, cells_x, cells_y, cells_z = flow_field.shape
    slabs_x = lax.axis_size("gx")
    total_x = cells_x * slabs_x
    total_z = cells_z * lax.axis_size("gz")
    total_q = variables * batches * local_snaps * lax.axis_size("vert")
    factor_stream = test_streams[0]
    core_stream = test_streams[1]
    rank_ids = jnp.arange(K, dtype=jnp.int32)
    sketch_ids = jnp.arange(S, dtype=jnp.int32)
    x_ids = lax.axis_index("gx") * cells_x + jnp.arange(cells_x, dtype=jnp.int32)
    y_ids = jnp.arange(cells_y, dtype=jnp.int32)
    z_ids = lax.axis_index("gz") * cells_z + jnp.arange(cells_z, dtype=jnp.int32)
    ax_tab = test_table(x_ids, rank_ids, K, factor_stream, 1).astype(jnp.float32)
    ay_low = test_table(y_ids, rank_ids, K, factor_stream, 2)
    az_low = test_table(z_ids, rank_ids, K, factor_stream, 3)
    ay_tab = ay_low.astype(jnp.float32)
    phy_low = test_table(sketch_ids, y_ids, cells_y, core_stream, 6)
    phz_low = test_table(sketch_ids, z_ids, total_z, core_stream, 7)

    def batch_terms(batch_idx):
        blocks = flow_field[batch_idx].reshape(-1, cells_x, cells_y, cells_z)
        pairs = blocks.shape[0]
        q_ids = (
            snapshot_ids[batch_idx][:, None] * variables
            + jnp.arange(variables, dtype=jnp.int32)[None, :]
        ).reshape(-1)
        aq_tab = test_table(q_ids, rank_ids, K, factor_stream, 4).astype(jnp.float32)
        phq_low = test_table(q_ids, jnp.arange(E, dtype=jnp.int32), E, core_stream, 8)
        rows_z = blocks.reshape(-1, cells_z)
        along_z = jnp.dot(rows_z, az_low, preferred_element_type=jnp.float32).reshape(
            pairs, cells_x, cells_y, K
        )
        along_y = jnp.einsum("qxyz,yk->qxzk", blocks, ay_low, preferred_element_type=jnp.float32)
        weights = aq_tab[:, None, :] * ax_tab[None, :, :]
        part_x = jnp.sum(
            jnp.sum(along_z * ay_tab[None, None, :, :], axis=2) * aq_tab[:, None, :], axis=0
        )
        part_y = jnp.sum(along_z * weights[:, :, None, :], axis=(0, 1))
        part_z = jnp.sum(along_y * weights[:, :, None, :], axis=(0, 1))
        first = jnp.dot(rows_z, phz_low.T, preferred_element_type=jnp.float32).reshape(
            pairs, cells_x, cells_y, S
        )
        second = jnp.einsum("qxyc,by->qxbc", first, phy_low.astype(jnp.float32), precision=highest)
        partial_core = jnp.einsum(
            "qxbc,qe->bcex", second, phq_low.astype(jnp.float32), precision=highest
        )
        return (part_x, part_y, part_z, partial_core.reshape(S * S, E, cells_x))

    def finish(part_x, part_y, part_z, partial_core):
        summed, sum_x = lax.psum((partial_core, part_x), ("gz", "vert"))
        phx_whole = test_table(
            sketch_ids, jnp.arange(total_x, dtype=jnp.int32), total_x, core_stream, 5
        ).astype(jnp.float32)
        core = jnp.einsum(
            "rex,ax->rea",
            lax.all_to_all(summed, "gx", split_axis=0, concat_axis=2, tiled=True),
            phx_whole,
            precision=highest,
        )
        sum_z = lax.psum_scatter(part_z, ("gx", "vert"), scatter_dimension=1, tiled=True)
        sum_y = lax.psum_scatter(part_y, ("gx", "gz", "vert"), scatter_dimension=0, tiled=True)
        return (sum_x, sum_y, sum_z, core)

    terms = [batch_terms(batch_idx) for batch_idx in range(batches)]
    totals = finish(terms[0][0], terms[0][1], terms[0][2], terms[0][3])
    for later in terms[1:]:
        latest = finish(later[0], later[1], later[2], later[3])
        totals = tuple((earlier + newer for earlier, newer in zip(totals, latest)))
    scale_x = 3.0**1.5 / math.sqrt(cells_y * total_z * total_q)
    scale_y = 3.0**1.5 / math.sqrt(total_x * total_z * total_q)
    scale_z = 3.0**1.5 / math.sqrt(total_x * cells_y * total_q)
    scale_core = 9.0 / math.sqrt(total_x * cells_y * total_z * total_q)
    return (totals[0] * scale_x, totals[1] * scale_y, totals[2] * scale_z, totals[3] * scale_core)


MESH = pl.DeviceIdType.MESH
PAD = 16


def iota(shape, dim):
    return lax.broadcasted_iota(jnp.int32, shape, dim)


def unit_f32(index, stream, salt):
    return unit_value(index, stream, salt).astype(jnp.float32)


def dot_f32(left, right):
    return jnp.dot(left, right, preferred_element_type=jnp.float32)


def dot_split(left, right):
    upper = left.astype(jnp.bfloat16)
    lower = (left - upper.astype(jnp.float32)).astype(jnp.bfloat16)
    return dot_f32(upper, right) + dot_f32(lower, right)


def sketch_kernel(
    sizes,
    scales,
    streams_hbm,
    snaps_hbm,
    flow_hbm,
    out_x,
    out_y,
    out_z,
    out_core,
    streams,
    snaps,
    flow,
    y_send,
    y_got,
    y_out,
    y_in,
    z_send,
    z_got,
    z_out,
    z_in,
    c_send,
    c_got,
    c_out,
    c_in,
    small_sem,
    load_sem,
    pair_send,
    pair_recv,
    y_ssem,
    y_rsem,
    c_ssem,
    c_rsem,
    z_ssem,
    z_rsem,
):
    slabs, zsplit, batches, local_snaps, variables, cells_y, cells_z = sizes
    scale_x, scale_y, scale_z, scale_core = scales
    pairs = batches * local_snaps
    total_q = pairs * variables
    chips = slabs * zsplit
    rows_y = cells_y // (2 * chips)
    rows_z = K // (2 * slabs)
    rows_m = S // slabs
    rows_c = slabs * PAD
    total_z = cells_z * zsplit
    gx = lax.axis_index("gx")
    gz = lax.axis_index("gz")
    vert = lax.axis_index("vert")
    other = 1 - vert
    offsets = [(dx, dz) for dx in range(slabs) for dz in range(zsplit)]
    far_first = sorted(range(1, chips), key=lambda i: -min(offsets[i][0], slabs - offsets[i][0]))

    def target(dx, dz):
        return {"gx": lax.rem(gx + dx, slabs), "gz": lax.rem(gz + dz, zsplit)}

    smalls = [
        pltpu.make_async_copy(streams_hbm, streams, small_sem.at[0]),
        pltpu.make_async_copy(snaps_hbm, snaps, small_sem.at[1]),
    ]
    loads = [
        pltpu.make_async_copy(
            flow_hbm.at[pl.ds(p * variables, variables)],
            flow.at[pl.ds(p * variables, variables)],
            load_sem.at[p],
        )
        for p in range(pairs)
    ]
    for load in smalls + loads:
        load.start()
    barrier = pltpu.get_barrier_semaphore()
    pl.semaphore_signal(barrier, inc=1, device_id={"vert": other}, device_id_type=MESH)
    for dx, dz in offsets[1:]:
        pl.semaphore_signal(barrier, inc=1, device_id=target(dx, dz), device_id_type=MESH)

    low = jnp.bfloat16
    select_at = iota((1, 640), 1)
    lane_m = select_at // S
    lane_n = select_at - lane_m * S
    spread = jnp.where((iota((K, 640), 0) & 63) == lane_n, 1.0, 0.0).astype(low)
    keep = (iota((rows_c, 640), 0) & (PAD - 1)) == lane_m
    for load in smalls:
        load.wait()
    fac = streams[0]
    cor = streams[1]

    def run_ids(q_index):
        ids = jnp.zeros(q_index.shape, jnp.int32)
        for q in range(total_q):
            p = q // variables
            run = snaps[p // local_snaps, p % local_snaps] * variables + q % variables
            ids = jnp.where(q_index == q, run, ids)
        return ids

    z_base = gz * cells_z
    ay_turned = unit_value(iota((K, cells_y), 1) * K + iota((K, cells_y), 0), fac, 2)
    m_row = iota((rows_c, cells_y), 0)
    m_ids = (m_row >> 4) * rows_m + (m_row & (PAD - 1))
    phy_tab = unit_value(m_ids * cells_y + iota((rows_c, cells_y), 1), cor, 6)
    turned = jnp.concatenate([ay_turned, phy_tab], axis=0)
    q_rows = -(-total_q // 8) * 8
    r_rows = run_ids(iota((q_rows, K), 0))
    aq_tab = unit_f32(r_rows * K + iota((q_rows, K), 1), fac, 4)
    phq_tab = [unit_f32(r_rows * E + e, cor, 8) for e in range(E)]
    aq_turned = unit_f32(run_ids(iota((1, K), 1)) * K + iota((K, K), 0), fac, 4)
    ax_turned = unit_f32(gx * K + iota((K, K), 0), fac, 1)
    az_tab = unit_value(
        (z_base + iota((cells_z, K), 0)) * K + iota((cells_z, K), 1), fac, 3
    )

    deep = jnp.zeros((K, cells_z), jnp.float32)
    halves = [jnp.zeros((rows_c, cells_z), jnp.float32) for e in range(E)]
    waited = 0
    for first in range(0, total_q, 2):
        while waited * variables < min(first + 2, total_q):
            loads[waited].wait()
            waited += 1
        group = range(first, min(first + 2, total_q))
        both = dot_f32(turned, jnp.concatenate([flow[q].reshape(cells_y, cells_z) for q in group], axis=1))
        for i, q in enumerate(group):
            lanes = both[:, i * cells_z : (i + 1) * cells_z]
            deep = deep + lanes[:K] * aq_turned[:, q : q + 1]
            for e in range(E):
                halves[e] = halves[e] + lanes[K:] * phq_tab[e][q : q + 1]
    for g in range(slabs):
        for v in range(2):
            at = (2 * g + v) * rows_z
            z_send[v, g] = deep[at : at + rows_z] * ax_turned[at : at + rows_z]

    pl.semaphore_wait(barrier, chips)

    def pair_copy(src, dst, which):
        return pltpu.make_async_remote_copy(
            src_ref=src,
            dst_ref=dst,
            send_sem=pair_send.at[which],
            recv_sem=pair_recv.at[which],
            device_id={"vert": other},
            device_id_type=MESH,
        )

    pair_z = pair_copy(z_send.at[other], z_got, 0)
    pair_z.start()
    lane = iota((cells_z, K), 1)
    phz_tab = unit_f32((lane & 63) * total_z + z_base + iota((cells_z, K), 0), cor, 7)
    core = None
    for e in range(E):
        right = jnp.where((lane >> 6) == e, phz_tab, 0.0).astype(low)
        part = dot_split(halves[e], right)
        core = part if core is None else core + part
    x_row = jnp.sum(deep.T * az_tab.astype(jnp.float32), axis=0, keepdims=True)
    core = jnp.where((iota((rows_c, K), 0) & (PAD - 1)) == rows_m, x_row, core)
    for g in range(slabs):
        c_send[g] = core[g * PAD : g * PAD + rows_m + 1]
    pair_c = pair_copy(c_send, c_got, 1)
    pair_c.start()

    ax_row = unit_f32(gx * K + iota((8, K), 1), fac, 1)[0:1]
    z_copies = []
    c_copies = [None] * chips
    for h, side in enumerate((other, vert)):
        wide = jnp.zeros((chips * rows_y, K), jnp.float32)
        for q in range(total_q):
            rows = flow[q, :, side].reshape(chips * rows_y, cells_z)
            wide = wide + dot_f32(rows, az_tab) * aq_tab[q : q + 1]
        wide = (wide * ax_row).reshape(chips, rows_y, K)
        if h == 0:
            y_send[...] = wide
            pair_y = pair_copy(y_send, y_got, 2)
            pair_y.start()
        if h == 0:
            pair_z.wait_recv()
            z_out[...] = z_send[vert] + z_got[...]
            for dx in range(1, slabs):
                to = lax.rem(gx + dx, slabs)
                copy = pltpu.make_async_remote_copy(
                    src_ref=z_out.at[to],
                    dst_ref=z_in.at[dx - 1],
                    send_sem=z_ssem.at[dx - 1],
                    recv_sem=z_rsem.at[dx - 1],
                    device_id={"gx": to},
                    device_id_type=MESH,
                )
                copy.start()
                z_copies.append(copy)
            pair_c.wait_recv()
            c_out[...] = c_send[...] + c_got[...]
            for i in far_first:
                dest = target(*offsets[i])
                copy = pltpu.make_async_remote_copy(
                    src_ref=c_out.at[dest["gx"]],
                    dst_ref=c_in.at[i - 1],
                    send_sem=c_ssem.at[i - 1],
                    recv_sem=c_rsem.at[i - 1],
                    device_id=dest,
                    device_id_type=MESH,
                )
                copy.start()
                c_copies[i] = copy
    pair_y.wait_recv()
    y_out[...] = wide + y_got[...]
    y_copies = [None] * chips
    for i in far_first:
        dest = target(*offsets[i])
        copy = pltpu.make_async_remote_copy(
            src_ref=y_out.at[dest["gx"] * zsplit + dest["gz"]],
            dst_ref=y_in.at[i - 1],
            send_sem=y_ssem.at[i - 1],
            recv_sem=y_rsem.at[i - 1],
            device_id=dest,
            device_id_type=MESH,
        )
        copy.start()
        y_copies[i] = copy
    total = z_out[gx]
    for i, copy in enumerate(z_copies):
        copy.wait_recv()
        total = total + z_in[i]
    out_z[...] = total * scale_z
    slots = []
    for dx in range(slabs):
        total = c_out[gx] if dx == 0 else None
        for dz in range(zsplit):
            i = dx * zsplit + dz
            if i == 0:
                continue
            c_copies[i].wait_recv()
            total = c_in[i - 1] if total is None else total + c_in[i - 1]
        if dx == 0:
            out_x[...] = total[rows_m : rows_m + 1] * scale_x
        slots.append(jnp.concatenate([total, jnp.zeros((PAD - rows_m - 1, K), jnp.float32)], axis=0))
    core = jnp.concatenate(slots, axis=0) * scale_core
    upper = core.astype(low)
    lower = (core - upper.astype(jnp.float32)).astype(low)
    core_lane = iota((rows_c, K), 1) >> 6
    zero = jnp.zeros((rows_c, K), low)
    left = jnp.concatenate(
        [jnp.where(core_lane == e, part, zero) for e in range(E) for part in (upper, lower)],
        axis=0,
    )
    placed = dot_f32(left, spread)
    slot = iota((S, K), 1) >> 4
    x_ids = (gx - slot + 2 * slabs) & (slabs - 1)
    phx = unit_value(iota((S, K), 0) * slabs + x_ids, cor, 5)
    for e in range(E):
        at = 2 * e * rows_c
        right = jnp.concatenate(
            [
                jnp.where(keep, placed[at + s * rows_c : at + (s + 1) * rows_c], 0.0)
                for s in range(2)
            ],
            axis=0,
        ).astype(low)
        out_core[e] = dot_f32(phx, right)[:, : rows_m * S]

    total = y_out[gx * zsplit + gz]
    for i in range(1, chips):
        y_copies[i].wait_recv()
        total = total + y_in[i - 1]
    out_y[...] = total * scale_y
    started = [pair_z, pair_c, pair_y] + z_copies + c_copies[1:] + y_copies[1:]
    for copy in started:
        copy.wait_send()


def finish_kernel(*refs):
    count = len(refs) // 2
    for i in range(count):
        refs[count + i][...] = refs[i][...]


def shards_fused(sizes, flow_field, test_streams, snapshot_ids):
    slabs, zsplit, batches, local_snaps, variables, cells_y, cells_z = sizes
    pairs = batches * local_snaps
    chips = slabs * zsplit
    rows_y = cells_y // (2 * chips)
    rows_z = K // (2 * slabs)
    rows_m = S // slabs
    total_q = pairs * variables
    f32 = jnp.float32
    anywhere = pl.BlockSpec(memory_space=pl.ANY)
    vmem = pl.BlockSpec(memory_space=pltpu.VMEM)
    dma = pltpu.SemaphoreType.DMA
    total_z = cells_z * zsplit
    all_q = 2 * total_q
    scales = (
        3.0**1.5 / math.sqrt(cells_y * total_z * all_q),
        3.0**1.5 / math.sqrt(slabs * total_z * all_q),
        3.0**1.5 / math.sqrt(slabs * cells_y * all_q),
        9.0 / math.sqrt(slabs * cells_y * total_z * all_q),
    )
    outs = [
        jax.ShapeDtypeStruct((1, K), f32),
        jax.ShapeDtypeStruct((rows_y, K), f32),
        jax.ShapeDtypeStruct((rows_z, cells_z), f32),
        jax.ShapeDtypeStruct((E, S, rows_m * S), f32),
    ]
    parts = pl.pallas_call(
        functools.partial(sketch_kernel, sizes, scales),
        name="sketch",
        out_shape=outs,
        in_specs=[anywhere] * 3,
        out_specs=[vmem] * 4,
        scratch_shapes=[
            pltpu.SMEM(test_streams.shape, jnp.int32),
            pltpu.SMEM(snapshot_ids.shape, jnp.int32),
            pltpu.VMEM((total_q, chips, 2, rows_y, cells_z), jnp.bfloat16),
            pltpu.VMEM((chips, rows_y, K), f32),
            pltpu.VMEM((chips, rows_y, K), f32),
            pltpu.VMEM((chips, rows_y, K), f32),
            pltpu.VMEM((chips - 1, rows_y, K), f32),
            pltpu.VMEM((2, slabs, rows_z, cells_z), f32),
            pltpu.VMEM((slabs, rows_z, cells_z), f32),
            pltpu.VMEM((slabs, rows_z, cells_z), f32),
            pltpu.VMEM((slabs - 1, rows_z, cells_z), f32),
            pltpu.VMEM((slabs, rows_m + 1, K), f32),
            pltpu.VMEM((slabs, rows_m + 1, K), f32),
            pltpu.VMEM((slabs, rows_m + 1, K), f32),
            pltpu.VMEM((chips - 1, rows_m + 1, K), f32),
            dma((2,)),
            dma((pairs,)),
            dma((3,)),
            dma((3,)),
            dma((chips - 1,)),
            dma((chips - 1,)),
            dma((chips - 1,)),
            dma((chips - 1,)),
            dma((slabs - 1,)),
            dma((slabs - 1,)),
        ],
        compiler_params=pltpu.CompilerParams(
            collective_id=0, has_side_effects=True, vmem_limit_bytes=63 * 2**20
        ),
    )(test_streams, snapshot_ids, flow_field.reshape(total_q, chips, 2, rows_y, cells_z))
    out_x, out_y, out_z, out_core = pl.pallas_call(
        finish_kernel,
        name="finish",
        out_shape=outs,
        in_specs=[vmem] * 4,
        out_specs=[vmem] * 4,
        compiler_params=pltpu.CompilerParams(vmem_limit_bytes=63 * 2**20),
    )(*parts)
    return (out_x, out_y, out_z.T, jnp.transpose(out_core, (2, 0, 1)))


def shards(flow_field, test_streams, snapshot_ids):
    batches, local_snaps, variables, cells_x, cells_y, cells_z = flow_field.shape
    slabs = lax.axis_size("gx")
    zsplit = lax.axis_size("gz")
    fits = (
        lax.axis_size("vert") == 2
        and cells_x == 1
        and cells_z == K
        and cells_y % (16 * slabs * zsplit) == 0
        and slabs == 4
        and zsplit > 1
        and cells_y % (32 * slabs * zsplit) == 0
        and batches * local_snaps * variables <= K
    )
    if not fits:
        return shards_general(flow_field, test_streams, snapshot_ids)
    sizes = (slabs, zsplit, batches, local_snaps, variables, cells_y, cells_z)
    return shards_fused(sizes, flow_field, test_streams, snapshot_ids)


def solution(mesh):
    in_specs = (P("groups", "vert", None, "gx", None, "gz"), P("groups"), P("groups", "vert"))
    out_specs = (
        P(("groups", "gx"), None),
        P(("groups", "gx", "gz", "vert"), None),
        P(("groups", "gz"), ("gx", "vert")),
        P(("groups", "gx"), None, None),
    )
    return jax.shard_map(shards, mesh=mesh, in_specs=in_specs, out_specs=out_specs, check_vma=False)
```

```python
import functools
import math

import jax
import jax.numpy as jnp
from jax import lax
from jax.experimental import pallas as pl
from jax.experimental.pallas import tpu as pltpu
from jax.sharding import PartitionSpec as P

K = 128
S = 48
E = 2


def hash_index(index, stream, salt):
    mixed = index * -1640531535 + stream * -2048144777 + salt
    mixed = jnp.bitwise_xor(mixed, lax.shift_right_logical(mixed, jnp.int32(16)))
    mixed = mixed * 739982445
    mixed = jnp.bitwise_xor(mixed, lax.shift_right_logical(mixed, jnp.int32(13)))
    mixed = mixed * 695872825
    return jnp.bitwise_xor(mixed, lax.shift_right_logical(mixed, jnp.int32(16)))


def unit_value(index, stream, salt):
    upper = lax.shift_right_logical(hash_index(index, stream, salt), jnp.int32(9))
    return ((2 * upper + 1).astype(jnp.float32) * 2.0 ** (-24) - 1.0).astype(jnp.bfloat16)


def test_table(row_ids, col_ids, stride, stream, salt):
    return unit_value(row_ids[:, None] * stride + col_ids[None, :], stream, salt)


def shards_general(flow_field, test_streams, snapshot_ids):
    highest = lax.Precision.HIGHEST
    batches, local_snaps, variables, cells_x, cells_y, cells_z = flow_field.shape
    slabs_x = lax.axis_size("gx")
    total_x = cells_x * slabs_x
    total_z = cells_z * lax.axis_size("gz")
    total_q = variables * batches * local_snaps * lax.axis_size("vert")
    factor_stream = test_streams[0]
    core_stream = test_streams[1]
    rank_ids = jnp.arange(K, dtype=jnp.int32)
    sketch_ids = jnp.arange(S, dtype=jnp.int32)
    x_ids = lax.axis_index("gx") * cells_x + jnp.arange(cells_x, dtype=jnp.int32)
    y_ids = jnp.arange(cells_y, dtype=jnp.int32)
    z_ids = lax.axis_index("gz") * cells_z + jnp.arange(cells_z, dtype=jnp.int32)
    ax_tab = test_table(x_ids, rank_ids, K, factor_stream, 1).astype(jnp.float32)
    ay_low = test_table(y_ids, rank_ids, K, factor_stream, 2)
    az_low = test_table(z_ids, rank_ids, K, factor_stream, 3)
    ay_tab = ay_low.astype(jnp.float32)
    phy_low = test_table(sketch_ids, y_ids, cells_y, core_stream, 6)
    phz_low = test_table(sketch_ids, z_ids, total_z, core_stream, 7)

    def batch_terms(batch_idx):
        blocks = flow_field[batch_idx].reshape(-1, cells_x, cells_y, cells_z)
        pairs = blocks.shape[0]
        q_ids = (
            snapshot_ids[batch_idx][:, None] * variables
            + jnp.arange(variables, dtype=jnp.int32)[None, :]
        ).reshape(-1)
        aq_tab = test_table(q_ids, rank_ids, K, factor_stream, 4).astype(jnp.float32)
        phq_low = test_table(q_ids, jnp.arange(E, dtype=jnp.int32), E, core_stream, 8)
        rows_z = blocks.reshape(-1, cells_z)
        along_z = jnp.dot(rows_z, az_low, preferred_element_type=jnp.float32).reshape(
            pairs, cells_x, cells_y, K
        )
        along_y = jnp.einsum("qxyz,yk->qxzk", blocks, ay_low, preferred_element_type=jnp.float32)
        weights = aq_tab[:, None, :] * ax_tab[None, :, :]
        part_x = jnp.sum(
            jnp.sum(along_z * ay_tab[None, None, :, :], axis=2) * aq_tab[:, None, :], axis=0
        )
        part_y = jnp.sum(along_z * weights[:, :, None, :], axis=(0, 1))
        part_z = jnp.sum(along_y * weights[:, :, None, :], axis=(0, 1))
        first = jnp.dot(rows_z, phz_low.T, preferred_element_type=jnp.float32).reshape(
            pairs, cells_x, cells_y, S
        )
        second = jnp.einsum("qxyc,by->qxbc", first, phy_low.astype(jnp.float32), precision=highest)
        partial_core = jnp.einsum(
            "qxbc,qe->bcex", second, phq_low.astype(jnp.float32), precision=highest
        )
        return (part_x, part_y, part_z, partial_core.reshape(S * S, E, cells_x))

    def finish(part_x, part_y, part_z, partial_core):
        summed, sum_x = lax.psum((partial_core, part_x), ("gz", "vert"))
        phx_whole = test_table(
            sketch_ids, jnp.arange(total_x, dtype=jnp.int32), total_x, core_stream, 5
        ).astype(jnp.float32)
        core = jnp.einsum(
            "rex,ax->rea",
            lax.all_to_all(summed, "gx", split_axis=0, concat_axis=2, tiled=True),
            phx_whole,
            precision=highest,
        )
        sum_z = lax.psum_scatter(part_z, ("gx", "vert"), scatter_dimension=1, tiled=True)
        sum_y = lax.psum_scatter(part_y, ("gx", "gz", "vert"), scatter_dimension=0, tiled=True)
        return (sum_x, sum_y, sum_z, core)

    terms = [batch_terms(batch_idx) for batch_idx in range(batches)]
    totals = finish(terms[0][0], terms[0][1], terms[0][2], terms[0][3])
    for later in terms[1:]:
        latest = finish(later[0], later[1], later[2], later[3])
        totals = tuple((earlier + newer for earlier, newer in zip(totals, latest)))
    scale_x = 3.0**1.5 / math.sqrt(cells_y * total_z * total_q)
    scale_y = 3.0**1.5 / math.sqrt(total_x * total_z * total_q)
    scale_z = 3.0**1.5 / math.sqrt(total_x * cells_y * total_q)
    scale_core = 9.0 / math.sqrt(total_x * cells_y * total_z * total_q)
    return (totals[0] * scale_x, totals[1] * scale_y, totals[2] * scale_z, totals[3] * scale_core)


MESH = pl.DeviceIdType.MESH
PAD = 16


def iota(shape, dim):
    return lax.broadcasted_iota(jnp.int32, shape, dim)


def unit_f32(index, stream, salt):
    return unit_value(index, stream, salt).astype(jnp.float32)


def dot_f32(left, right):
    return jnp.dot(left, right, preferred_element_type=jnp.float32)


def dot_split(left, right):
    upper = left.astype(jnp.bfloat16)
    lower = (left - upper.astype(jnp.float32)).astype(jnp.bfloat16)
    return dot_f32(upper, right) + dot_f32(lower, right)


def sketch_kernel(
    sizes,
    scales,
    streams_hbm,
    snaps_hbm,
    flow_hbm,
    out_x,
    out_y,
    out_z,
    out_core,
    streams,
    snaps,
    flow,
    y_send,
    y_got,
    y_out,
    y_in,
    z_send,
    z_got,
    z_out,
    z_in,
    c_send,
    c_got,
    c_out,
    c_in,
    small_sem,
    load_sem,
    pair_send,
    pair_recv,
    y_ssem,
    y_rsem,
    c_ssem,
    c_rsem,
    z_ssem,
    z_rsem,
):
    slabs, zsplit, batches, local_snaps, variables, cells_y, cells_z = sizes
    scale_x, scale_y, scale_z, scale_core = scales
    pairs = batches * local_snaps
    total_q = pairs * variables
    chips = slabs * zsplit
    rows_y = cells_y // (2 * chips)
    rows_z = K // (2 * slabs)
    rows_m = S // slabs
    rows_c = slabs * PAD
    total_z = cells_z * zsplit
    gx = lax.axis_index("gx")
    gz = lax.axis_index("gz")
    vert = lax.axis_index("vert")
    other = 1 - vert
    offsets = [(dx, dz) for dx in range(slabs) for dz in range(zsplit)]
    far_first = sorted(range(1, chips), key=lambda i: -min(offsets[i][0], slabs - offsets[i][0]))

    def target(dx, dz):
        return {"gx": lax.rem(gx + dx, slabs), "gz": lax.rem(gz + dz, zsplit)}

    smalls = [
        pltpu.make_async_copy(streams_hbm, streams, small_sem.at[0]),
        pltpu.make_async_copy(snaps_hbm, snaps, small_sem.at[1]),
    ]
    loads = [
        pltpu.make_async_copy(
            flow_hbm.at[pl.ds(p * variables, variables)],
            flow.at[pl.ds(p * variables, variables)],
            load_sem.at[p],
        )
        for p in range(pairs)
    ]
    for load in smalls + loads:
        load.start()
    barrier = pltpu.get_barrier_semaphore()
    pl.semaphore_signal(barrier, inc=1, device_id={"vert": other}, device_id_type=MESH)
    for dx, dz in offsets[1:]:
        pl.semaphore_signal(barrier, inc=1, device_id=target(dx, dz), device_id_type=MESH)

    low = jnp.bfloat16
    select_at = iota((1, 640), 1)
    lane_m = select_at // S
    lane_n = select_at - lane_m * S
    spread = jnp.where((iota((K, 640), 0) & 63) == lane_n, 1.0, 0.0).astype(low)
    keep = (iota((rows_c, 640), 0) & (PAD - 1)) == lane_m
    for load in smalls:
        load.wait()
    fac = streams[0]
    cor = streams[1]

    def run_ids(q_index):
        ids = jnp.zeros(q_index.shape, jnp.int32)
        for q in range(total_q):
            p = q // variables
            run = snaps[p // local_snaps, p % local_snaps] * variables + q % variables
            ids = jnp.where(q_index == q, run, ids)
        return ids

    z_base = gz * cells_z
    ay_turned = unit_value(iota((K, cells_y), 1) * K + iota((K, cells_y), 0), fac, 2)
    m_row = iota((rows_c, cells_y), 0)
    m_ids = (m_row >> 4) * rows_m + (m_row & (PAD - 1))
    phy_tab = unit_value(m_ids * cells_y + iota((rows_c, cells_y), 1), cor, 6)
    turned = jnp.concatenate([ay_turned, phy_tab], axis=0)
    q_rows = -(-total_q // 8) * 8
    r_rows = run_ids(iota((q_rows, K), 0))
    aq_tab = unit_f32(r_rows * K + iota((q_rows, K), 1), fac, 4)
    phq_tab = [unit_f32(r_rows * E + e, cor, 8) for e in range(E)]
    aq_turned = unit_f32(run_ids(iota((1, K), 1)) * K + iota((K, K), 0), fac, 4)
    ax_turned = unit_f32(gx * K + iota((K, K), 0), fac, 1)
    az_tab = unit_value(
        (z_base + iota((cells_z, K), 0)) * K + iota((cells_z, K), 1), fac, 3
    )

    deep = jnp.zeros((K, cells_z), jnp.float32)
    halves = [jnp.zeros((rows_c, cells_z), jnp.float32) for e in range(E)]
    waited = 0
    for first in range(0, total_q, 2):
        while waited * variables < min(first + 2, total_q):
            loads[waited].wait()
            waited += 1
        group = range(first, min(first + 2, total_q))
        both = dot_f32(turned, jnp.concatenate([flow[q].reshape(cells_y, cells_z) for q in group], axis=1))
        for i, q in enumerate(group):
            lanes = both[:, i * cells_z : (i + 1) * cells_z]
            deep = deep + lanes[:K] * aq_turned[:, q : q + 1]
            for e in range(E):
                halves[e] = halves[e] + lanes[K:] * phq_tab[e][q : q + 1]
    for g in range(slabs):
        for v in range(2):
            at = (2 * g + v) * rows_z
            z_send[v, g] = deep[at : at + rows_z] * ax_turned[at : at + rows_z]

    pl.semaphore_wait(barrier, chips)

    def pair_copy(src, dst, which):
        return pltpu.make_async_remote_copy(
            src_ref=src,
            dst_ref=dst,
            send_sem=pair_send.at[which],
            recv_sem=pair_recv.at[which],
            device_id={"vert": other},
            device_id_type=MESH,
        )

    pair_z = pair_copy(z_send.at[other], z_got, 0)
    pair_z.start()
    lane = iota((cells_z, K), 1)
    phz_tab = unit_f32((lane & 63) * total_z + z_base + iota((cells_z, K), 0), cor, 7)
    core = None
    for e in range(E):
        right = jnp.where((lane >> 6) == e, phz_tab, 0.0).astype(low)
        part = dot_split(halves[e], right)
        core = part if core is None else core + part
    x_row = jnp.sum(deep.T * az_tab.astype(jnp.float32), axis=0, keepdims=True)
    core = jnp.where((iota((rows_c, K), 0) & (PAD - 1)) == rows_m, x_row, core)
    for g in range(slabs):
        c_send[g] = core[g * PAD : g * PAD + rows_m + 1]
    pair_c = pair_copy(c_send, c_got, 1)
    pair_c.start()

    ax_row = unit_f32(gx * K + iota((8, K), 1), fac, 1)[0:1]
    z_copies = []
    c_copies = [None] * chips
    for h, side in enumerate((other, vert)):
        wide = jnp.zeros((chips * rows_y, K), jnp.float32)
        for q in range(total_q):
            rows = flow[q, :, side].reshape(chips * rows_y, cells_z)
            wide = wide + dot_f32(rows, az_tab) * aq_tab[q : q + 1]
            if h == 0 and q == total_q // 2:
                pair_z.wait_recv()
                z_out[...] = z_send[vert] + z_got[...]
                for dx in range(1, slabs):
                    to = lax.rem(gx + dx, slabs)
                    copy = pltpu.make_async_remote_copy(
                        src_ref=z_out.at[to],
                        dst_ref=z_in.at[dx - 1],
                        send_sem=z_ssem.at[dx - 1],
                        recv_sem=z_rsem.at[dx - 1],
                        device_id={"gx": to},
                        device_id_type=MESH,
                    )
                    copy.start()
                    z_copies.append(copy)
        wide = (wide * ax_row).reshape(chips, rows_y, K)
        if h == 0:
            y_send[...] = wide
            pair_y = pair_copy(y_send, y_got, 2)
            pair_y.start()
        if h == 0:
            pair_c.wait_recv()
            c_out[...] = c_send[...] + c_got[...]
            for i in far_first:
                dest = target(*offsets[i])
                copy = pltpu.make_async_remote_copy(
                    src_ref=c_out.at[dest["gx"]],
                    dst_ref=c_in.at[i - 1],
                    send_sem=c_ssem.at[i - 1],
                    recv_sem=c_rsem.at[i - 1],
                    device_id=dest,
                    device_id_type=MESH,
                )
                copy.start()
                c_copies[i] = copy
    pair_y.wait_recv()
    y_out[...] = wide + y_got[...]
    y_copies = [None] * chips
    for i in far_first:
        dest = target(*offsets[i])
        copy = pltpu.make_async_remote_copy(
            src_ref=y_out.at[dest["gx"] * zsplit + dest["gz"]],
            dst_ref=y_in.at[i - 1],
            send_sem=y_ssem.at[i - 1],
            recv_sem=y_rsem.at[i - 1],
            device_id=dest,
            device_id_type=MESH,
        )
        copy.start()
        y_copies[i] = copy
    total = z_out[gx]
    for i, copy in enumerate(z_copies):
        copy.wait_recv()
        total = total + z_in[i]
    out_z[...] = total * scale_z
    slots = []
    for dx in range(slabs):
        total = c_out[gx] if dx == 0 else None
        for dz in range(zsplit):
            i = dx * zsplit + dz
            if i == 0:
                continue
            c_copies[i].wait_recv()
            total = c_in[i - 1] if total is None else total + c_in[i - 1]
        if dx == 0:
            out_x[...] = total[rows_m : rows_m + 1] * scale_x
        slots.append(jnp.concatenate([total, jnp.zeros((PAD - rows_m - 1, K), jnp.float32)], axis=0))
    core = jnp.concatenate(slots, axis=0) * scale_core
    upper = core.astype(low)
    lower = (core - upper.astype(jnp.float32)).astype(low)
    core_lane = iota((rows_c, K), 1) >> 6
    zero = jnp.zeros((rows_c, K), low)
    left = jnp.concatenate(
        [jnp.where(core_lane == e, part, zero) for e in range(E) for part in (upper, lower)],
        axis=0,
    )
    placed = dot_f32(left, spread)
    slot = iota((S, K), 1) >> 4
    x_ids = (gx - slot + 2 * slabs) & (slabs - 1)
    phx = unit_value(iota((S, K), 0) * slabs + x_ids, cor, 5)
    for e in range(E):
        at = 2 * e * rows_c
        right = jnp.concatenate(
            [
                jnp.where(keep, placed[at + s * rows_c : at + (s + 1) * rows_c], 0.0)
                for s in range(2)
            ],
            axis=0,
        ).astype(low)
        out_core[e] = dot_f32(phx, right)[:, : rows_m * S]

    total = y_out[gx * zsplit + gz]
    for i in range(1, chips):
        y_copies[i].wait_recv()
        total = total + y_in[i - 1]
    out_y[...] = total * scale_y
    started = [pair_z, pair_c, pair_y] + z_copies + c_copies[1:] + y_copies[1:]
    for copy in started:
        copy.wait_send()


def finish_kernel(*refs):
    count = len(refs) // 2
    for i in range(count):
        refs[count + i][...] = refs[i][...]


def shards_fused(sizes, flow_field, test_streams, snapshot_ids):
    slabs, zsplit, batches, local_snaps, variables, cells_y, cells_z = sizes
    pairs = batches * local_snaps
    chips = slabs * zsplit
    rows_y = cells_y // (2 * chips)
    rows_z = K // (2 * slabs)
    rows_m = S // slabs
    total_q = pairs * variables
    f32 = jnp.float32
    anywhere = pl.BlockSpec(memory_space=pl.ANY)
    vmem = pl.BlockSpec(memory_space=pltpu.VMEM)
    dma = pltpu.SemaphoreType.DMA
    total_z = cells_z * zsplit
    all_q = 2 * total_q
    scales = (
        3.0**1.5 / math.sqrt(cells_y * total_z * all_q),
        3.0**1.5 / math.sqrt(slabs * total_z * all_q),
        3.0**1.5 / math.sqrt(slabs * cells_y * all_q),
        9.0 / math.sqrt(slabs * cells_y * total_z * all_q),
    )
    outs = [
        jax.ShapeDtypeStruct((1, K), f32),
        jax.ShapeDtypeStruct((rows_y, K), f32),
        jax.ShapeDtypeStruct((rows_z, cells_z), f32),
        jax.ShapeDtypeStruct((E, S, rows_m * S), f32),
    ]
    parts = pl.pallas_call(
        functools.partial(sketch_kernel, sizes, scales),
        name="sketch",
        out_shape=outs,
        in_specs=[anywhere] * 3,
        out_specs=[vmem] * 4,
        scratch_shapes=[
            pltpu.SMEM(test_streams.shape, jnp.int32),
            pltpu.SMEM(snapshot_ids.shape, jnp.int32),
            pltpu.VMEM((total_q, chips, 2, rows_y, cells_z), jnp.bfloat16),
            pltpu.VMEM((chips, rows_y, K), f32),
            pltpu.VMEM((chips, rows_y, K), f32),
            pltpu.VMEM((chips, rows_y, K), f32),
            pltpu.VMEM((chips - 1, rows_y, K), f32),
            pltpu.VMEM((2, slabs, rows_z, cells_z), f32),
            pltpu.VMEM((slabs, rows_z, cells_z), f32),
            pltpu.VMEM((slabs, rows_z, cells_z), f32),
            pltpu.VMEM((slabs - 1, rows_z, cells_z), f32),
            pltpu.VMEM((slabs, rows_m + 1, K), f32),
            pltpu.VMEM((slabs, rows_m + 1, K), f32),
            pltpu.VMEM((slabs, rows_m + 1, K), f32),
            pltpu.VMEM((chips - 1, rows_m + 1, K), f32),
            dma((2,)),
            dma((pairs,)),
            dma((3,)),
            dma((3,)),
            dma((chips - 1,)),
            dma((chips - 1,)),
            dma((chips - 1,)),
            dma((chips - 1,)),
            dma((slabs - 1,)),
            dma((slabs - 1,)),
        ],
        compiler_params=pltpu.CompilerParams(
            collective_id=0, has_side_effects=True, vmem_limit_bytes=63 * 2**20
        ),
    )(test_streams, snapshot_ids, flow_field.reshape(total_q, chips, 2, rows_y, cells_z))
    out_x, out_y, out_z, out_core = pl.pallas_call(
        finish_kernel,
        name="finish",
        out_shape=outs,
        in_specs=[vmem] * 4,
        out_specs=[vmem] * 4,
        compiler_params=pltpu.CompilerParams(vmem_limit_bytes=63 * 2**20),
    )(*parts)
    return (out_x, out_y, out_z.T, jnp.transpose(out_core, (2, 0, 1)))


def shards(flow_field, test_streams, snapshot_ids):
    batches, local_snaps, variables, cells_x, cells_y, cells_z = flow_field.shape
    slabs = lax.axis_size("gx")
    zsplit = lax.axis_size("gz")
    fits = (
        lax.axis_size("vert") == 2
        and cells_x == 1
        and cells_z == K
        and cells_y % (16 * slabs * zsplit) == 0
        and slabs == 4
        and zsplit > 1
        and cells_y % (32 * slabs * zsplit) == 0
        and batches * local_snaps * variables <= K
    )
    if not fits:
        return shards_general(flow_field, test_streams, snapshot_ids)
    sizes = (slabs, zsplit, batches, local_snaps, variables, cells_y, cells_z)
    return shards_fused(sizes, flow_field, test_streams, snapshot_ids)


def solution(mesh):
    in_specs = (P("groups", "vert", None, "gx", None, "gz"), P("groups"), P("groups", "vert"))
    out_specs = (
        P(("groups", "gx"), None),
        P(("groups", "gx", "gz", "vert"), None),
        P(("groups", "gz"), ("gx", "vert")),
        P(("groups", "gx"), None, None),
    )
    return jax.shard_map(shards, mesh=mesh, in_specs=in_specs, out_specs=out_specs, check_vma=False)
```
